512 devices in a mesh: dp: 32 (over y_lo, x, core), tensor: 16 (over y_hi, z).
Axes of the slice: x: 4, y: 8 (y_hi: 2, y_lo: 4; y = y_hi * 4 + y_lo), z: 8, core: 2. Of those that a mesh axis runs over, the one named last changes fastest.
Arguments:
- hidden_in: bfloat16 [4096, 7168], P('dp', 'tensor'), may hold values from -6 to 6
- norm_gain: float32 [7168], replicated, may hold values from 0.1 to 1.9
- norm_bias: float32 [7168], replicated, may hold values from -3 to 3
- w_qkv: bfloat16 [7168, 6144], P('dp', 'tensor'), may hold values from -0.0625 to 0.0625
- b_qkv: float32 [6144], P('tensor'), may hold values from -3 to 3
- w_out: bfloat16 [2048, 7168], P('tensor', 'dp'), may hold values from -0.125 to 0.125
- out_grad: bfloat16 [4096, 7168], P('dp', 'tensor'), may hold values from -2 to 2
Outputs:
- grad_input: bfloat16 [4096, 7168], P('dp', 'tensor')
- grad_out_weight: float32 [2048, 7168], P('tensor', 'dp')
The draws below stay inside these ranges and needn't reach their ends.
All inputs are finite; a program needn't handle non-finite values.
Results may differ from the reference program's by a relative error of at most 0.03.
Values may be sent and summed in bfloat16 or wider, within the bound.
No kernel may reach another device: no remote copies, remote signals or barrier semaphores. Data moves between devices by JAX's collectives and lax.ppermute only.
A program may use at most 64 MiB of HBM per device.

```python
import jax
import jax.numpy as jnp
from jax import lax

D = 7168
E = 128
HEADS_DEV = 1
SEQ = 128
HEADS = 16
TOKENS = 4096
N_DP = 32
N_TENSOR = 16


def with_spikes(values, own_key, source, target, parts, factor):
    owner, partner = [(jnp.arange(values.shape[dim]) // (values.shape[dim] // parts)).reshape([-1 if axis == dim else 1 for axis in range(values.ndim)]) for dim in (source, target)]
    chosen = jax.random.permutation(own_key, parts)[partner]
    strong = (owner == chosen) | (owner == (partner + parts // 2) % parts)
    return jnp.where(strong, factor * values, values)


def level_of(rng, extent, shards, low, largest):
    gain = 1.0
    for position, blocks in shards:
        heights = jax.random.uniform(jax.random.fold_in(jax.random.fold_in(rng, 6), position), (blocks,), jnp.float32, low / len(shards), largest / len(shards))
        gain = gain * jnp.repeat(jnp.exp(heights), extent[position] // blocks).reshape((-1,) + (1,) * (len(extent) - 1 - position))
    return gain


def bell_draw(key, dims, deviation, bound, split=(), dtype=jnp.bfloat16):
    values = deviation * jax.random.normal(key, dims, jnp.float32)
    if split:
        values = values * level_of(key, dims, split, -0.22, 0.18)
    return jnp.clip(values, -bound, bound).astype(dtype)


def bell_draw_with(key, extent, scale, bound, shards, heavy, kind=jnp.bfloat16):
    entries = scale * jax.random.normal(key, extent, jnp.float32)
    if shards:
        entries = entries * level_of(key, extent, shards, -0.22, 0.18)
    return jnp.clip(with_spikes(entries, jax.random.fold_in(key, 3), *heavy), -bound, bound).astype(kind)


def setup_inputs(seed: int = 0) -> dict:
    streams_of = jax.random.split(jax.random.key(seed), 8)
    hidden_in = bell_draw(streams_of[0], (TOKENS, D), 1.0, 6.0, ((0, 32), (1, 16)))
    norm_gain = jnp.clip(1.0 + 0.18 * jax.random.normal(streams_of[1], (D,), jnp.float32), 0.1, 1.9)
    norm_bias = bell_draw(streams_of[2], (D,), 0.5, 3.0, (), jnp.float32)
    w_qkv = bell_draw(streams_of[3], (D, HEADS * 3 * E), D ** -0.5, 0.0625, ((0, 32), (1, 16)))
    b_qkv = bell_draw(streams_of[4], (HEADS * 3 * E,), 0.5, 3.0, ((0, 16),), jnp.float32)
    w_out = bell_draw(streams_of[5], (HEADS * E, D), (HEADS * E) ** -0.5, 0.125, ((0, 16), (1, 32)))
    out_grad = bell_draw_with(streams_of[6], (TOKENS, D), 0.25, 2.0, ((0, 32), (1, 16)), (0, 1, 32, 2.75))
    return {"hidden_in": hidden_in, "norm_gain": norm_gain, "norm_bias": norm_bias, "w_qkv": w_qkv, "b_qkv": b_qkv, "w_out": w_out, "out_grad": out_grad}


norm_eps = 1e-05

def to_bf16(array):
    return lax.optimization_barrier(array.astype(jnp.bfloat16)).astype(jnp.float32)

def normalize(rows, norm_gain, norm_bias):
    rows_f = rows.astype(jnp.float32)
    center = rows_f - lax.optimization_barrier(jnp.mean(rows_f, axis=-1, keepdims=True))
    inv_std = lax.rsqrt(lax.optimization_barrier(jnp.mean(center * center, axis=-1, keepdims=True)) + norm_eps)
    scaled = center * inv_std
    normed = (scaled * norm_gain + norm_bias).astype(jnp.bfloat16)
    return (scaled, inv_std, normed)

def reference(hidden_in, norm_gain, norm_bias, w_qkv, b_qkv, w_out, out_grad):
    slopes = 2.0 ** (-8.0 * (jnp.arange(HEADS) + 1).astype(jnp.float32) / HEADS)
    offsets = (jnp.arange(SEQ)[None, :] - jnp.arange(SEQ)[:, None]).astype(jnp.float32)
    causal = offsets <= 0.0
    out_three = w_out.astype(jnp.float32).reshape(HEADS, E, D)
    joined_three = w_qkv.astype(jnp.float32).reshape(D, HEADS, 3 * E)

    def micro_batch(pair):
        rows, grads_in = pair
        scaled, inv_std, normed = normalize(rows, norm_gain, norm_bias)
        joined = (jnp.dot(normed, w_qkv, preferred_element_type=jnp.float32) + b_qkv).astype(jnp.bfloat16)
        joined = joined.astype(jnp.float32).reshape(SEQ, HEADS, 3, E)
        queries = joined[:, :, 0]
        key_rows = joined[:, :, 1]
        values = joined[:, :, 2]
        scores = jnp.einsum('ihe,jhe->hij', queries, key_rows) * E ** (-0.5) + slopes[:, None, None] * offsets[None]
        scores = jnp.where(causal[None], scores, -1e+30)
        soft_weight = jax.nn.softmax(scores, axis=-1)
        soft_round = to_bf16(soft_weight)
        context = to_bf16(jnp.einsum('hij,jhe->ihe', soft_round, values))
        grads_f = grads_in.astype(jnp.float32)
        context_grad = to_bf16(jnp.einsum('id,hed->ihe', grads_f, out_three))
        weight_part = jnp.einsum('ihe,id->hed', context, grads_f).astype(jnp.bfloat16)
        prob_grad = jnp.einsum('ihe,jhe->hij', context_grad, values)
        value_grad = jnp.einsum('hij,ihe->jhe', soft_round, context_grad)
        row_dot = lax.optimization_barrier(jnp.sum(soft_weight * prob_grad, axis=-1, keepdims=True))
        score_grad = to_bf16(soft_weight * (prob_grad - row_dot) * E ** (-0.5))
        query_grad = jnp.einsum('hij,jhe->ihe', score_grad, key_rows)
        key_grad = jnp.einsum('hij,ihe->jhe', score_grad, queries)
        joined_grad = to_bf16(jnp.stack([query_grad, key_grad, value_grad], axis=2)).reshape(SEQ, HEADS, 3 * E)
        head_parts = jnp.einsum('ihc,dhc->hid', joined_grad, joined_three)
        group_parts = to_bf16(lax.optimization_barrier(jnp.sum(head_parts.reshape(N_TENSOR, HEADS_DEV, SEQ, D), axis=1)))
        normed_grad = lax.optimization_barrier(jnp.sum(group_parts, axis=0))
        scaled_grad = normed_grad * norm_gain
        mean_grad = lax.optimization_barrier(jnp.mean(scaled_grad, axis=-1, keepdims=True))
        mean_cross = lax.optimization_barrier(jnp.mean(scaled_grad * scaled, axis=-1, keepdims=True))
        input_grad = inv_std * (scaled_grad - mean_grad - scaled * mean_cross)
        return (input_grad.astype(jnp.bfloat16), weight_part)
    input_all, weight_all = lax.map(micro_batch, (hidden_in.reshape(N_DP, SEQ, D), out_grad.reshape(N_DP, SEQ, D)))
    grad_input = input_all.reshape(TOKENS, D)
    grad_out_weight = lax.optimization_barrier(jnp.sum(weight_all.astype(jnp.float32), axis=0)).reshape(HEADS * E, D)
    return (grad_input, grad_out_weight)
```

```python
import jax
import jax.numpy as jnp
from jax import lax
from jax.sharding import PartitionSpec as P

SEQ = 128
E = 128
norm_eps = 1e-05
f32 = jnp.float32
bf16 = jnp.bfloat16


def groups(count, key):
    found = {}
    for i in range(count):
        found.setdefault(key(i), []).append(i)
    return [found[k] for k in sorted(found)]


def swap_cores(x):
    n = lax.axis_size("dp")
    return lax.ppermute(x, "dp", [(i, i ^ 1) for i in range(n)])


def split(x):
    high = lax.reduce_precision(x, 8, 7)
    return high.astype(bf16), (x - high).astype(bf16)


def dot(a, b, dims):
    return lax.dot_general(a, b, (dims, ((), ())), preferred_element_type=f32)


def attention(joined, context_grad, slope):
    queries = joined[:, :E]
    key_rows = joined[:, E : 2 * E]
    values = joined[:, 2 * E :]
    scores = dot(queries, key_rows, ((1,), (1,))) * E ** (-0.5)
    row = lax.broadcasted_iota(jnp.int32, (SEQ, SEQ), 0)
    col = lax.broadcasted_iota(jnp.int32, (SEQ, SEQ), 1)
    offsets = (col - row).astype(f32)
    scores = jnp.where(offsets <= 0.0, scores + slope * offsets, -1e30)
    soft = jax.nn.softmax(scores, axis=-1)
    soft_round = soft.astype(bf16)
    context = dot(soft_round, values, ((1,), (0,))).astype(bf16)
    prob_grad = dot(context_grad, values, ((1,), (1,)))
    value_grad = dot(soft_round, context_grad, ((0,), (0,)))
    row_dot = jnp.sum(soft * prob_grad, axis=-1, keepdims=True)
    score_grad = (soft * (prob_grad - row_dot) * E ** (-0.5)).astype(bf16)
    query_grad = dot(score_grad, key_rows, ((1,), (0,)))
    key_grad = dot(score_grad, queries, ((0,), (0,)))
    joined_grad = jnp.concatenate([query_grad, key_grad, value_grad], axis=1).astype(bf16)
    return context, joined_grad


def body(hidden_in, norm_gain, norm_bias, w_qkv, b_qkv, w_out, out_grad):
    n_dp, n_tensor = lax.axis_size("dp"), lax.axis_size("tensor")
    depth = norm_gain.shape[0]
    width = depth // n_tensor
    part = width // 2
    core = lax.axis_index("dp") % 2
    rank = lax.axis_index("tensor")
    chips = groups(n_dp, lambda i: i % 2)

    weight_block = jnp.concatenate([w_qkv, w_out.T], axis=1)
    weights = lax.all_gather(weight_block, "dp", axis=0, tiled=True, axis_index_groups=chips)

    hidden_t = hidden_in.T
    acts = jnp.concatenate([hidden_t, out_grad.T], axis=1).reshape(2, part, 2 * SEQ)
    mine = jnp.where(core == 0, acts[0], acts[1])
    other = swap_cores(jnp.where(core == 0, acts[1], acts[0]))
    block = jnp.concatenate([mine[:, :SEQ], other[:, :SEQ], mine[:, SEQ:], other[:, SEQ:]], axis=1)
    rows = lax.all_to_all(
        jnp.broadcast_to(block[None], (n_tensor, part, 4 * SEQ)), "tensor", 0, 0, tiled=True
    ).reshape(n_tensor * part, 4 * SEQ)
    hidden = rows[:, : 2 * SEQ].astype(f32)
    grads = rows[:, 2 * SEQ :]

    half = depth // 2
    mean_half = jnp.sum(hidden, axis=0) / half
    square_half = jnp.sum((hidden - mean_half) ** 2, axis=0)
    stats = jnp.stack([mean_half, square_half])
    stats_other = swap_cores(stats)
    stats_other = jnp.concatenate([stats_other[:, SEQ:], stats_other[:, :SEQ]], axis=1)
    mean = 0.5 * (mean_half + stats_other[0])
    square = square_half + stats_other[1] + (mean_half - stats_other[0]) ** 2 * (half / 2)
    inv_std = lax.rsqrt(square / depth + norm_eps)

    def own_half(vector):
        pair = vector.reshape(n_tensor, 2, part)
        return jnp.where(core == 0, pair[:, 0], pair[:, 1]).reshape(half)

    gain, bias = own_half(norm_gain), own_half(norm_bias)
    normed = ((hidden - mean) * inv_std * gain[:, None] + bias[:, None]).astype(bf16)
    joined_weight = weights[:, : 3 * E]
    out_weight = weights[:, 3 * E :]
    joined_part = dot(normed, joined_weight, ((0,), (0,)))
    context_grad_part = dot(grads, out_weight, ((0,), (0,)))
    gain_high, gain_low = split(gain)
    bias_high, bias_low = split(bias)
    vectors = dot(jnp.stack([gain_high, gain_low, bias_high, bias_low]), joined_weight, ((1,), (0,)))
    gain_weight = vectors[0] + vectors[1]
    bias_weight = vectors[2] + vectors[3]

    parts = jnp.concatenate([joined_part, context_grad_part], axis=1)
    whole = parts[:SEQ] + swap_cores(parts[SEQ:])
    joined = (whole[:, : 3 * E] + b_qkv).astype(bf16)
    context_grad = whole[:, 3 * E :].astype(bf16)
    slope = 2.0 ** (-8.0 * (rank + 1).astype(f32) / n_tensor)
    context, joined_grad = attention(joined, context_grad, slope)

    context = jnp.concatenate([context, swap_cores(context)], axis=0)
    weight_part = dot(grads, context, ((1,), (0,))).astype(bf16)
    weight_parts = lax.all_to_all(
        weight_part.reshape(n_tensor, part, E), "dp", 0, 0, tiled=True, axis_index_groups=chips
    )
    grad_out_weight = jnp.sum(weight_parts.astype(f32), axis=0).T

    joined_grad = jnp.concatenate([joined_grad, swap_cores(joined_grad)], axis=0)
    group_part = dot(joined_weight, joined_grad, ((1,), (1,))).astype(bf16)
    joined_grad_f = joined_grad.astype(f32)
    sum_grad = jnp.sum(joined_grad_f * gain_weight, axis=1)
    sum_cross = jnp.sum(joined_grad_f * (joined_part - bias_weight), axis=1)
    extra = jnp.stack([*split(sum_grad), *split(sum_cross)])
    extra = jnp.concatenate([extra, jnp.zeros((12, 2 * SEQ), bf16)])
    extra = jnp.broadcast_to(extra[None], (n_tensor, 16, 2 * SEQ))
    payload = jnp.concatenate([group_part.reshape(n_tensor, part, 2 * SEQ), extra], axis=1)
    group_parts = lax.all_to_all(payload, "tensor", 0, 0, tiled=True)
    total = jnp.sum(group_parts.astype(f32), axis=0)
    total_other = swap_cores(total[:, SEQ:])
    total = total[:, :SEQ]
    normed_grad = jnp.where(
        core == 0,
        jnp.concatenate([total[:part], total_other[:part]]),
        jnp.concatenate([total_other[:part], total[:part]]),
    )
    sums = total[part:] + total_other[part:]
    mean_grad = (sums[0] + sums[1]) / depth
    mean_cross = (sums[2] + sums[3]) / depth

    own_gain = lax.dynamic_slice_in_dim(norm_gain, rank * width, width)
    scaled_grad = normed_grad * own_gain[:, None]
    scaled = (hidden_t.astype(f32) - mean[:SEQ]) * inv_std[:SEQ]
    input_grad = inv_std[:SEQ] * (scaled_grad - mean_grad - scaled * mean_cross)
    return input_grad.astype(bf16).T, grad_out_weight


def solution(mesh):
    in_specs = (
        P("dp", "tensor"),
        P(),
        P(),
        P("dp", "tensor"),
        P("tensor"),
        P("tensor", "dp"),
        P("dp", "tensor"),
    )
    out_specs = (P("dp", "tensor"), P("tensor", "dp"))
    return jax.shard_map(body, mesh=mesh, in_specs=in_specs, out_specs=out_specs, check_vma=False)
```

```python
import jax
import jax.numpy as jnp
from jax import lax
from jax.sharding import PartitionSpec as P

SEQ = 128
E = 128
Z_COUNT = 8
norm_eps = 1e-05
f32 = jnp.float32
bf16 = jnp.bfloat16


def groups(count, key):
    found = {}
    for i in range(count):
        found.setdefault(key(i), []).append(i)
    return [found[k] for k in sorted(found)]


def swap_cores(x):
    n = lax.axis_size("dp")
    return lax.ppermute(x, "dp", [(i, i ^ 1) for i in range(n)])


def ring_gather(own, z_count):
    n = lax.axis_size("tensor")
    rank = lax.axis_index("tensor")

    def shift(x, step):
        return lax.ppermute(
            x, "tensor", [(i, i - i % z_count + (i + step) % z_count) for i in range(n)]
        )

    far = lax.ppermute(own, "tensor", [(i, (i + z_count) % n) for i in range(n)])
    first = rank < z_count
    pair = jnp.stack([jnp.where(first, own, far), jnp.where(first, far, own)])
    found = {0: pair}
    up = down = pair
    for step in range(1, z_count // 2):
        up, down = shift(up, 1), shift(down, -1)
        found[step], found[z_count - step] = up, down
    found[z_count // 2] = jnp.concatenate([shift(up[:1], 1), shift(down[1:], -1)])
    blocks = [found[z_count - 1 - j] for j in range(z_count)]
    line = jnp.stack(blocks + blocks[:-1], axis=1)
    z = rank % z_count
    line = lax.dynamic_slice_in_dim(line, z_count - 1 - z, z_count, 1)
    return line.reshape(n * own.shape[0], own.shape[1])


def split(x):
    high = lax.reduce_precision(x, 8, 7)
    return high.astype(bf16), (x - high).astype(bf16)


def dot(a, b, dims):
    return lax.dot_general(a, b, (dims, ((), ())), preferred_element_type=f32)


def attention(joined, context_grad, slope):
    queries = joined[:, :E]
    key_rows = joined[:, E : 2 * E]
    values = joined[:, 2 * E :]
    scores = dot(queries, key_rows, ((1,), (1,))) * E ** (-0.5)
    row = lax.broadcasted_iota(jnp.int32, (SEQ, SEQ), 0)
    col = lax.broadcasted_iota(jnp.int32, (SEQ, SEQ), 1)
    offsets = (col - row).astype(f32)
    scores = jnp.where(offsets <= 0.0, scores + slope * offsets, -1e30)
    soft = jax.nn.softmax(scores, axis=-1)
    soft_round = soft.astype(bf16)
    context = dot(soft_round, values, ((1,), (0,))).astype(bf16)
    prob_grad = dot(context_grad, values, ((1,), (1,)))
    value_grad = dot(soft_round, context_grad, ((0,), (0,)))
    row_dot = jnp.sum(soft * prob_grad, axis=-1, keepdims=True)
    score_grad = (soft * (prob_grad - row_dot) * E ** (-0.5)).astype(bf16)
    query_grad = dot(score_grad, key_rows, ((1,), (0,)))
    key_grad = dot(score_grad, queries, ((0,), (0,)))
    joined_grad = jnp.concatenate([query_grad, key_grad, value_grad], axis=1).astype(bf16)
    return context, joined_grad


def body(hidden_in, norm_gain, norm_bias, w_qkv, b_qkv, w_out, out_grad):
    n_dp, n_tensor = lax.axis_size("dp"), lax.axis_size("tensor")
    depth = norm_gain.shape[0]
    width = depth // n_tensor
    part = width // 2
    core = lax.axis_index("dp") % 2
    rank = lax.axis_index("tensor")
    chips = groups(n_dp, lambda i: i % 2)

    weight_block = jnp.concatenate([w_qkv, w_out.T], axis=1)
    weights = lax.all_gather(weight_block, "dp", axis=0, tiled=True, axis_index_groups=chips)

    hidden_t = hidden_in.T
    acts = jnp.concatenate([hidden_t, out_grad.T], axis=1).reshape(2, part, 2 * SEQ)
    mine = jnp.where(core == 0, acts[0], acts[1])
    other = swap_cores(jnp.where(core == 0, acts[1], acts[0]))
    hidden = ring_gather(jnp.concatenate([mine[:, :SEQ], other[:, :SEQ]], axis=1), Z_COUNT).astype(f32)
    grads = ring_gather(jnp.concatenate([mine[:, SEQ:], other[:, SEQ:]], axis=1), Z_COUNT)

    half = depth // 2
    mean_half = jnp.sum(hidden, axis=0) / half
    square_half = jnp.sum((hidden - mean_half) ** 2, axis=0)
    stats = jnp.stack([mean_half, square_half])
    stats_other = swap_cores(stats)
    stats_other = jnp.concatenate([stats_other[:, SEQ:], stats_other[:, :SEQ]], axis=1)
    mean = 0.5 * (mean_half + stats_other[0])
    square = square_half + stats_other[1] + (mean_half - stats_other[0]) ** 2 * (half / 2)
    inv_std = lax.rsqrt(square / depth + norm_eps)

    def own_half(vector):
        pair = vector.reshape(n_tensor, 2, part)
        return jnp.where(core == 0, pair[:, 0], pair[:, 1]).reshape(half)

    gain, bias = own_half(norm_gain), own_half(norm_bias)
    normed = ((hidden - mean) * inv_std * gain[:, None] + bias[:, None]).astype(bf16)
    joined_weight = weights[:, : 3 * E]
    out_weight = weights[:, 3 * E :]
    joined_part = dot(normed, joined_weight, ((0,), (0,)))
    context_grad_part = dot(grads, out_weight, ((0,), (0,)))
    gain_high, gain_low = split(gain)
    bias_high, bias_low = split(bias)
    vectors = dot(jnp.stack([gain_high, gain_low, bias_high, bias_low]), joined_weight, ((1,), (0,)))
    gain_weight = vectors[0] + vectors[1]
    bias_weight = vectors[2] + vectors[3]

    parts = jnp.concatenate([joined_part, context_grad_part], axis=1)
    whole = parts[:SEQ] + swap_cores(parts[SEQ:])
    joined = (whole[:, : 3 * E] + b_qkv).astype(bf16)
    context_grad = whole[:, 3 * E :].astype(bf16)
    slope = 2.0 ** (-8.0 * (rank + 1).astype(f32) / n_tensor)
    context, joined_grad = attention(joined, context_grad, slope)

    context = jnp.concatenate([context, swap_cores(context)], axis=0)
    weight_part = dot(grads, context, ((1,), (0,))).astype(bf16)
    weight_part, joined_grad = lax.optimization_barrier((weight_part, joined_grad))
    weight_parts = lax.all_to_all(
        weight_part.reshape(n_tensor, part, E), "dp", 0, 0, tiled=True, axis_index_groups=chips
    )
    grad_out_weight = jnp.sum(weight_parts.astype(f32), axis=0).T

    joined_grad = jnp.concatenate([joined_grad, swap_cores(joined_grad)], axis=0)
    group_part = dot(joined_weight, joined_grad, ((1,), (1,))).astype(bf16)
    joined_grad_f = joined_grad.astype(f32)
    sum_grad = jnp.sum(joined_grad_f * gain_weight, axis=1)
    sum_cross = jnp.sum(joined_grad_f * (joined_part - bias_weight), axis=1)
    extra = jnp.stack([*split(sum_grad), *split(sum_cross)])
    extra = jnp.concatenate([extra, jnp.zeros((12, 2 * SEQ), bf16)])
    extra = jnp.broadcast_to(extra[None], (n_tensor, 16, 2 * SEQ))
    payload = jnp.concatenate([group_part.reshape(n_tensor, part, 2 * SEQ), extra], axis=1)
    group_parts = lax.all_to_all(payload, "tensor", 0, 0, tiled=True)
    total = jnp.sum(group_parts.astype(f32), axis=0)
    total_other = swap_cores(total[:, SEQ:])
    total = total[:, :SEQ]
    normed_grad = jnp.where(
        core == 0,
        jnp.concatenate([total[:part], total_other[:part]]),
        jnp.concatenate([total_other[:part], total[:part]]),
    )
    sums = total[part:] + total_other[part:]
    mean_grad = (sums[0] + sums[1]) / depth
    mean_cross = (sums[2] + sums[3]) / depth

    own_gain = lax.dynamic_slice_in_dim(norm_gain, rank * width, width)
    scaled_grad = normed_grad * own_gain[:, None]
    scaled = (hidden_t.astype(f32) - mean[:SEQ]) * inv_std[:SEQ]
    input_grad = inv_std[:SEQ] * (scaled_grad - mean_grad - scaled * mean_cross)
    return input_grad.astype(bf16).T, grad_out_weight


def solution(mesh):
    in_specs = (
        P("dp", "tensor"),
        P(),
        P(),
        P("dp", "tensor"),
        P("tensor"),
        P("tensor", "dp"),
        P("dp", "tensor"),
    )
    out_specs = (P("dp", "tensor"), P("tensor", "dp"))
    return jax.shard_map(body, mesh=mesh, in_specs=in_specs, out_specs=out_specs, check_vma=False)
```

```python
import jax
import jax.numpy as jnp
from jax import lax
from jax.sharding import PartitionSpec as P

SEQ = 128
E = 128
Z_COUNT = 8
X_COUNT = 4
norm_eps = 1e-05
f32 = jnp.float32
bf16 = jnp.bfloat16


def groups(count, key):
    found = {}
    for i in range(count):
        found.setdefault(key(i), []).append(i)
    return [found[k] for k in sorted(found)]


def swap_cores(x):
    n = lax.axis_size("dp")
    return lax.ppermute(x, "dp", [(i, i ^ 1) for i in range(n)])


def shift_z(x, step):
    n = lax.axis_size("tensor")
    pairs = [(i, i - i % Z_COUNT + (i + step) % Z_COUNT) for i in range(n)]
    return lax.ppermute(x, "tensor", pairs)


def swap_far(x):
    n = lax.axis_size("tensor")
    return lax.ppermute(x, "tensor", [(i, (i + Z_COUNT) % n) for i in range(n)])


def shift_x(x, step):
    n = lax.axis_size("dp")
    row = 2 * X_COUNT
    return lax.ppermute(x, "dp", [(i, i - i % row + (i + 2 * step) % row) for i in range(n)])


def shift_y(x, step):
    n = lax.axis_size("dp")
    return lax.ppermute(x, "dp", [(i, (i + 2 * X_COUNT * step) % n) for i in range(n)])


def ring_gather(own, shift, count, place):
    found = {0: own}
    up = down = own
    middle = own.shape[0] // 2
    for step in range(1, count // 2):
        up, down = shift(up, 1), shift(down, -1)
        found[step], found[count - step] = up, down
    found[count // 2] = jnp.concatenate([shift(up[:middle], 1), shift(down[middle:], -1)])
    blocks = [found[count - 1 - j] for j in range(count)]
    line = jnp.stack(blocks + blocks[:-1], axis=1)
    return lax.dynamic_slice_in_dim(line, count - 1 - place, count, 1)


def ring_scatter_x(parts, place):
    def part(step):
        return lax.dynamic_index_in_dim(parts, (place + step) % X_COUNT, 0, keepdims=False)

    across = part(2)
    middle = across.shape[0] // 2
    up = shift_x(across[:middle], 1).astype(f32)
    down = shift_x(across[middle:], -1).astype(f32)
    ahead, behind = part(1).astype(f32), part(-1).astype(f32)
    ahead = jnp.concatenate([ahead[:middle] + up, ahead[middle:]])
    behind = jnp.concatenate([behind[:middle], behind[middle:] + down])
    up, down = shift_x(ahead.astype(bf16), 1), shift_x(behind.astype(bf16), -1)
    return part(0).astype(f32) + up.astype(f32) + down.astype(f32)


def scatter_y(parts, place):
    count = parts.shape[0]
    sent = parts.astype(bf16)
    total = lax.dynamic_index_in_dim(parts, place, 0, keepdims=False)
    for step in range(1, count):
        one = lax.dynamic_index_in_dim(sent, (place + step) % count, 0, keepdims=False)
        total = total + shift_y(one, step).astype(f32)
    return total


def split(x):
    high = lax.reduce_precision(x, 8, 7)
    return high.astype(bf16), (x - high).astype(bf16)


def dot(a, b, dims):
    return lax.dot_general(a, b, (dims, ((), ())), preferred_element_type=f32)


def attention(joined, context_grad, slope):
    queries = joined[:, :E]
    key_rows = joined[:, E : 2 * E]
    values = joined[:, 2 * E :]
    scores = dot(queries, key_rows, ((1,), (1,))) * E ** (-0.5)
    row = lax.broadcasted_iota(jnp.int32, (SEQ, SEQ), 0)
    col = lax.broadcasted_iota(jnp.int32, (SEQ, SEQ), 1)
    offsets = (col - row).astype(f32)
    scores = jnp.where(offsets <= 0.0, scores + slope * offsets, -1e30)
    soft = jax.nn.softmax(scores, axis=-1)
    soft_round = soft.astype(bf16)
    context = dot(soft_round, values, ((1,), (0,))).astype(bf16)
    prob_grad = dot(context_grad, values, ((1,), (1,)))
    value_grad = dot(soft_round, context_grad, ((0,), (0,)))
    row_dot = jnp.sum(soft * prob_grad, axis=-1, keepdims=True)
    score_grad = (soft * (prob_grad - row_dot) * E ** (-0.5)).astype(bf16)
    query_grad = dot(score_grad, key_rows, ((1,), (0,)))
    key_grad = dot(score_grad, queries, ((0,), (0,)))
    joined_grad = jnp.concatenate([query_grad, key_grad, value_grad], axis=1).astype(bf16)
    return context, joined_grad


def body(hidden_in, norm_gain, norm_bias, w_qkv, b_qkv, w_out, out_grad):
    n_dp, n_tensor = lax.axis_size("dp"), lax.axis_size("tensor")
    depth = norm_gain.shape[0]
    width = depth // n_tensor
    part = width // 2
    core = lax.axis_index("dp") % 2
    rank = lax.axis_index("tensor")
    lines = groups(n_dp, lambda i: i % (2 * X_COUNT))
    rings = groups(n_tensor, lambda i: i // Z_COUNT)
    x = lax.axis_index("dp") // 2 % X_COUNT
    y = lax.axis_index("dp") // (2 * X_COUNT)
    z, far = rank % Z_COUNT, rank // Z_COUNT

    weight_block = jnp.concatenate([w_qkv, w_out.T], axis=1)
    column = lax.all_gather(weight_block, "dp", axis=0, axis_index_groups=lines)
    weights = ring_gather(column, shift_x, X_COUNT, x).reshape(n_tensor * part, 4 * E)

    hidden_t = hidden_in.T
    acts = jnp.concatenate([hidden_t, out_grad.T], axis=1).reshape(2, part, 2 * SEQ)
    mine = jnp.where(core == 0, acts[0], acts[1])
    other = swap_cores(jnp.where(core == 0, acts[1], acts[0]))
    block = jnp.concatenate([mine[:, :SEQ], other[:, :SEQ], mine[:, SEQ:], other[:, SEQ:]], axis=1)
    block_far = swap_far(block)
    pair = jnp.stack(
        [jnp.where(far == 0, block, block_far), jnp.where(far == 0, block_far, block)]
    )
    rows = ring_gather(pair, shift_z, Z_COUNT, z).reshape(n_tensor * part, 4 * SEQ)
    hidden = rows[:, : 2 * SEQ].astype(f32)
    grads = rows[:, 2 * SEQ :]

    half = depth // 2
    mean_half = jnp.sum(hidden, axis=0) / half
    square_half = jnp.sum((hidden - mean_half) ** 2, axis=0)
    stats = jnp.stack([mean_half, square_half])
    stats_other = swap_cores(stats)
    stats_other = jnp.concatenate([stats_other[:, SEQ:], stats_other[:, :SEQ]], axis=1)
    mean = 0.5 * (mean_half + stats_other[0])
    square = square_half + stats_other[1] + (mean_half - stats_other[0]) ** 2 * (half / 2)
    inv_std = lax.rsqrt(square / depth + norm_eps)

    def own_half(vector):
        pair = vector.reshape(n_tensor, 2, part)
        return jnp.where(core == 0, pair[:, 0], pair[:, 1]).reshape(half)

    gain, bias = own_half(norm_gain), own_half(norm_bias)
    normed = ((hidden - mean) * inv_std * gain[:, None] + bias[:, None]).astype(bf16)
    joined_weight = weights[:, : 3 * E]
    out_weight = weights[:, 3 * E :]
    joined_part = dot(normed, joined_weight, ((0,), (0,)))
    context_grad_part = dot(grads, out_weight, ((0,), (0,)))
    gain_high, gain_low = split(gain)
    bias_high, bias_low = split(bias)
    vectors = dot(jnp.stack([gain_high, gain_low, bias_high, bias_low]), joined_weight, ((1,), (0,)))
    gain_weight = vectors[0] + vectors[1]
    bias_weight = vectors[2] + vectors[3]

    parts = jnp.concatenate([joined_part, context_grad_part], axis=1)
    whole = parts[:SEQ] + swap_cores(parts[SEQ:])
    joined = (whole[:, : 3 * E] + b_qkv).astype(bf16)
    context_grad = whole[:, 3 * E :].astype(bf16)
    slope = 2.0 ** (-8.0 * (rank + 1).astype(f32) / n_tensor)
    context, joined_grad = attention(joined, context_grad, slope)

    context = jnp.concatenate([context, swap_cores(context)], axis=0)
    weight_part = dot(grads, context, ((1,), (0,))).astype(bf16)
    weight_parts = weight_part.reshape(-1, X_COUNT, part, E).swapaxes(0, 1)
    grad_out_weight = scatter_y(ring_scatter_x(weight_parts, x), y).T

    joined_grad = jnp.concatenate([joined_grad, swap_cores(joined_grad)], axis=0)
    group_part = dot(joined_weight, joined_grad, ((1,), (1,))).astype(bf16)
    joined_grad_f = joined_grad.astype(f32)
    sum_grad = jnp.sum(joined_grad_f * gain_weight, axis=1)
    sum_cross = jnp.sum(joined_grad_f * (joined_part - bias_weight), axis=1)
    extra = jnp.stack([*split(sum_grad), *split(sum_cross)])
    extra = jnp.concatenate([extra, jnp.zeros((12, 2 * SEQ), bf16)])
    extra = jnp.broadcast_to(extra[None], (Z_COUNT, 16, 2 * SEQ))
    group_part = group_part.reshape(2, Z_COUNT, part, 2 * SEQ)
    payload = jnp.concatenate([group_part[0], group_part[1], extra], axis=1)
    group_parts = lax.all_to_all(
        payload, "tensor", 0, 0, tiled=True, axis_index_groups=rings
    ).astype(f32)
    both = jnp.sum(group_parts[:, : 2 * part], axis=0)
    sums = jnp.sum(group_parts[:, 2 * part :], axis=0)
    sums = jnp.stack([sums[0] + sums[1], sums[2] + sums[3]])
    sent = jnp.where(far == 0, both[part:], both[:part]).astype(bf16)
    sent = jnp.concatenate([sent, *(v[None] for v in split(sums[0]) + split(sums[1]))])
    sent = jnp.concatenate([sent, jnp.zeros((12, 2 * SEQ), bf16)])
    sent = swap_far(sent).astype(f32)
    total = jnp.where(far == 0, both[:part], both[part:]) + sent[:part]
    sums = sums + jnp.stack([sent[part] + sent[part + 1], sent[part + 2] + sent[part + 3]])
    total = jnp.concatenate([total, sums, jnp.zeros((6, 2 * SEQ), f32)])
    total_other = swap_cores(total[:, SEQ:])
    total = total[:, :SEQ]
    normed_grad = jnp.where(
        core == 0,
        jnp.concatenate([total[:part], total_other[:part]]),
        jnp.concatenate([total_other[:part], total[:part]]),
    )
    sums = total[part:] + total_other[part:]
    mean_grad = sums[0] / depth
    mean_cross = sums[1] / depth

    own_gain = lax.dynamic_slice_in_dim(norm_gain, rank * width, width)
    scaled_grad = normed_grad * own_gain[:, None]
    scaled = (hidden_t.astype(f32) - mean[:SEQ]) * inv_std[:SEQ]
    input_grad = inv_std[:SEQ] * (scaled_grad - mean_grad - scaled * mean_cross)
    return input_grad.astype(bf16).T, grad_out_weight


def solution(mesh):
    in_specs = (
        P("dp", "tensor"),
        P(),
        P(),
        P("dp", "tensor"),
        P("tensor"),
        P("tensor", "dp"),
        P("dp", "tensor"),
    )
    out_specs = (P("dp", "tensor"), P("tensor", "dp"))
    return jax.shard_map(body, mesh=mesh, in_specs=in_specs, out_specs=out_specs, check_vma=False)
```

```python
import jax
import jax.numpy as jnp
from jax import lax
from jax.sharding import PartitionSpec as P

SEQ = 128
E = 128
Z_COUNT = 8
X_COUNT = 4
norm_eps = 1e-05
f32 = jnp.float32
bf16 = jnp.bfloat16


def groups(count, key):
    found = {}
    for i in range(count):
        found.setdefault(key(i), []).append(i)
    return [found[k] for k in sorted(found)]


def swap_cores(x):
    n = lax.axis_size("dp")
    return lax.ppermute(x, "dp", [(i, i ^ 1) for i in range(n)])


def shift_z(x, step):
    n = lax.axis_size("tensor")
    pairs = [(i, i - i % Z_COUNT + (i + step) % Z_COUNT) for i in range(n)]
    return lax.ppermute(x, "tensor", pairs)


def swap_far(x):
    n = lax.axis_size("tensor")
    return lax.ppermute(x, "tensor", [(i, (i + Z_COUNT) % n) for i in range(n)])


def shift_x(x, step):
    n = lax.axis_size("dp")
    row = 2 * X_COUNT
    return lax.ppermute(x, "dp", [(i, i - i % row + (i + 2 * step) % row) for i in range(n)])


def along_y(x, target):
    n_dp, n_tensor = lax.axis_size("dp"), lax.axis_size("tensor")
    row = 2 * X_COUNT
    pairs = []
    for d in range(n_dp):
        for t in range(n_tensor):
            half, place = target(t // Z_COUNT, d // row)
            to = (place * row + d % row) * n_tensor + half * Z_COUNT + t % Z_COUNT
            pairs.append((d * n_tensor + t, to))
    return lax.ppermute(x, ("dp", "tensor"), pairs)


def move_weights(x):
    return along_y(x, lambda half, place: (place // 2, 2 * half + place % 2))


def ring_gather(own, shift, count, place, axis):
    found = {0: own}
    up = down = own
    middle = own.shape[0] // 2
    for step in range(1, count // 2):
        up, down = shift(up, 1), shift(down, -1)
        found[step], found[count - step] = up, down
    found[count // 2] = jnp.concatenate([shift(up[:middle], 1), shift(down[middle:], -1)])
    blocks = [found[count - 1 - j] for j in range(count)]
    line = jnp.stack(blocks + blocks[:-1], axis=axis)
    return lax.dynamic_slice_in_dim(line, count - 1 - place, count, axis)


def ring_scatter_x(parts, place):
    def part(step):
        return lax.dynamic_index_in_dim(parts, (place + step) % X_COUNT, 0, keepdims=False)

    across = part(2)
    middle = across.shape[0] // 2
    up = shift_x(across[:middle], 1).astype(f32)
    down = shift_x(across[middle:], -1).astype(f32)
    ahead, behind = part(1).astype(f32), part(-1).astype(f32)
    ahead = jnp.concatenate([ahead[:middle] + up, ahead[middle:]])
    behind = jnp.concatenate([behind[:middle], behind[middle:] + down])
    up, down = shift_x(ahead.astype(bf16), 1), shift_x(behind.astype(bf16), -1)
    return part(0).astype(f32) + up.astype(f32) + down.astype(f32)


def scatter_y(parts, place):
    count = parts.shape[0]
    sent = parts.astype(bf16)
    total = None
    for step in range(count):
        one = lax.dynamic_index_in_dim(sent, (place + step) % count, 0, keepdims=False)

        def target(half, place):
            part = (place + step) % count
            return part // 2, 2 * half + part % 2

        one = along_y(one, target).astype(f32)
        total = one if total is None else total + one
    return total


def split(x):
    high = lax.reduce_precision(x, 8, 7)
    return high.astype(bf16), (x - high).astype(bf16)


def dot(a, b, dims):
    return lax.dot_general(a, b, (dims, ((), ())), preferred_element_type=f32)


def attention(joined, context_grad, slope):
    queries = joined[:, :E]
    key_rows = joined[:, E : 2 * E]
    values = joined[:, 2 * E :]
    scores = dot(queries, key_rows, ((1,), (1,))) * E ** (-0.5)
    row = lax.broadcasted_iota(jnp.int32, (SEQ, SEQ), 0)
    col = lax.broadcasted_iota(jnp.int32, (SEQ, SEQ), 1)
    offsets = (col - row).astype(f32)
    scores = jnp.where(offsets <= 0.0, scores + slope * offsets, -1e30)
    soft = jax.nn.softmax(scores, axis=-1)
    soft_round = soft.astype(bf16)
    context = dot(soft_round, values, ((1,), (0,))).astype(bf16)
    prob_grad = dot(context_grad, values, ((1,), (1,)))
    value_grad = dot(soft_round, context_grad, ((0,), (0,)))
    row_dot = jnp.sum(soft * prob_grad, axis=-1, keepdims=True)
    score_grad = (soft * (prob_grad - row_dot) * E ** (-0.5)).astype(bf16)
    query_grad = dot(score_grad, key_rows, ((1,), (0,)))
    key_grad = dot(score_grad, queries, ((0,), (0,)))
    joined_grad = jnp.concatenate([query_grad, key_grad, value_grad], axis=1).astype(bf16)
    return context, joined_grad


def body(hidden_in, norm_gain, norm_bias, w_qkv, b_qkv, w_out, out_grad):
    n_tensor = lax.axis_size("tensor")
    depth = norm_gain.shape[0]
    width = depth // n_tensor
    part = width // 2
    quarter = Z_COUNT * part
    rank = lax.axis_index("tensor")
    z, far = rank % Z_COUNT, rank // Z_COUNT
    dp = lax.axis_index("dp")
    core, x, y = dp % 2, dp // 2 % X_COUNT, dp // (2 * X_COUNT)
    lines = groups(lax.axis_size("dp"), lambda i: i % (2 * X_COUNT))
    rings = groups(n_tensor, lambda i: i // Z_COUNT)

    def by_far(own, other):
        return jnp.stack([jnp.where(far == 0, own, other), jnp.where(far == 0, other, own)])

    hidden_t = hidden_in.T
    acts = jnp.concatenate([hidden_t, out_grad.T], axis=1).reshape(2, part, 2 * SEQ)
    mine = jnp.where(core == 0, acts[0], acts[1])
    other = swap_cores(jnp.where(core == 0, acts[1], acts[0]))
    block = jnp.concatenate([mine[:, :SEQ], other[:, :SEQ], mine[:, SEQ:], other[:, SEQ:]], axis=1)

    weight_block = move_weights(jnp.concatenate([w_qkv, w_out.T], axis=1))
    weight_block, block = lax.optimization_barrier((weight_block, block))
    column = lax.all_gather(weight_block, "dp", axis=0, axis_index_groups=lines)

    rows = ring_gather(block, shift_z, Z_COUNT, z, 0).reshape(quarter, 4 * SEQ)
    hidden = rows[:, : 2 * SEQ].astype(f32)
    grads = rows[:, 2 * SEQ :]
    joined_weight = ring_gather(column[:, :, : 3 * E], shift_x, X_COUNT, x, 1)
    joined_weight = joined_weight.reshape(2, quarter, 3 * E)
    out_weight = ring_gather(column[:, :, 3 * E :], shift_x, X_COUNT, x, 1)
    out_weight = out_weight.reshape(2, quarter, E)

    def merge(stats, stats_other, count):
        gap = stats[0] - stats_other[0]
        return jnp.stack(
            [
                0.5 * (stats[0] + stats_other[0]),
                stats[1] + stats_other[1] + gap * gap * (count / 2),
            ]
        )

    mean_part = jnp.sum(hidden, axis=0) / quarter
    stats = jnp.stack([mean_part, jnp.sum((hidden - mean_part) ** 2, axis=0)])
    stats = merge(stats, swap_far(stats), quarter)
    stats_other = swap_cores(stats)
    stats_other = jnp.concatenate([stats_other[:, SEQ:], stats_other[:, :SEQ]], axis=1)
    stats = merge(stats, stats_other, 2 * quarter)
    mean = stats[0]
    inv_std = lax.rsqrt(stats[1] / depth + norm_eps)

    def own_part(vector):
        vector = vector.reshape(2, Z_COUNT, 2, part)
        vector = jnp.where(far == 0, vector[0], vector[1])
        return jnp.where(core == 0, vector[:, 0], vector[:, 1]).reshape(quarter)

    gain, bias = own_part(norm_gain), own_part(norm_bias)
    normed = ((hidden - mean) * inv_std * gain[:, None] + bias[:, None]).astype(bf16)
    vectors = jnp.stack([*split(gain), *split(bias)])

    def own_head(pair):
        return jnp.where(far == 0, pair[0], pair[1]), jnp.where(far == 0, pair[1], pair[0])

    vector_parts = [dot(vectors, joined_weight[h], ((1,), (0,))) for h in range(2)]
    vector_parts = [
        jnp.stack([v[0] + v[1], v[2] + v[3], jnp.zeros_like(v[0]), jnp.zeros_like(v[0])])
        for v in vector_parts
    ]
    vector_parts = [jnp.concatenate([v, jnp.zeros_like(v)]) for v in vector_parts]
    joined_parts = [dot(normed, joined_weight[h], ((0,), (0,))) for h in range(2)]
    sent = jnp.stack(
        [jnp.concatenate([j[SEQ:], v]) for j, v in zip(joined_parts, vector_parts)]
    )
    kept = jnp.stack(
        [jnp.concatenate([j[:SEQ], v]) for j, v in zip(joined_parts, vector_parts)]
    )
    own, away = own_head(kept + swap_cores(sent))
    away_high, away_low = split(away[SEQ:])
    away = swap_far(jnp.concatenate([away[:SEQ].astype(bf16), away_high, away_low]))
    away = away.astype(f32)
    plain = own[:SEQ] + away[:SEQ]
    vector = own[SEQ:] + away[SEQ : SEQ + 8] + away[SEQ + 8 :]
    gain_weight, bias_weight = vector[0], vector[1]
    joined = (plain + b_qkv).astype(bf16)

    grad_parts = jnp.stack([dot(grads, out_weight[h], ((0,), (0,))) for h in range(2)])
    own, away = own_head(grad_parts[:, :SEQ] + swap_cores(grad_parts[:, SEQ:]))
    context_grad = (own + swap_far(away.astype(bf16)).astype(f32)).astype(bf16)

    slope = 2.0 ** (-8.0 * (rank + 1).astype(f32) / n_tensor)
    context, joined_grad = attention(joined, context_grad, slope)
    joined_grad_f = joined_grad.astype(f32)
    sums = jnp.stack(
        [
            jnp.sum(joined_grad_f * gain_weight, axis=1),
            jnp.sum(joined_grad_f * (plain - bias_weight), axis=1),
        ]
    )

    def pack(sums):
        high, low = split(sums)
        return jnp.concatenate([high, low, jnp.zeros((12, sums.shape[1]), bf16)])

    def unpack(rows):
        rows = rows.astype(f32)
        return rows[0:2] + rows[2:4]

    packed = jnp.pad(pack(sums), ((0, 0), (0, 3 * E)))
    result = jnp.concatenate([jnp.concatenate([context, joined_grad], axis=1), packed])
    result_far = swap_far(result)
    sums = sums + unpack(result_far[SEQ:, :SEQ])
    heads = by_far(result[:SEQ], result_far[:SEQ])
    packed = jnp.pad(pack(sums), ((0, 0), (0, 3 * E)))
    heads_sent = jnp.concatenate([heads, jnp.stack([packed, jnp.zeros_like(packed)])], axis=1)
    heads_other = swap_cores(heads_sent)
    sums = jnp.concatenate([sums, unpack(heads_other[0, SEQ:, :SEQ])], axis=1)
    heads = jnp.concatenate([heads, heads_other[:, :SEQ]], axis=1)

    context_pair = jnp.concatenate([heads[0, :, :E], heads[1, :, :E]], axis=1)
    weight_part = dot(grads, context_pair, ((1,), (0,))).astype(bf16)
    weight_part = weight_part.reshape(2, X_COUNT, part, 2, E)
    weight_parts = weight_part.transpose(1, 3, 0, 2, 4).reshape(X_COUNT, 4, part, E)

    group_part = sum(
        dot(joined_weight[h], heads[h, :, E:], ((1,), (1,))) for h in range(2)
    ).astype(bf16)
    extra = jnp.broadcast_to(pack(sums)[None], (Z_COUNT, 16, 2 * SEQ))
    payload = jnp.concatenate([group_part.reshape(Z_COUNT, part, 2 * SEQ), extra], axis=1)
    group_parts = lax.all_to_all(payload, "tensor", 0, 0, tiled=True, axis_index_groups=rings)
    total = jnp.sum(group_parts.astype(f32), axis=0)
    sums = total[part : part + 2, :SEQ] + total[part + 2 : part + 4, :SEQ]
    total = total[:part]
    total_other = swap_cores(total[:, SEQ:])
    total = total[:, :SEQ]
    normed_grad = jnp.where(
        core == 0,
        jnp.concatenate([total, total_other]),
        jnp.concatenate([total_other, total]),
    )
    mean_grad = sums[0] / depth
    mean_cross = sums[1] / depth

    own_gain = lax.dynamic_slice_in_dim(norm_gain, rank * width, width)
    scaled_grad = normed_grad * own_gain[:, None]
    scaled = (hidden_t.astype(f32) - mean[:SEQ]) * inv_std[:SEQ]
    input_grad = inv_std[:SEQ] * (scaled_grad - mean_grad - scaled * mean_cross)

    grad_out_weight = scatter_y(ring_scatter_x(weight_parts, x), y)
    return input_grad.astype(bf16).T, grad_out_weight.T


def solution(mesh):
    in_specs = (
        P("dp", "tensor"),
        P(),
        P(),
        P("dp", "tensor"),
        P("tensor"),
        P("tensor", "dp"),
        P("dp", "tensor"),
    )
    out_specs = (P("dp", "tensor"), P("tensor", "dp"))
    return jax.shard_map(body, mesh=mesh, in_specs=in_specs, out_specs=out_specs, check_vma=False)
```

```python
import jax
import jax.numpy as jnp
from jax import lax
from jax.sharding import PartitionSpec as P

SEQ = 128
E = 128
Z_COUNT = 8
X_COUNT = 4
norm_eps = 1e-05
f32 = jnp.float32
bf16 = jnp.bfloat16


def groups(count, key):
    found = {}
    for i in range(count):
        found.setdefault(key(i), []).append(i)
    return [found[k] for k in sorted(found)]


def swap_cores(x):
    n = lax.axis_size("dp")
    return lax.ppermute(x, "dp", [(i, i ^ 1) for i in range(n)])


def shift_z(x, step):
    n = lax.axis_size("tensor")
    pairs = [(i, i - i % Z_COUNT + (i + step) % Z_COUNT) for i in range(n)]
    return lax.ppermute(x, "tensor", pairs)


def swap_far(x):
    n = lax.axis_size("tensor")
    return lax.ppermute(x, "tensor", [(i, (i + Z_COUNT) % n) for i in range(n)])


def shift_x(x, step):
    n = lax.axis_size("dp")
    row = 2 * X_COUNT
    return lax.ppermute(x, "dp", [(i, i - i % row + (i + 2 * step) % row) for i in range(n)])


def along_y(x, target):
    n_dp, n_tensor = lax.axis_size("dp"), lax.axis_size("tensor")
    row = 2 * X_COUNT
    pairs = []
    for d in range(n_dp):
        for t in range(n_tensor):
            half, place = target(t // Z_COUNT, d // row)
            to = (place * row + d % row) * n_tensor + half * Z_COUNT + t % Z_COUNT
            pairs.append((d * n_tensor + t, to))
    return lax.ppermute(x, ("dp", "tensor"), pairs)


def move_weights(x):
    return along_y(x, lambda half, place: (place // 2, 2 * half + place % 2))


def ring_gather(own, shift, count, place, axis):
    found = {0: own}
    up = down = own
    middle = own.shape[0] // 2
    for step in range(1, count // 2):
        up, down = shift(up, 1), shift(down, -1)
        found[step], found[count - step] = up, down
    found[count // 2] = jnp.concatenate([shift(up[:middle], 1), shift(down[middle:], -1)])
    blocks = [found[count - 1 - j] for j in range(count)]
    line = jnp.stack(blocks + blocks[:-1], axis=axis)
    return lax.dynamic_slice_in_dim(line, count - 1 - place, count, axis)


def ring_scatter_x(part, across):
    middle = across.shape[0] // 2
    up = shift_x(across[:middle], 1).astype(f32)
    down = shift_x(across[middle:], -1).astype(f32)
    ahead, behind = part(1).astype(f32), part(-1).astype(f32)
    ahead = jnp.concatenate([ahead[:middle] + up, ahead[middle:]])
    behind = jnp.concatenate([behind[:middle], behind[middle:] + down])
    up, down = shift_x(ahead.astype(bf16), 1), shift_x(behind.astype(bf16), -1)
    return part(0).astype(f32) + up.astype(f32) + down.astype(f32)


def scatter_y(parts, place):
    count = parts.shape[0]
    sent = parts.astype(bf16)
    total = None
    for step in range(count):
        one = lax.dynamic_index_in_dim(sent, (place + step) % count, 0, keepdims=False)

        def target(half, place):
            part = (place + step) % count
            return part // 2, 2 * half + part % 2

        one = along_y(one, target).astype(f32)
        total = one if total is None else total + one
    return total


def split(x):
    high = lax.reduce_precision(x, 8, 7)
    return high.astype(bf16), (x - high).astype(bf16)


def dot(a, b, dims):
    return lax.dot_general(a, b, (dims, ((), ())), preferred_element_type=f32)


def attention(joined, context_grad, slope):
    queries = joined[:, :E]
    key_rows = joined[:, E : 2 * E]
    values = joined[:, 2 * E :]
    scores = dot(queries, key_rows, ((1,), (1,))) * E ** (-0.5)
    row = lax.broadcasted_iota(jnp.int32, (SEQ, SEQ), 0)
    col = lax.broadcasted_iota(jnp.int32, (SEQ, SEQ), 1)
    offsets = (col - row).astype(f32)
    scores = jnp.where(offsets <= 0.0, scores + slope * offsets, -1e30)
    soft = jax.nn.softmax(scores, axis=-1)
    soft_round = soft.astype(bf16)
    context = dot(soft_round, values, ((1,), (0,))).astype(bf16)
    prob_grad = dot(context_grad, values, ((1,), (1,)))
    value_grad = dot(soft_round, context_grad, ((0,), (0,)))
    row_dot = jnp.sum(soft * prob_grad, axis=-1, keepdims=True)
    score_grad = (soft * (prob_grad - row_dot) * E ** (-0.5)).astype(bf16)
    query_grad = dot(score_grad, key_rows, ((1,), (0,)))
    key_grad = dot(score_grad, queries, ((0,), (0,)))
    joined_grad = jnp.concatenate([query_grad, key_grad, value_grad], axis=1).astype(bf16)
    return context, joined_grad


def body(hidden_in, norm_gain, norm_bias, w_qkv, b_qkv, w_out, out_grad):
    n_tensor = lax.axis_size("tensor")
    depth = norm_gain.shape[0]
    width = depth // n_tensor
    part = width // 2
    quarter = Z_COUNT * part
    rank = lax.axis_index("tensor")
    z, far = rank % Z_COUNT, rank // Z_COUNT
    dp = lax.axis_index("dp")
    core, x, y = dp % 2, dp // 2 % X_COUNT, dp // (2 * X_COUNT)
    lines = groups(lax.axis_size("dp"), lambda i: i % (2 * X_COUNT))
    rings = groups(n_tensor, lambda i: i // Z_COUNT)

    def by_far(own, other):
        return jnp.stack([jnp.where(far == 0, own, other), jnp.where(far == 0, other, own)])

    hidden_t = hidden_in.T
    acts = jnp.concatenate([hidden_t, out_grad.T], axis=1).reshape(2, part, 2 * SEQ)
    mine = jnp.where(core == 0, acts[0], acts[1])
    other = swap_cores(jnp.where(core == 0, acts[1], acts[0]))
    block = jnp.concatenate([mine[:, :SEQ], other[:, :SEQ], mine[:, SEQ:], other[:, SEQ:]], axis=1)

    weight_block = move_weights(jnp.concatenate([w_qkv, w_out.T], axis=1))
    weight_block, block = lax.optimization_barrier((weight_block, block))
    column = lax.all_gather(weight_block, "dp", axis=0, axis_index_groups=lines)

    rows = lax.all_gather(block, "tensor", axis=0, tiled=True, axis_index_groups=rings)
    hidden = rows[:, : 2 * SEQ].astype(f32)
    grads = rows[:, 2 * SEQ :]
    weights = ring_gather(column, shift_x, X_COUNT, x, 1).reshape(2, quarter, 4 * E)
    joined_weight, out_weight = weights[:, :, : 3 * E], weights[:, :, 3 * E :]

    def merge(stats, stats_other, count):
        gap = stats[0] - stats_other[0]
        return jnp.stack(
            [
                0.5 * (stats[0] + stats_other[0]),
                stats[1] + stats_other[1] + gap * gap * (count / 2),
            ]
        )

    mean_part = jnp.sum(hidden, axis=0) / quarter
    stats = jnp.stack([mean_part, jnp.sum((hidden - mean_part) ** 2, axis=0)])
    stats = merge(stats, swap_far(stats), quarter)
    stats_other = swap_cores(stats)
    stats_other = jnp.concatenate([stats_other[:, SEQ:], stats_other[:, :SEQ]], axis=1)
    stats = merge(stats, stats_other, 2 * quarter)
    mean = stats[0]
    inv_std = lax.rsqrt(stats[1] / depth + norm_eps)

    def own_part(vector):
        vector = vector.reshape(2, Z_COUNT, 2, part)
        vector = jnp.where(far == 0, vector[0], vector[1])
        return jnp.where(core == 0, vector[:, 0], vector[:, 1]).reshape(quarter)

    gain, bias = own_part(norm_gain), own_part(norm_bias)
    normed = ((hidden - mean) * inv_std * gain[:, None] + bias[:, None]).astype(bf16)
    vectors = jnp.stack([*split(gain), *split(bias)])

    def own_head(pair):
        return jnp.where(far == 0, pair[0], pair[1]), jnp.where(far == 0, pair[1], pair[0])

    vector_parts = [dot(vectors, joined_weight[h], ((1,), (0,))) for h in range(2)]
    vector_parts = [
        jnp.stack([v[0] + v[1], v[2] + v[3], jnp.zeros_like(v[0]), jnp.zeros_like(v[0])])
        for v in vector_parts
    ]
    vector_parts = [jnp.pad(v, ((0, 4), (0, E))) for v in vector_parts]
    parts = [
        jnp.concatenate(
            [
                dot(normed, joined_weight[h], ((0,), (0,))),
                dot(grads, out_weight[h], ((0,), (0,))),
            ],
            axis=1,
        )
        for h in range(2)
    ]
    sent = jnp.stack([jnp.concatenate([p[SEQ:], v]) for p, v in zip(parts, vector_parts)])
    kept = jnp.stack([jnp.concatenate([p[:SEQ], v]) for p, v in zip(parts, vector_parts)])
    own, away = own_head(kept + swap_cores(sent))
    away_high, away_low = split(away[SEQ:])
    away = swap_far(jnp.concatenate([away[:SEQ].astype(bf16), away_high, away_low]))
    away = away.astype(f32)
    vector = own[SEQ:] + away[SEQ : SEQ + 8] + away[SEQ + 8 :]
    gain_weight, bias_weight = vector[0, : 3 * E], vector[1, : 3 * E]
    whole = own[:SEQ] + away[:SEQ]
    plain = whole[:, : 3 * E]
    joined = (plain + b_qkv).astype(bf16)
    context_grad = whole[:, 3 * E :].astype(bf16)

    slope = 2.0 ** (-8.0 * (rank + 1).astype(f32) / n_tensor)
    context, joined_grad = attention(joined, context_grad, slope)
    joined_grad_f = joined_grad.astype(f32)
    sums = jnp.stack(
        [
            jnp.sum(joined_grad_f * gain_weight, axis=1),
            jnp.sum(joined_grad_f * (plain - bias_weight), axis=1),
        ]
    )

    def pack(sums):
        high, low = split(sums)
        return jnp.concatenate([high, low, jnp.zeros((12, sums.shape[1]), bf16)])

    def unpack(rows):
        rows = rows.astype(f32)
        return rows[0:2] + rows[2:4]

    packed = jnp.pad(pack(sums), ((0, 0), (0, 3 * E)))
    result = jnp.concatenate([jnp.concatenate([context, joined_grad], axis=1), packed])
    result_far = swap_far(result)
    sums = sums + unpack(result_far[SEQ:, :SEQ])
    heads = by_far(result[:SEQ], result_far[:SEQ])
    packed = jnp.pad(pack(sums), ((0, 0), (0, 3 * E)))
    heads_sent = jnp.concatenate([heads, jnp.stack([packed, jnp.zeros_like(packed)])], axis=1)
    heads_other = swap_cores(heads_sent)
    sums = jnp.concatenate([sums, unpack(heads_other[0, SEQ:, :SEQ])], axis=1)
    heads = jnp.concatenate([heads, heads_other[:, :SEQ]], axis=1)

    weight_parts = [
        dot(grads, heads[h, :, :E], ((1,), (0,))).astype(bf16).reshape(2, X_COUNT, part, E)
        for h in range(2)
    ]

    def weight_to(step):
        place = (x + step) % X_COUNT
        return jnp.concatenate(
            [lax.dynamic_index_in_dim(w, place, 1, keepdims=False) for w in weight_parts]
        )

    across, heads = lax.optimization_barrier((weight_to(2), heads))

    group_part = sum(
        dot(joined_weight[h], heads[h, :, E:], ((1,), (1,))) for h in range(2)
    ).astype(bf16)
    extra = jnp.broadcast_to(pack(sums)[None], (Z_COUNT, 16, 2 * SEQ))
    payload = jnp.concatenate([group_part.reshape(Z_COUNT, part, 2 * SEQ), extra], axis=1)
    group_parts = lax.all_to_all(payload, "tensor", 0, 0, tiled=True, axis_index_groups=rings)
    total = jnp.sum(group_parts.astype(f32), axis=0)
    sums = total[part : part + 2, :SEQ] + total[part + 2 : part + 4, :SEQ]
    total = total[:part]
    total_other = swap_cores(total[:, SEQ:])
    total = total[:, :SEQ]
    normed_grad = jnp.where(
        core == 0,
        jnp.concatenate([total, total_other]),
        jnp.concatenate([total_other, total]),
    )
    mean_grad = sums[0] / depth
    mean_cross = sums[1] / depth

    own_gain = lax.dynamic_slice_in_dim(norm_gain, rank * width, width)
    scaled_grad = normed_grad * own_gain[:, None]
    scaled = (hidden_t.astype(f32) - mean[:SEQ]) * inv_std[:SEQ]
    input_grad = inv_std[:SEQ] * (scaled_grad - mean_grad - scaled * mean_cross)

    grad_out_weight = scatter_y(ring_scatter_x(weight_to, across), y)
    return input_grad.astype(bf16).T, grad_out_weight.T


def solution(mesh):
    in_specs = (
        P("dp", "tensor"),
        P(),
        P(),
        P("dp", "tensor"),
        P("tensor"),
        P("tensor", "dp"),
        P("dp", "tensor"),
    )
    out_specs = (P("dp", "tensor"), P("tensor", "dp"))
    return jax.shard_map(body, mesh=mesh, in_specs=in_specs, out_specs=out_specs, check_vma=False)
```

```python
import jax
import jax.numpy as jnp
from jax import lax
from jax.sharding import PartitionSpec as P

SEQ = 128
E = 128
Z_COUNT = 8
X_COUNT = 4
norm_eps = 1e-05
f32 = jnp.float32
bf16 = jnp.bfloat16


def groups(count, key):
    found = {}
    for i in range(count):
        found.setdefault(key(i), []).append(i)
    return [found[k] for k in sorted(found)]


def swap_cores(x):
    n = lax.axis_size("dp")
    return lax.ppermute(x, "dp", [(i, i ^ 1) for i in range(n)])


def shift_z(x, step):
    n = lax.axis_size("tensor")
    pairs = [(i, i - i % Z_COUNT + (i + step) % Z_COUNT) for i in range(n)]
    return lax.ppermute(x, "tensor", pairs)


def swap_far(x):
    n = lax.axis_size("tensor")
    return lax.ppermute(x, "tensor", [(i, (i + Z_COUNT) % n) for i in range(n)])


def shift_x(x, step):
    n = lax.axis_size("dp")
    row = 2 * X_COUNT
    return lax.ppermute(x, "dp", [(i, i - i % row + (i + 2 * step) % row) for i in range(n)])


def along_y(x, target):
    n_dp, n_tensor = lax.axis_size("dp"), lax.axis_size("tensor")
    row = 2 * X_COUNT
    pairs = []
    for d in range(n_dp):
        for t in range(n_tensor):
            half, place = target(t // Z_COUNT, d // row)
            to = (place * row + d % row) * n_tensor + half * Z_COUNT + t % Z_COUNT
            pairs.append((d * n_tensor + t, to))
    return lax.ppermute(x, ("dp", "tensor"), pairs)


def move_weights(x):
    return along_y(x, lambda half, place: (place // 2, 2 * half + place % 2))


def x_gather(own, place, early):
    middle = own.shape[0] // 2
    up, down = shift_x(own, 1), shift_x(own, -1)
    up, down, early = lax.optimization_barrier((up, down, early))
    across = jnp.concatenate([shift_x(up[:middle], 1), shift_x(down[middle:], -1)])
    line = jnp.stack([down, across, up, own, down, across, up], axis=1)
    return lax.dynamic_slice_in_dim(line, X_COUNT - 1 - place, X_COUNT, 1), early


def ring_scatter_x(part, across):
    ahead = part(1).astype(f32) + shift_x(across, 1).astype(f32)
    up, down = shift_x(ahead.astype(bf16), 1), shift_x(part(-1), -1)
    return part(0).astype(f32) + up.astype(f32) + down.astype(f32)


def scatter_y(parts, place, early):
    count = parts.shape[0]
    sent = parts.astype(bf16)
    total = None
    for step in range(count):
        if step == count // 2:
            sent, early = lax.optimization_barrier((sent, early))
        one = lax.dynamic_index_in_dim(sent, (place + step) % count, 0, keepdims=False)

        def target(half, place):
            part = (place + step) % count
            return part // 2, 2 * half + part % 2

        one = along_y(one, target).astype(f32)
        total = one if total is None else total + one
    return total, early


def split(x):
    high = lax.reduce_precision(x, 8, 7)
    return high.astype(bf16), (x - high).astype(bf16)


def dot(a, b, dims):
    return lax.dot_general(a, b, (dims, ((), ())), preferred_element_type=f32)


def attention(joined, context_grad, slope):
    queries = joined[:, :E]
    key_rows = joined[:, E : 2 * E]
    values = joined[:, 2 * E :]
    scores = dot(queries, key_rows, ((1,), (1,))) * E ** (-0.5)
    row = lax.broadcasted_iota(jnp.int32, (SEQ, SEQ), 0)
    col = lax.broadcasted_iota(jnp.int32, (SEQ, SEQ), 1)
    offsets = (col - row).astype(f32)
    scores = jnp.where(offsets <= 0.0, scores + slope * offsets, -1e30)
    soft = jax.nn.softmax(scores, axis=-1)
    soft_round = soft.astype(bf16)
    context = dot(soft_round, values, ((1,), (0,))).astype(bf16)
    prob_grad = dot(context_grad, values, ((1,), (1,)))
    value_grad = dot(soft_round, context_grad, ((0,), (0,)))
    row_dot = jnp.sum(soft * prob_grad, axis=-1, keepdims=True)
    score_grad = (soft * (prob_grad - row_dot) * E ** (-0.5)).astype(bf16)
    query_grad = dot(score_grad, key_rows, ((1,), (0,)))
    key_grad = dot(score_grad, queries, ((0,), (0,)))
    joined_grad = jnp.concatenate([query_grad, key_grad, value_grad], axis=1).astype(bf16)
    return context, joined_grad


def body(hidden_in, norm_gain, norm_bias, w_qkv, b_qkv, w_out, out_grad):
    n_tensor = lax.axis_size("tensor")
    depth = norm_gain.shape[0]
    width = depth // n_tensor
    part = width // 2
    quarter = Z_COUNT * part
    rank = lax.axis_index("tensor")
    z, far = rank % Z_COUNT, rank // Z_COUNT
    dp = lax.axis_index("dp")
    core, x, y = dp % 2, dp // 2 % X_COUNT, dp // (2 * X_COUNT)
    lines = groups(lax.axis_size("dp"), lambda i: i % (2 * X_COUNT))
    rings = groups(n_tensor, lambda i: i // Z_COUNT)

    def by_far(own, other):
        return jnp.stack([jnp.where(far == 0, own, other), jnp.where(far == 0, other, own)])

    hidden_t = hidden_in.T
    acts = jnp.concatenate([hidden_t, out_grad.T], axis=1).reshape(2, part, 2 * SEQ)
    mine = jnp.where(core == 0, acts[0], acts[1])
    other = swap_cores(jnp.where(core == 0, acts[1], acts[0]))
    block = jnp.concatenate([mine[:, :SEQ], other[:, :SEQ], mine[:, SEQ:], other[:, SEQ:]], axis=1)

    weight_block = move_weights(jnp.concatenate([w_qkv, w_out.T], axis=1))
    weight_block, block = lax.optimization_barrier((weight_block, block))
    column = lax.all_gather(weight_block, "dp", axis=0, axis_index_groups=lines)

    rows = lax.all_gather(block, "tensor", axis=0, tiled=True, axis_index_groups=rings)
    hidden = rows[:, : 2 * SEQ].astype(f32)
    grads = rows[:, 2 * SEQ :]
    mean_part = jnp.sum(hidden, axis=0) / quarter
    stats = jnp.stack([mean_part, jnp.sum((hidden - mean_part) ** 2, axis=0)])
    weights, stats = x_gather(column, x, stats)
    weights = weights.reshape(2, quarter, 4 * E)
    joined_weight, out_weight = weights[:, :, : 3 * E], weights[:, :, 3 * E :]

    def merge(stats, stats_other, count):
        gap = stats[0] - stats_other[0]
        return jnp.stack(
            [
                0.5 * (stats[0] + stats_other[0]),
                stats[1] + stats_other[1] + gap * gap * (count / 2),
            ]
        )

    stats = merge(stats, swap_far(stats), quarter)
    stats_other = swap_cores(stats)
    stats_other = jnp.concatenate([stats_other[:, SEQ:], stats_other[:, :SEQ]], axis=1)
    stats = merge(stats, stats_other, 2 * quarter)
    mean = stats[0]
    inv_std = lax.rsqrt(stats[1] / depth + norm_eps)

    def own_part(vector):
        vector = vector.reshape(2, Z_COUNT, 2, part)
        vector = jnp.where(far == 0, vector[0], vector[1])
        return jnp.where(core == 0, vector[:, 0], vector[:, 1]).reshape(quarter)

    gain, bias = own_part(norm_gain), own_part(norm_bias)
    normed = ((hidden - mean) * inv_std * gain[:, None] + bias[:, None]).astype(bf16)
    vectors = jnp.stack([*split(gain), *split(bias)])

    def own_head(pair):
        return jnp.where(far == 0, pair[0], pair[1]), jnp.where(far == 0, pair[1], pair[0])

    vector_parts = [dot(vectors, joined_weight[h], ((1,), (0,))) for h in range(2)]
    vector_parts = [
        jnp.stack([v[0] + v[1], v[2] + v[3], jnp.zeros_like(v[0]), jnp.zeros_like(v[0])])
        for v in vector_parts
    ]
    vector_parts = [jnp.pad(v, ((0, 4), (0, E))) for v in vector_parts]
    parts = [
        jnp.concatenate(
            [
                dot(normed, joined_weight[h], ((0,), (0,))),
                dot(grads, out_weight[h], ((0,), (0,))),
            ],
            axis=1,
        )
        for h in range(2)
    ]
    sent = jnp.stack([jnp.concatenate([p[SEQ:], v]) for p, v in zip(parts, vector_parts)])
    kept = jnp.stack([jnp.concatenate([p[:SEQ], v]) for p, v in zip(parts, vector_parts)])
    own, away = own_head(kept + swap_cores(sent))
    away_high, away_low = split(away[SEQ:])
    away = swap_far(jnp.concatenate([away[:SEQ].astype(bf16), away_high, away_low]))
    away = away.astype(f32)
    vector = own[SEQ:] + away[SEQ : SEQ + 8] + away[SEQ + 8 :]
    gain_weight, bias_weight = vector[0, : 3 * E], vector[1, : 3 * E]
    whole = own[:SEQ] + away[:SEQ]
    plain = whole[:, : 3 * E]
    joined = (plain + b_qkv).astype(bf16)
    context_grad = whole[:, 3 * E :].astype(bf16)

    slope = 2.0 ** (-8.0 * (rank + 1).astype(f32) / n_tensor)
    context, joined_grad = attention(joined, context_grad, slope)
    joined_grad_f = joined_grad.astype(f32)
    sums = jnp.stack(
        [
            jnp.sum(joined_grad_f * gain_weight, axis=1),
            jnp.sum(joined_grad_f * (plain - bias_weight), axis=1),
        ]
    )

    def pack(sums):
        high, low = split(sums)
        return jnp.concatenate([high, low, jnp.zeros((12, sums.shape[1]), bf16)])

    def unpack(rows):
        rows = rows.astype(f32)
        return rows[0:2] + rows[2:4]

    packed = jnp.pad(pack(sums), ((0, 0), (0, 3 * E)))
    result = jnp.concatenate([jnp.concatenate([context, joined_grad], axis=1), packed])
    result_far = swap_far(result)
    sums = sums + unpack(result_far[SEQ:, :SEQ])
    heads = by_far(result[:SEQ], result_far[:SEQ])
    packed = jnp.pad(pack(sums), ((0, 0), (0, 3 * E)))
    heads_sent = jnp.concatenate([heads, jnp.stack([packed, jnp.zeros_like(packed)])], axis=1)
    heads_other = swap_cores(heads_sent)
    sums = jnp.concatenate([sums, unpack(heads_other[0, SEQ:, :SEQ])], axis=1)
    heads = jnp.concatenate([heads, heads_other[:, :SEQ]], axis=1)

    weight_parts = [
        dot(grads, heads[h, :, :E], ((1,), (0,))).astype(bf16).reshape(2, X_COUNT, part, E)
        for h in range(2)
    ]

    def weight_to(step):
        place = (x + step) % X_COUNT
        return jnp.concatenate(
            [lax.dynamic_index_in_dim(w, place, 1, keepdims=False) for w in weight_parts]
        )

    across, heads = lax.optimization_barrier((weight_to(2), heads))

    group_part = sum(
        dot(joined_weight[h], heads[h, :, E:], ((1,), (1,))) for h in range(2)
    ).astype(bf16)
    extra = jnp.broadcast_to(pack(sums)[None], (Z_COUNT, 16, 2 * SEQ))
    payload = jnp.concatenate([group_part.reshape(Z_COUNT, part, 2 * SEQ), extra], axis=1)
    group_parts = lax.all_to_all(payload, "tensor", 0, 0, tiled=True, axis_index_groups=rings)
    total = jnp.sum(group_parts.astype(f32), axis=0)
    weight_parts = ring_scatter_x(weight_to, across)
    grad_out_weight, total = scatter_y(weight_parts, y, total)
    sums = total[part : part + 2, :SEQ] + total[part + 2 : part + 4, :SEQ]
    total = total[:part]
    total_other = swap_cores(total[:, SEQ:])
    total = total[:, :SEQ]
    normed_grad = jnp.where(
        core == 0,
        jnp.concatenate([total, total_other]),
        jnp.concatenate([total_other, total]),
    )
    mean_grad = sums[0] / depth
    mean_cross = sums[1] / depth

    own_gain = lax.dynamic_slice_in_dim(norm_gain, rank * width, width)
    scaled_grad = normed_grad * own_gain[:, None]
    scaled = (hidden_t.astype(f32) - mean[:SEQ]) * inv_std[:SEQ]
    input_grad = inv_std[:SEQ] * (scaled_grad - mean_grad - scaled * mean_cross)

    return input_grad.astype(bf16).T, grad_out_weight.T


def solution(mesh):
    in_specs = (
        P("dp", "tensor"),
        P(),
        P(),
        P("dp", "tensor"),
        P("tensor"),
        P("tensor", "dp"),
        P("dp", "tensor"),
    )
    out_specs = (P("dp", "tensor"), P("tensor", "dp"))
    return jax.shard_map(body, mesh=mesh, in_specs=in_specs, out_specs=out_specs, check_vma=False)
```

```python
import jax
import jax.numpy as jnp
from jax import lax
from jax.sharding import PartitionSpec as P

SEQ = 128
E = 128
Z_COUNT = 8
X_COUNT = 4
norm_eps = 1e-05
f32 = jnp.float32
bf16 = jnp.bfloat16


def groups(count, key):
    found = {}
    for i in range(count):
        found.setdefault(key(i), []).append(i)
    return [found[k] for k in sorted(found)]


def swap_cores(x):
    n = lax.axis_size("dp")
    return lax.ppermute(x, "dp", [(i, i ^ 1) for i in range(n)])


def shift_z(x, step):
    n = lax.axis_size("tensor")
    pairs = [(i, i - i % Z_COUNT + (i + step) % Z_COUNT) for i in range(n)]
    return lax.ppermute(x, "tensor", pairs)


def swap_far(x):
    n = lax.axis_size("tensor")
    return lax.ppermute(x, "tensor", [(i, (i + Z_COUNT) % n) for i in range(n)])


def shift_x(x, step):
    n = lax.axis_size("dp")
    row = 2 * X_COUNT
    return lax.ppermute(x, "dp", [(i, i - i % row + (i + 2 * step) % row) for i in range(n)])


def along_y(x, target):
    n_dp, n_tensor = lax.axis_size("dp"), lax.axis_size("tensor")
    row = 2 * X_COUNT
    pairs = []
    for d in range(n_dp):
        for t in range(n_tensor):
            half, place = target(t // Z_COUNT, d // row)
            to = (place * row + d % row) * n_tensor + half * Z_COUNT + t % Z_COUNT
            pairs.append((d * n_tensor + t, to))
    return lax.ppermute(x, ("dp", "tensor"), pairs)


def move_weights(x):
    return along_y(x, lambda half, place: (place // 2, 2 * half + place % 2))


def x_gather(own, place, early):
    middle = own.shape[0] // 2
    up, down = shift_x(own, 1), shift_x(own, -1)
    up, down, early = lax.optimization_barrier((up, down, early))
    across = jnp.concatenate([shift_x(up[:middle], 1), shift_x(down[middle:], -1)])
    return [own, down, across, up], early


def in_order(blocks, place):
    line = jnp.stack(blocks[1:] + blocks, axis=1)
    return lax.dynamic_slice_in_dim(line, X_COUNT - 1 - place, X_COUNT, 1)


def ring_scatter_x(part, across):
    ahead = part(1).astype(f32) + across.astype(f32)
    up, down = shift_x(ahead.astype(bf16), 1), shift_x(part(-1), -1)
    return part(0).astype(f32) + up.astype(f32) + down.astype(f32)


def scatter_y(parts, place, early):
    count = parts.shape[0]
    sent = parts.astype(bf16)
    total = None
    for step in range(count):
        if step == count // 2:
            sent, early = lax.optimization_barrier((sent, early))
        one = lax.dynamic_index_in_dim(sent, (place + step) % count, 0, keepdims=False)

        def target(half, place):
            part = (place + step) % count
            return part // 2, 2 * half + part % 2

        one = along_y(one, target).astype(f32)
        total = one if total is None else total + one
    return total, early


def split(x):
    high = lax.reduce_precision(x, 8, 7)
    return high.astype(bf16), (x - high).astype(bf16)


def dot(a, b, dims):
    return lax.dot_general(a, b, (dims, ((), ())), preferred_element_type=f32)


def attention(joined, context_grad, slope):
    queries = joined[:, :E]
    key_rows = joined[:, E : 2 * E]
    values = joined[:, 2 * E :]
    scores = dot(queries, key_rows, ((1,), (1,))) * E ** (-0.5)
    row = lax.broadcasted_iota(jnp.int32, (SEQ, SEQ), 0)
    col = lax.broadcasted_iota(jnp.int32, (SEQ, SEQ), 1)
    offsets = (col - row).astype(f32)
    scores = jnp.where(offsets <= 0.0, scores + slope * offsets, -1e30)
    soft = jax.nn.softmax(scores, axis=-1)
    soft_round = soft.astype(bf16)
    context = dot(soft_round, values, ((1,), (0,))).astype(bf16)
    prob_grad = dot(context_grad, values, ((1,), (1,)))
    value_grad = dot(soft_round, context_grad, ((0,), (0,)))
    row_dot = jnp.sum(soft * prob_grad, axis=-1, keepdims=True)
    score_grad = (soft * (prob_grad - row_dot) * E ** (-0.5)).astype(bf16)
    query_grad = dot(score_grad, key_rows, ((1,), (0,)))
    key_grad = dot(score_grad, queries, ((0,), (0,)))
    joined_grad = jnp.concatenate([query_grad, key_grad, value_grad], axis=1).astype(bf16)
    return context, joined_grad


def body(hidden_in, norm_gain, norm_bias, w_qkv, b_qkv, w_out, out_grad):
    n_tensor = lax.axis_size("tensor")
    depth = norm_gain.shape[0]
    width = depth // n_tensor
    part = width // 2
    quarter = Z_COUNT * part
    rank = lax.axis_index("tensor")
    z, far = rank % Z_COUNT, rank // Z_COUNT
    dp = lax.axis_index("dp")
    core, x, y = dp % 2, dp // 2 % X_COUNT, dp // (2 * X_COUNT)
    lines = groups(lax.axis_size("dp"), lambda i: i % (2 * X_COUNT))
    rings = groups(n_tensor, lambda i: i // Z_COUNT)

    def by_far(own, other):
        return jnp.stack([jnp.where(far == 0, own, other), jnp.where(far == 0, other, own)])

    hidden_t = hidden_in.T
    acts = jnp.concatenate([hidden_t, out_grad.T], axis=1).reshape(2, part, 2 * SEQ)
    mine = jnp.where(core == 0, acts[0], acts[1])
    other = swap_cores(jnp.where(core == 0, acts[1], acts[0]))
    block = jnp.concatenate([mine[:, :SEQ], other[:, :SEQ], mine[:, SEQ:], other[:, SEQ:]], axis=1)

    weight_block = move_weights(jnp.concatenate([w_qkv, w_out.T], axis=1))
    hidden = lax.all_gather(
        block[:, : 2 * SEQ], "tensor", axis=0, tiled=True, axis_index_groups=rings
    )
    weight_block, hidden = lax.optimization_barrier((weight_block, hidden))
    column = lax.all_gather(weight_block, "dp", axis=0, axis_index_groups=lines)
    column, block = lax.optimization_barrier((column, block))
    grads = lax.all_gather(
        block[:, 2 * SEQ :], "tensor", axis=0, tiled=True, axis_index_groups=rings
    )
    blocks, grads = x_gather(column, x, grads)
    hidden = hidden.astype(f32)
    mean_part = jnp.sum(hidden, axis=0) / quarter
    stats = jnp.stack([mean_part, jnp.sum((hidden - mean_part) ** 2, axis=0)])

    def merge(stats, stats_other, count):
        gap = stats[0] - stats_other[0]
        return jnp.stack(
            [
                0.5 * (stats[0] + stats_other[0]),
                stats[1] + stats_other[1] + gap * gap * (count / 2),
            ]
        )

    stats = merge(stats, swap_far(stats), quarter)
    stats_other = swap_cores(stats)
    stats_other = jnp.concatenate([stats_other[:, SEQ:], stats_other[:, :SEQ]], axis=1)
    stats = merge(stats, stats_other, 2 * quarter)
    mean = stats[0]
    inv_std = lax.rsqrt(stats[1] / depth + norm_eps)

    def own_part(vector):
        vector = vector.reshape(2, Z_COUNT, 2, part)
        vector = jnp.where(far == 0, vector[0], vector[1])
        return jnp.where(core == 0, vector[:, 0], vector[:, 1]).reshape(quarter)

    gain, bias = own_part(norm_gain), own_part(norm_bias)
    normed = ((hidden - mean) * inv_std * gain[:, None] + bias[:, None]).astype(bf16)
    vectors = jnp.stack([*split(gain), *split(bias)] + [jnp.zeros_like(gain, bf16)] * 4)
    left = jnp.concatenate([normed, vectors.T], axis=1).reshape(2, X_COUNT, part, 2 * SEQ + 8)
    right = grads.reshape(2, X_COUNT, part, 2 * SEQ)

    def own_head(pair):
        return jnp.where(far == 0, pair[0], pair[1]), jnp.where(far == 0, pair[1], pair[0])

    joined_parts, grad_parts = [0.0, 0.0], [0.0, 0.0]
    for step in (0, 3, 1, 2):
        place = (x + step) % X_COUNT
        left_part = lax.dynamic_index_in_dim(left, place, 1, keepdims=False)
        right_part = lax.dynamic_index_in_dim(right, place, 1, keepdims=False)
        left_part = left_part.reshape(2 * part, 2 * SEQ + 8)
        right_part = right_part.reshape(2 * part, 2 * SEQ)
        for h in range(2):
            weight = blocks[step][2 * h : 2 * h + 2].reshape(2 * part, 4 * E)
            joined_parts[h] += dot(left_part, weight[:, : 3 * E], ((0,), (0,)))
            grad_parts[h] += dot(right_part, weight[:, 3 * E :], ((0,), (0,)))
    parts = []
    for j, g in zip(joined_parts, grad_parts):
        v = j[2 * SEQ :]
        v = jnp.stack([v[0] + v[1], v[2] + v[3]])
        parts.append((jnp.concatenate([j[: 2 * SEQ], g], axis=1), jnp.pad(v, ((0, 6), (0, E)))))
    sent = jnp.stack([jnp.concatenate([p[SEQ:], v]) for p, v in parts])
    kept = jnp.stack([jnp.concatenate([p[:SEQ], v]) for p, v in parts])
    own, away = own_head(kept + swap_cores(sent))
    away_high, away_low = split(away[SEQ:])
    away = swap_far(jnp.concatenate([away[:SEQ].astype(bf16), away_high, away_low]))
    away = away.astype(f32)
    vector = own[SEQ:] + away[SEQ : SEQ + 8] + away[SEQ + 8 :]
    gain_weight, bias_weight = vector[0, : 3 * E], vector[1, : 3 * E]
    whole = own[:SEQ] + away[:SEQ]
    plain = whole[:, : 3 * E]
    joined = (plain + b_qkv).astype(bf16)
    context_grad = whole[:, 3 * E :].astype(bf16)

    slope = 2.0 ** (-8.0 * (rank + 1).astype(f32) / n_tensor)
    context, joined_grad = attention(joined, context_grad, slope)
    joined_grad_f = joined_grad.astype(f32)
    sums = jnp.stack(
        [
            jnp.sum(joined_grad_f * gain_weight, axis=1),
            jnp.sum(joined_grad_f * (plain - bias_weight), axis=1),
        ]
    )

    def pack(sums):
        high, low = split(sums)
        return jnp.concatenate([high, low, jnp.zeros((12, sums.shape[1]), bf16)])

    def unpack(rows):
        rows = rows.astype(f32)
        return rows[0:2] + rows[2:4]

    packed = jnp.pad(pack(sums), ((0, 0), (0, 3 * E)))
    result = jnp.concatenate([jnp.concatenate([context, joined_grad], axis=1), packed])
    result_far = swap_far(result)
    sums = sums + unpack(result_far[SEQ:, :SEQ])
    heads = by_far(result[:SEQ], result_far[:SEQ])
    packed = jnp.pad(pack(sums), ((0, 0), (0, 3 * E)))
    heads_sent = jnp.concatenate([heads, jnp.stack([packed, jnp.zeros_like(packed)])], axis=1)
    heads_other = swap_cores(heads_sent)
    sums = jnp.concatenate([sums, unpack(heads_other[0, SEQ:, :SEQ])], axis=1)
    heads = jnp.concatenate([heads, heads_other[:, :SEQ]], axis=1)

    joined_weight = in_order([b[:, :, : 3 * E] for b in blocks], x).reshape(2, quarter, 3 * E)
    weight_parts = [
        dot(grads, heads[h, :, :E], ((1,), (0,))).astype(bf16).reshape(2, X_COUNT, part, E)
        for h in range(2)
    ]

    def weight_to(step):
        place = (x + step) % X_COUNT
        return jnp.concatenate(
            [lax.dynamic_index_in_dim(w, place, 1, keepdims=False) for w in weight_parts]
        )

    across = shift_x(weight_to(2), 1)
    across, heads = lax.optimization_barrier((across, heads))

    group_part = sum(
        dot(joined_weight[h], heads[h, :, E:], ((1,), (1,))) for h in range(2)
    ).astype(bf16)
    extra = jnp.broadcast_to(pack(sums)[None], (Z_COUNT, 16, 2 * SEQ))
    payload = jnp.concatenate([group_part.reshape(Z_COUNT, part, 2 * SEQ), extra], axis=1)
    group_parts = lax.all_to_all(payload, "tensor", 0, 0, tiled=True, axis_index_groups=rings)
    total = jnp.sum(group_parts.astype(f32), axis=0)
    weight_parts = ring_scatter_x(weight_to, across)
    grad_out_weight, total = scatter_y(weight_parts, y, total)
    sums = total[part : part + 2, :SEQ] + total[part + 2 : part + 4, :SEQ]
    total = total[:part]
    total_other = swap_cores(total[:, SEQ:])
    total = total[:, :SEQ]
    normed_grad = jnp.where(
        core == 0,
        jnp.concatenate([total, total_other]),
        jnp.concatenate([total_other, total]),
    )
    mean_grad = sums[0] / depth
    mean_cross = sums[1] / depth

    own_gain = lax.dynamic_slice_in_dim(norm_gain, rank * width, width)
    scaled_grad = normed_grad * own_gain[:, None]
    scaled = (hidden_t.astype(f32) - mean[:SEQ]) * inv_std[:SEQ]
    input_grad = inv_std[:SEQ] * (scaled_grad - mean_grad - scaled * mean_cross)

    return input_grad.astype(bf16).T, grad_out_weight.T


def solution(mesh):
    in_specs = (
        P("dp", "tensor"),
        P(),
        P(),
        P("dp", "tensor"),
        P("tensor"),
        P("tensor", "dp"),
        P("dp", "tensor"),
    )
    out_specs = (P("dp", "tensor"), P("tensor", "dp"))
    return jax.shard_map(body, mesh=mesh, in_specs=in_specs, out_specs=out_specs, check_vma=False)
```

```python
import jax
import jax.numpy as jnp
from jax import lax
from jax.sharding import PartitionSpec as P

SEQ = 128
E = 128
Z_COUNT = 8
X_COUNT = 4
norm_eps = 1e-05
f32 = jnp.float32
bf16 = jnp.bfloat16


def groups(count, key):
    found = {}
    for i in range(count):
        found.setdefault(key(i), []).append(i)
    return [found[k] for k in sorted(found)]


def swap_cores(x):
    n = lax.axis_size("dp")
    return lax.ppermute(x, "dp", [(i, i ^ 1) for i in range(n)])


def shift_z(x, step):
    n = lax.axis_size("tensor")
    pairs = [(i, i - i % Z_COUNT + (i + step) % Z_COUNT) for i in range(n)]
    return lax.ppermute(x, "tensor", pairs)


def swap_far(x):
    n = lax.axis_size("tensor")
    return lax.ppermute(x, "tensor", [(i, (i + Z_COUNT) % n) for i in range(n)])


def shift_x(x, step):
    n = lax.axis_size("dp")
    row = 2 * X_COUNT
    return lax.ppermute(x, "dp", [(i, i - i % row + (i + 2 * step) % row) for i in range(n)])


def swap_heads(x):
    n = lax.axis_size("tensor")
    return lax.ppermute(x, "tensor", [(i, i ^ 1) for i in range(n)])


def to_pair(x, step):
    n_dp, n_tensor = lax.axis_size("dp"), lax.axis_size("tensor")
    row = 2 * X_COUNT
    pairs = []
    for d in range(n_dp):
        for t in range(n_tensor):
            same = d // 2 % 2 == t % 2
            to, head = (d, t) if same else (d ^ 2, t ^ 1)
            pairs.append((d * n_tensor + t, (to + row * step) % n_dp * n_tensor + head))
    return lax.ppermute(x, ("dp", "tensor"), pairs)


def z_gather(pair, place):
    count = Z_COUNT // 2
    up, down = shift_z(pair, 2), shift_z(pair, -2)
    across = jnp.concatenate([shift_z(up[:1], 2), shift_z(down[1:], -2)])
    line = jnp.stack([down, across, up, pair, down, across, up], axis=1)
    return lax.dynamic_slice_in_dim(line, count - 1 - place, count, 1)


def x_gather(own):
    middle = own.shape[0] // 2
    up, down = shift_x(own, 1), shift_x(own, -1)
    across = jnp.concatenate([shift_x(up[:middle], 1), shift_x(down[middle:], -1)])
    return [own, down, across, up]


def ring_scatter_x(part, across):
    ahead = part(1).astype(f32) + shift_x(across, 1).astype(f32)
    up, down = shift_x(ahead.astype(bf16), 1), shift_x(part(-1), -1)
    return part(0).astype(f32) + up.astype(f32) + down.astype(f32)


def scatter_y(parts, place, early):
    count = parts.shape[0]
    sent = parts.astype(bf16)
    total = None
    for step in range(count):
        if step == count // 2:
            sent, early = lax.optimization_barrier((sent, early))
        one = lax.dynamic_index_in_dim(sent, (place + step) % count, 0, keepdims=False)
        one = to_pair(one, step).astype(f32)
        total = one if total is None else total + one
    return total, early


def split(x):
    high = lax.reduce_precision(x, 8, 7)
    return high.astype(bf16), (x - high).astype(bf16)


def dot(a, b, dims):
    return lax.dot_general(a, b, (dims, ((), ())), preferred_element_type=f32)


def attention(joined, context_grad, slope):
    queries = joined[:, :E]
    key_rows = joined[:, E : 2 * E]
    values = joined[:, 2 * E :]
    scores = dot(queries, key_rows, ((1,), (1,))) * E ** (-0.5)
    row = lax.broadcasted_iota(jnp.int32, (SEQ, SEQ), 0)
    col = lax.broadcasted_iota(jnp.int32, (SEQ, SEQ), 1)
    offsets = (col - row).astype(f32)
    scores = jnp.where(offsets <= 0.0, scores + slope * offsets, -1e30)
    soft = jax.nn.softmax(scores, axis=-1)
    soft_round = soft.astype(bf16)
    context = dot(soft_round, values, ((1,), (0,))).astype(bf16)
    prob_grad = dot(context_grad, values, ((1,), (1,)))
    value_grad = dot(soft_round, context_grad, ((0,), (0,)))
    row_dot = jnp.sum(soft * prob_grad, axis=-1, keepdims=True)
    score_grad = (soft * (prob_grad - row_dot) * E ** (-0.5)).astype(bf16)
    query_grad = dot(score_grad, key_rows, ((1,), (0,)))
    key_grad = dot(score_grad, queries, ((0,), (0,)))
    joined_grad = jnp.concatenate([query_grad, key_grad, value_grad], axis=1).astype(bf16)
    return context, joined_grad


def body(hidden_in, norm_gain, norm_bias, w_qkv, b_qkv, w_out, out_grad):
    n_tensor = lax.axis_size("tensor")
    depth = norm_gain.shape[0]
    width = depth // n_tensor
    part = width // 2
    quarter = Z_COUNT * part
    rank = lax.axis_index("tensor")
    z, far = rank % Z_COUNT, rank // Z_COUNT
    parity = z % 2
    dp = lax.axis_index("dp")
    core, x, y = dp % 2, dp // 2 % X_COUNT, dp // (2 * X_COUNT)
    lines = groups(lax.axis_size("dp"), lambda i: i % (2 * X_COUNT))
    rings = groups(n_tensor, lambda i: i % 2)

    def pick(condition, pair):
        return tuple(jnp.where(condition, p, q) for p, q in (pair, pair[::-1]))

    hidden_t = hidden_in.T
    acts = jnp.concatenate([hidden_t, out_grad.T], axis=1).reshape(2, part, 2 * SEQ)
    mine = jnp.where(core == 0, acts[0], acts[1])
    other = swap_cores(jnp.where(core == 0, acts[1], acts[0]))
    block = jnp.concatenate([mine[:, :SEQ], other[:, :SEQ], mine[:, SEQ:], other[:, SEQ:]], axis=1)

    weight_block = to_pair(jnp.concatenate([w_qkv, w_out.T], axis=1), 0)
    pair = jnp.stack(pick(far == 0, (block, swap_far(block))))
    weight_block, pair = lax.optimization_barrier((weight_block, pair))
    column = lax.all_gather(weight_block, "dp", axis=0, axis_index_groups=lines)
    rows = z_gather(pair, z // 2).reshape(quarter, 4 * SEQ)
    hidden = rows[:, : 2 * SEQ].astype(f32)
    grads = rows[:, 2 * SEQ :]
    blocks = x_gather(column)
    mean_part = jnp.sum(hidden, axis=0) / quarter
    stats = jnp.stack([mean_part, jnp.sum((hidden - mean_part) ** 2, axis=0)])

    def merge(stats, stats_other, count):
        gap = stats[0] - stats_other[0]
        return jnp.stack(
            [
                0.5 * (stats[0] + stats_other[0]),
                stats[1] + stats_other[1] + gap * gap * (count / 2),
            ]
        )

    stats = merge(stats, swap_heads(stats), quarter)
    stats_other = swap_cores(stats)
    stats_other = jnp.concatenate([stats_other[:, SEQ:], stats_other[:, :SEQ]], axis=1)
    stats = merge(stats, stats_other, 2 * quarter)
    mean = stats[0]
    inv_std = lax.rsqrt(stats[1] / depth + norm_eps)

    def own_part(vector):
        vector = vector.reshape(Z_COUNT, 2, 2, part)
        vector = jnp.where(parity == 0, vector[:, 0], vector[:, 1])
        return jnp.where(core == 0, vector[:, 0], vector[:, 1]).reshape(quarter)

    gain, bias = own_part(norm_gain), own_part(norm_bias)
    normed = ((hidden - mean) * inv_std * gain[:, None] + bias[:, None]).astype(bf16)
    vectors = jnp.stack([*split(gain), *split(bias)] + [jnp.zeros_like(gain, bf16)] * 4)
    left = jnp.concatenate([normed, vectors.T], axis=1)
    left = left.reshape(4, 2, part, 2 * SEQ + 8)
    right = grads.reshape(4, 2, part, 2 * SEQ)

    joined_parts, grad_parts = [0.0, 0.0], [0.0, 0.0]
    for step in (0, 3, 1, 2):
        half = (x + step) % X_COUNT // 2
        left_part = jnp.where(half == 0, left[:, 0], left[:, 1]).reshape(quarter // 2, -1)
        right_part = jnp.where(half == 0, right[:, 0], right[:, 1]).reshape(quarter // 2, -1)
        weight = blocks[step].reshape(quarter // 2, 4 * E)
        joined_parts[step % 2] += dot(left_part, weight[:, : 3 * E], ((0,), (0,)))
        grad_parts[step % 2] += dot(right_part, weight[:, 3 * E :], ((0,), (0,)))
    parts = []
    for j, g in zip(joined_parts, grad_parts):
        v = j[2 * SEQ :]
        v = jnp.stack([v[0] + v[1], v[2] + v[3]])
        parts.append((jnp.concatenate([j[: 2 * SEQ], g], axis=1), jnp.pad(v, ((0, 6), (0, E)))))
    sent = jnp.stack([jnp.concatenate([p[SEQ:], v]) for p, v in parts])
    kept = jnp.stack([jnp.concatenate([p[:SEQ], v]) for p, v in parts])
    own_first = x % 2 == parity
    own, away = pick(own_first, tuple(kept + swap_cores(sent)))
    away_high, away_low = split(away[SEQ:])
    away = swap_heads(jnp.concatenate([away[:SEQ].astype(bf16), away_high, away_low]))
    away = away.astype(f32)
    vector = own[SEQ:] + away[SEQ : SEQ + 8] + away[SEQ + 8 :]
    gain_weight, bias_weight = vector[0, : 3 * E], vector[1, : 3 * E]
    whole = own[:SEQ] + away[:SEQ]
    plain = whole[:, : 3 * E]
    joined = (plain + b_qkv).astype(bf16)
    context_grad = whole[:, 3 * E :].astype(bf16)

    slope = 2.0 ** (-8.0 * (rank + 1).astype(f32) / n_tensor)
    context, joined_grad = attention(joined, context_grad, slope)
    joined_grad_f = joined_grad.astype(f32)
    sums = jnp.stack(
        [
            jnp.sum(joined_grad_f * gain_weight, axis=1),
            jnp.sum(joined_grad_f * (plain - bias_weight), axis=1),
        ]
    )

    def pack(sums):
        high, low = split(sums)
        return jnp.concatenate([high, low, jnp.zeros((12, sums.shape[1]), bf16)])

    def unpack(rows):
        rows = rows.astype(f32)
        return rows[0:2] + rows[2:4]

    packed = jnp.pad(pack(sums), ((0, 0), (0, 3 * E)))
    result = jnp.concatenate([jnp.concatenate([context, joined_grad], axis=1), packed])
    result_pair = swap_heads(result)
    sums = sums + unpack(result_pair[SEQ:, :SEQ])
    heads = jnp.stack(pick(own_first, (result[:SEQ], result_pair[:SEQ])))
    packed = jnp.pad(pack(sums), ((0, 0), (0, 3 * E)))
    heads_sent = jnp.concatenate([heads, jnp.stack([packed, jnp.zeros_like(packed)])], axis=1)
    heads_other = swap_cores(heads_sent)
    sums = jnp.concatenate([sums, unpack(heads_other[0, SEQ:, :SEQ])], axis=1)
    heads = jnp.concatenate([heads, heads_other[:, :SEQ]], axis=1)

    weight_parts = [
        dot(grads, heads[h, :, :E], ((1,), (0,))).astype(bf16).reshape(4, 2, part, E)
        for h in range(2)
    ]

    def weight_to(step):
        pair = weight_parts[step % 2]
        return jnp.where((x + step) % X_COUNT // 2 == 0, pair[:, 0], pair[:, 1])

    across, heads = lax.optimization_barrier((weight_to(2), heads))

    near, away = pick(x % 2 == 0, (blocks[1][:, :, : 3 * E], blocks[3][:, :, : 3 * E]))

    def group_product(first, second):
        return sum(
            dot(w.reshape(quarter // 2, 3 * E), heads[h, :, E:], ((1,), (1,)))
            for h, w in enumerate((first[:, :, : 3 * E], second))
        ).astype(bf16).reshape(4, part, 2 * SEQ)

    group_part = pick(
        x // 2 == 0, (group_product(blocks[0], near), group_product(blocks[2], away))
    )
    group_part = jnp.stack(group_part, axis=1)
    extra = jnp.broadcast_to(pack(sums)[None], (Z_COUNT, 16, 2 * SEQ))
    payload = jnp.concatenate([group_part.reshape(Z_COUNT, part, 2 * SEQ), extra], axis=1)
    group_parts = lax.all_to_all(payload, "tensor", 0, 0, tiled=True, axis_index_groups=rings)
    total = jnp.sum(group_parts.astype(f32), axis=0)
    weight_parts = ring_scatter_x(weight_to, across)
    grad_out_weight, total = scatter_y(weight_parts, y, total)
    sums = total[part : part + 2, :SEQ] + total[part + 2 : part + 4, :SEQ]
    total = total[:part]
    total_other = swap_cores(total[:, SEQ:])
    total = total[:, :SEQ]
    normed_grad = jnp.where(
        core == 0,
        jnp.concatenate([total, total_other]),
        jnp.concatenate([total_other, total]),
    )
    mean_grad = sums[0] / depth
    mean_cross = sums[1] / depth

    own_gain = lax.dynamic_slice_in_dim(norm_gain, rank * width, width)
    scaled_grad = normed_grad * own_gain[:, None]
    scaled = (hidden_t.astype(f32) - mean[:SEQ]) * inv_std[:SEQ]
    input_grad = inv_std[:SEQ] * (scaled_grad - mean_grad - scaled * mean_cross)

    return input_grad.astype(bf16).T, grad_out_weight.T


def solution(mesh):
    in_specs = (
        P("dp", "tensor"),
        P(),
        P(),
        P("dp", "tensor"),
        P("tensor"),
        P("tensor", "dp"),
        P("dp", "tensor"),
    )
    out_specs = (P("dp", "tensor"), P("tensor", "dp"))
    return jax.shard_map(body, mesh=mesh, in_specs=in_specs, out_specs=out_specs, check_vma=False)
```

```python
import jax
import jax.numpy as jnp
from jax import lax
from jax.sharding import PartitionSpec as P

SEQ = 128
E = 128
Z_COUNT = 8
X_COUNT = 4
norm_eps = 1e-05
f32 = jnp.float32
bf16 = jnp.bfloat16


def groups(count, key):
    found = {}
    for i in range(count):
        found.setdefault(key(i), []).append(i)
    return [found[k] for k in sorted(found)]


def swap_cores(x):
    n = lax.axis_size("dp")
    return lax.ppermute(x, "dp", [(i, i ^ 1) for i in range(n)])


def shift_z(x, step):
    n = lax.axis_size("tensor")
    pairs = [(i, i - i % Z_COUNT + (i + step) % Z_COUNT) for i in range(n)]
    return lax.ppermute(x, "tensor", pairs)


def swap_far(x):
    n = lax.axis_size("tensor")
    return lax.ppermute(x, "tensor", [(i, (i + Z_COUNT) % n) for i in range(n)])


def shift_x(x, step):
    n = lax.axis_size("dp")
    row = 2 * X_COUNT
    return lax.ppermute(x, "dp", [(i, i - i % row + (i + 2 * step) % row) for i in range(n)])


def swap_heads(x):
    n = lax.axis_size("tensor")
    return lax.ppermute(x, "tensor", [(i, i ^ 1) for i in range(n)])


def to_pair(x, step):
    n_dp, n_tensor = lax.axis_size("dp"), lax.axis_size("tensor")
    row = 2 * X_COUNT
    pairs = []
    for d in range(n_dp):
        for t in range(n_tensor):
            same = d // 2 % 2 == t % 2
            to, head = (d, t) if same else (d ^ 2, t ^ 1)
            pairs.append((d * n_tensor + t, (to + row * step) % n_dp * n_tensor + head))
    return lax.ppermute(x, ("dp", "tensor"), pairs)


def gather_both(pair, place, column):
    middle = column.shape[0] // 2
    x_up, x_down = shift_x(column, 1), shift_x(column, -1)
    z_up, z_down = shift_z(pair, 2), shift_z(pair, -2)
    x_up, x_down, z_up, z_down = lax.optimization_barrier((x_up, x_down, z_up, z_down))
    x_across = jnp.concatenate([shift_x(x_up[:middle], 1), shift_x(x_down[middle:], -1)])
    z_across = jnp.concatenate([shift_z(z_up[:1], 2), shift_z(z_down[1:], -2)])
    count = Z_COUNT // 2
    line = jnp.stack([z_down, z_across, z_up, pair, z_down, z_across, z_up], axis=1)
    rows = lax.dynamic_slice_in_dim(line, count - 1 - place, count, 1)
    return rows, [column, x_down, x_across, x_up]


def ring_scatter_x(part, across):
    ahead = part(1).astype(f32) + shift_x(across, 1).astype(f32)
    up, down = shift_x(ahead.astype(bf16), 1), shift_x(part(-1), -1)
    return part(0).astype(f32) + up.astype(f32) + down.astype(f32)


def scatter_y(parts, place):
    count = parts.shape[0]
    sent = parts.astype(bf16)
    total = None
    for step in range(count):
        one = lax.dynamic_index_in_dim(sent, (place + step) % count, 0, keepdims=False)
        one = to_pair(one, step).astype(f32)
        total = one if total is None else total + one
    return total


def split(x):
    high = lax.reduce_precision(x, 8, 7)
    return high.astype(bf16), (x - high).astype(bf16)


def dot(a, b, dims):
    return lax.dot_general(a, b, (dims, ((), ())), preferred_element_type=f32)


def attention(joined, context_grad, slope):
    queries = joined[:, :E]
    key_rows = joined[:, E : 2 * E]
    values = joined[:, 2 * E :]
    scores = dot(queries, key_rows, ((1,), (1,))) * E ** (-0.5)
    row = lax.broadcasted_iota(jnp.int32, (SEQ, SEQ), 0)
    col = lax.broadcasted_iota(jnp.int32, (SEQ, SEQ), 1)
    offsets = (col - row).astype(f32)
    scores = jnp.where(offsets <= 0.0, scores + slope * offsets, -1e30)
    soft = jax.nn.softmax(scores, axis=-1)
    soft_round = soft.astype(bf16)
    context = dot(soft_round, values, ((1,), (0,))).astype(bf16)
    prob_grad = dot(context_grad, values, ((1,), (1,)))
    value_grad = dot(soft_round, context_grad, ((0,), (0,)))
    row_dot = jnp.sum(soft * prob_grad, axis=-1, keepdims=True)
    score_grad = (soft * (prob_grad - row_dot) * E ** (-0.5)).astype(bf16)
    query_grad = dot(score_grad, key_rows, ((1,), (0,)))
    key_grad = dot(score_grad, queries, ((0,), (0,)))
    joined_grad = jnp.concatenate([query_grad, key_grad, value_grad], axis=1).astype(bf16)
    return context, joined_grad


def body(hidden_in, norm_gain, norm_bias, w_qkv, b_qkv, w_out, out_grad):
    n_tensor = lax.axis_size("tensor")
    depth = norm_gain.shape[0]
    width = depth // n_tensor
    part = width // 2
    quarter = Z_COUNT * part
    rank = lax.axis_index("tensor")
    z, far = rank % Z_COUNT, rank // Z_COUNT
    parity = z % 2
    dp = lax.axis_index("dp")
    core, x, y = dp % 2, dp // 2 % X_COUNT, dp // (2 * X_COUNT)
    lines = groups(lax.axis_size("dp"), lambda i: i % (2 * X_COUNT))
    rings = groups(n_tensor, lambda i: i % 2)

    def pick(condition, pair):
        return tuple(jnp.where(condition, p, q) for p, q in (pair, pair[::-1]))

    hidden_t = hidden_in.T
    acts = jnp.concatenate([hidden_t, out_grad.T], axis=1).reshape(2, part, 2 * SEQ)
    mine = jnp.where(core == 0, acts[0], acts[1])
    other = swap_cores(jnp.where(core == 0, acts[1], acts[0]))
    block = jnp.concatenate([mine[:, :SEQ], other[:, :SEQ], mine[:, SEQ:], other[:, SEQ:]], axis=1)

    weight_block = to_pair(jnp.concatenate([w_qkv, w_out.T], axis=1), 0)

    slice_f = hidden_t.astype(f32)
    mean_part = jnp.mean(slice_f, axis=0)
    stats = jnp.stack([mean_part, jnp.sum((slice_f - mean_part) ** 2, axis=0)])
    stats = lax.all_to_all(
        jnp.broadcast_to(stats[None], (n_tensor, 2, SEQ)), "tensor", 0, 0, tiled=True
    )
    weight_block, stats = lax.optimization_barrier((weight_block, stats))
    column = lax.all_gather(weight_block, "dp", axis=0, axis_index_groups=lines)
    mean = jnp.mean(stats[:, 0], axis=0)
    square = jnp.sum(stats[:, 1], axis=0) + width * jnp.sum((stats[:, 0] - mean) ** 2, axis=0)
    stats = jnp.stack([mean, lax.rsqrt(square / depth + norm_eps)])
    mean, inv_std = jnp.concatenate([stats, swap_cores(stats)], axis=1)

    pair = jnp.stack(pick(far == 0, (block, swap_far(block))))
    column, pair = lax.optimization_barrier((column, pair))
    rows, blocks = gather_both(pair, z // 2, column)
    rows = rows.reshape(quarter, 4 * SEQ)
    hidden = rows[:, : 2 * SEQ].astype(f32)
    grads = rows[:, 2 * SEQ :]

    def own_part(vector):
        vector = vector.reshape(Z_COUNT, 2, 2, part)
        vector = jnp.where(parity == 0, vector[:, 0], vector[:, 1])
        return jnp.where(core == 0, vector[:, 0], vector[:, 1]).reshape(quarter)

    gain, bias = own_part(norm_gain), own_part(norm_bias)
    normed = ((hidden - mean) * inv_std * gain[:, None] + bias[:, None]).astype(bf16)
    vectors = jnp.stack([*split(gain), *split(bias)] + [jnp.zeros_like(gain, bf16)] * 4)
    left = jnp.concatenate([normed, vectors.T], axis=1)
    left = left.reshape(4, 2, part, 2 * SEQ + 8)
    right = grads.reshape(4, 2, part, 2 * SEQ)

    joined_parts, grad_parts = [0.0, 0.0], [0.0, 0.0]
    for step in (0, 3, 1, 2):
        half = (x + step) % X_COUNT // 2
        left_part = jnp.where(half == 0, left[:, 0], left[:, 1]).reshape(quarter // 2, -1)
        right_part = jnp.where(half == 0, right[:, 0], right[:, 1]).reshape(quarter // 2, -1)
        weight = blocks[step].reshape(quarter // 2, 4 * E)
        joined_parts[step % 2] += dot(left_part, weight[:, : 3 * E], ((0,), (0,)))
        grad_parts[step % 2] += dot(right_part, weight[:, 3 * E :], ((0,), (0,)))
    parts = []
    for j, g in zip(joined_parts, grad_parts):
        v = j[2 * SEQ :]
        v = jnp.stack([v[0] + v[1], v[2] + v[3]])
        parts.append((jnp.concatenate([j[: 2 * SEQ], g], axis=1), jnp.pad(v, ((0, 6), (0, E)))))
    sent = jnp.stack([jnp.concatenate([p[SEQ:], v]) for p, v in parts])
    kept = jnp.stack([jnp.concatenate([p[:SEQ], v]) for p, v in parts])
    own_first = x % 2 == parity
    own, away = pick(own_first, tuple(kept + swap_cores(sent)))
    away_high, away_low = split(away[SEQ:])
    away = swap_heads(jnp.concatenate([away[:SEQ].astype(bf16), away_high, away_low]))
    away = away.astype(f32)
    vector = own[SEQ:] + away[SEQ : SEQ + 8] + away[SEQ + 8 :]
    gain_weight, bias_weight = vector[0, : 3 * E], vector[1, : 3 * E]
    whole = own[:SEQ] + away[:SEQ]
    plain = whole[:, : 3 * E]
    joined = (plain + b_qkv).astype(bf16)
    context_grad = whole[:, 3 * E :].astype(bf16)

    slope = 2.0 ** (-8.0 * (rank + 1).astype(f32) / n_tensor)
    context, joined_grad = attention(joined, context_grad, slope)
    joined_grad_f = joined_grad.astype(f32)
    sums = jnp.stack(
        [
            jnp.sum(joined_grad_f * gain_weight, axis=1),
            jnp.sum(joined_grad_f * (plain - bias_weight), axis=1),
        ]
    )

    def pack(sums):
        high, low = split(sums)
        return jnp.concatenate([high, low, jnp.zeros((12, sums.shape[1]), bf16)])

    def unpack(rows):
        rows = rows.astype(f32)
        return rows[0:2] + rows[2:4]

    packed = jnp.pad(pack(sums), ((0, 0), (0, 3 * E)))
    result = jnp.concatenate([jnp.concatenate([context, joined_grad], axis=1), packed])
    result_pair = swap_heads(result)
    sums = sums + unpack(result_pair[SEQ:, :SEQ])
    heads = jnp.stack(pick(own_first, (result[:SEQ], result_pair[:SEQ])))
    packed = jnp.pad(pack(sums), ((0, 0), (0, 3 * E)))
    heads_sent = jnp.concatenate([heads, jnp.stack([packed, jnp.zeros_like(packed)])], axis=1)
    heads_other = swap_cores(heads_sent)
    sums = jnp.concatenate([sums, unpack(heads_other[0, SEQ:, :SEQ])], axis=1)
    heads = jnp.concatenate([heads, heads_other[:, :SEQ]], axis=1)

    weight_parts = [
        dot(grads, heads[h, :, :E], ((1,), (0,))).astype(bf16).reshape(4, 2, part, E)
        for h in range(2)
    ]

    def weight_to(step):
        pair = weight_parts[step % 2]
        return jnp.where((x + step) % X_COUNT // 2 == 0, pair[:, 0], pair[:, 1])

    across, heads = lax.optimization_barrier((weight_to(2), heads))

    products = [
        dot(w[:, :, : 3 * E].reshape(quarter // 2, 3 * E), heads[i % 2, :, E:], ((1,), (1,)))
        for i, w in enumerate(blocks)
    ]
    near, away = pick(x % 2 == 0, (products[1], products[3]))
    group_part = pick(x // 2 == 0, (products[0] + near, products[2] + away))
    group_part = jnp.stack([g.astype(bf16).reshape(4, part, 2 * SEQ) for g in group_part], axis=1)
    extra = jnp.broadcast_to(pack(sums)[None], (Z_COUNT, 16, 2 * SEQ))
    payload = jnp.concatenate([group_part.reshape(Z_COUNT, part, 2 * SEQ), extra], axis=1)
    group_parts = lax.all_to_all(payload, "tensor", 0, 0, tiled=True, axis_index_groups=rings)
    total = jnp.sum(group_parts.astype(f32), axis=0)
    weight_parts = ring_scatter_x(weight_to, across)
    grad_out_weight = scatter_y(weight_parts, y)
    sums = total[part : part + 2, :SEQ] + total[part + 2 : part + 4, :SEQ]
    total = total[:part]
    total_other = swap_cores(total[:, SEQ:])
    total = total[:, :SEQ]
    normed_grad = jnp.where(
        core == 0,
        jnp.concatenate([total, total_other]),
        jnp.concatenate([total_other, total]),
    )
    mean_grad = sums[0] / depth
    mean_cross = sums[1] / depth

    own_gain = lax.dynamic_slice_in_dim(norm_gain, rank * width, width)
    scaled_grad = normed_grad * own_gain[:, None]
    scaled = (hidden_t.astype(f32) - mean[:SEQ]) * inv_std[:SEQ]
    input_grad = inv_std[:SEQ] * (scaled_grad - mean_grad - scaled * mean_cross)

    return input_grad.astype(bf16).T, grad_out_weight.T


def solution(mesh):
    in_specs = (
        P("dp", "tensor"),
        P(),
        P(),
        P("dp", "tensor"),
        P("tensor"),
        P("tensor", "dp"),
        P("dp", "tensor"),
    )
    out_specs = (P("dp", "tensor"), P("tensor", "dp"))
    return jax.shard_map(body, mesh=mesh, in_specs=in_specs, out_specs=out_specs, check_vma=False)
```

```python
import jax
import jax.numpy as jnp
from jax import lax
from jax.sharding import PartitionSpec as P

SEQ = 128
E = 128
Z_COUNT = 8
X_COUNT = 4
norm_eps = 1e-05
f32 = jnp.float32
bf16 = jnp.bfloat16


def groups(count, key):
    found = {}
    for i in range(count):
        found.setdefault(key(i), []).append(i)
    return [found[k] for k in sorted(found)]


def swap_cores(x):
    n = lax.axis_size("dp")
    return lax.ppermute(x, "dp", [(i, i ^ 1) for i in range(n)])


def shift_z(x, step):
    n = lax.axis_size("tensor")
    pairs = [(i, i - i % Z_COUNT + (i + step) % Z_COUNT) for i in range(n)]
    return lax.ppermute(x, "tensor", pairs)


def swap_far(x):
    n = lax.axis_size("tensor")
    return lax.ppermute(x, "tensor", [(i, (i + Z_COUNT) % n) for i in range(n)])


def shift_x(x, step):
    n = lax.axis_size("dp")
    row = 2 * X_COUNT
    return lax.ppermute(x, "dp", [(i, i - i % row + (i + 2 * step) % row) for i in range(n)])


def along_y(x, target):
    n_dp, n_tensor = lax.axis_size("dp"), lax.axis_size("tensor")
    row = 2 * X_COUNT
    pairs = []
    for d in range(n_dp):
        for t in range(n_tensor):
            half, place = target(t // Z_COUNT, d // row)
            to = (place * row + d % row) * n_tensor + half * Z_COUNT + t % Z_COUNT
            pairs.append((d * n_tensor + t, to))
    return lax.ppermute(x, ("dp", "tensor"), pairs)


def move_weights(x):
    return along_y(x, lambda half, place: (place // 2, 2 * half + place % 2))


def x_gather(own, place, early):
    middle = own.shape[0] // 2
    up, down = shift_x(own, 1), shift_x(own, -1)
    up, down, early = lax.optimization_barrier((up, down, early))
    across = jnp.concatenate([shift_x(up[:middle], 1), shift_x(down[middle:], -1)])
    return [own, down, across, up], early


def in_order(blocks, place):
    line = jnp.stack(blocks[1:] + blocks, axis=1)
    return lax.dynamic_slice_in_dim(line, X_COUNT - 1 - place, X_COUNT, 1)


def ring_scatter_x(part, across):
    ahead = part(1).astype(f32) + shift_x(across, 1).astype(f32)
    up, down = shift_x(ahead.astype(bf16), 1), shift_x(part(-1), -1)
    return part(0).astype(f32) + up.astype(f32) + down.astype(f32)


def scatter_y(parts, place):
    count = parts.shape[0]
    sent = parts.astype(bf16)
    total = None
    for step in range(count):
        one = lax.dynamic_index_in_dim(sent, (place + step) % count, 0, keepdims=False)

        def target(half, place):
            part = (place + step) % count
            return part // 2, 2 * half + part % 2

        one = along_y(one, target).astype(f32)
        total = one if total is None else total + one
    return total


def split(x):
    high = lax.reduce_precision(x, 8, 7)
    return high.astype(bf16), (x - high).astype(bf16)


def dot(a, b, dims):
    return lax.dot_general(a, b, (dims, ((), ())), preferred_element_type=f32)


def attention(joined, context_grad, slope):
    queries = joined[:, :E]
    key_rows = joined[:, E : 2 * E]
    values = joined[:, 2 * E :]
    scores = dot(queries, key_rows, ((1,), (1,))) * E ** (-0.5)
    row = lax.broadcasted_iota(jnp.int32, (SEQ, SEQ), 0)
    col = lax.broadcasted_iota(jnp.int32, (SEQ, SEQ), 1)
    offsets = (col - row).astype(f32)
    scores = jnp.where(offsets <= 0.0, scores + slope * offsets, -1e30)
    soft = jax.nn.softmax(scores, axis=-1)
    soft_round = soft.astype(bf16)
    context = dot(soft_round, values, ((1,), (0,))).astype(bf16)
    prob_grad = dot(context_grad, values, ((1,), (1,)))
    value_grad = dot(soft_round, context_grad, ((0,), (0,)))
    row_dot = jnp.sum(soft * prob_grad, axis=-1, keepdims=True)
    score_grad = (soft * (prob_grad - row_dot) * E ** (-0.5)).astype(bf16)
    query_grad = dot(score_grad, key_rows, ((1,), (0,)))
    key_grad = dot(score_grad, queries, ((0,), (0,)))
    joined_grad = jnp.concatenate([query_grad, key_grad, value_grad], axis=1).astype(bf16)
    return context, joined_grad


def body(hidden_in, norm_gain, norm_bias, w_qkv, b_qkv, w_out, out_grad):
    n_tensor = lax.axis_size("tensor")
    depth = norm_gain.shape[0]
    width = depth // n_tensor
    part = width // 2
    quarter = Z_COUNT * part
    rank = lax.axis_index("tensor")
    z, far = rank % Z_COUNT, rank // Z_COUNT
    dp = lax.axis_index("dp")
    core, x, y = dp % 2, dp // 2 % X_COUNT, dp // (2 * X_COUNT)
    lines = groups(lax.axis_size("dp"), lambda i: i % (2 * X_COUNT))
    rings = groups(n_tensor, lambda i: i // Z_COUNT)

    def by_far(own, other):
        return jnp.stack([jnp.where(far == 0, own, other), jnp.where(far == 0, other, own)])

    hidden_t = hidden_in.T
    acts = jnp.concatenate([hidden_t, out_grad.T], axis=1).reshape(2, part, 2 * SEQ)
    mine = jnp.where(core == 0, acts[0], acts[1])
    other = swap_cores(jnp.where(core == 0, acts[1], acts[0]))
    block = jnp.concatenate([mine[:, :SEQ], other[:, :SEQ], mine[:, SEQ:], other[:, SEQ:]], axis=1)

    weight_block = move_weights(jnp.concatenate([w_qkv, w_out.T], axis=1))

    slice_f = hidden_t.astype(f32)
    mean_part = jnp.mean(slice_f, axis=0)
    stats = jnp.stack([mean_part, jnp.sum((slice_f - mean_part) ** 2, axis=0)])
    block, stats = lax.optimization_barrier((block, stats))
    stats = lax.all_to_all(
        jnp.broadcast_to(stats[None], (n_tensor, 2, SEQ)), "tensor", 0, 0, tiled=True
    )
    weight_block, stats = lax.optimization_barrier((weight_block, stats))
    column = lax.all_gather(weight_block, "dp", axis=0, axis_index_groups=lines)
    mean = jnp.mean(stats[:, 0], axis=0)
    square = jnp.sum(stats[:, 1], axis=0) + width * jnp.sum((stats[:, 0] - mean) ** 2, axis=0)
    stats = jnp.stack([mean, lax.rsqrt(square / depth + norm_eps)])
    mean, inv_std = jnp.concatenate([stats, swap_cores(stats)], axis=1)

    rows = lax.all_gather(block, "tensor", axis=0, tiled=True, axis_index_groups=rings)
    blocks, rows = x_gather(column, x, rows)
    hidden = rows[:, : 2 * SEQ].astype(f32)
    grads = rows[:, 2 * SEQ :]

    def own_part(vector):
        vector = vector.reshape(2, Z_COUNT, 2, part)
        vector = jnp.where(far == 0, vector[0], vector[1])
        return jnp.where(core == 0, vector[:, 0], vector[:, 1]).reshape(quarter)

    gain, bias = own_part(norm_gain), own_part(norm_bias)
    normed = ((hidden - mean) * inv_std * gain[:, None] + bias[:, None]).astype(bf16)
    vectors = jnp.stack([*split(gain), *split(bias)] + [jnp.zeros_like(gain, bf16)] * 4)
    left = jnp.concatenate([normed, vectors.T], axis=1).reshape(2, X_COUNT, part, 2 * SEQ + 8)
    right = grads.reshape(2, X_COUNT, part, 2 * SEQ)

    def own_head(pair):
        return jnp.where(far == 0, pair[0], pair[1]), jnp.where(far == 0, pair[1], pair[0])

    joined_parts, grad_parts = [0.0, 0.0], [0.0, 0.0]
    for step in (0, 3, 1, 2):
        place = (x + step) % X_COUNT
        left_part = lax.dynamic_index_in_dim(left, place, 1, keepdims=False)
        right_part = lax.dynamic_index_in_dim(right, place, 1, keepdims=False)
        left_part = left_part.reshape(2 * part, 2 * SEQ + 8)
        right_part = right_part.reshape(2 * part, 2 * SEQ)
        for h in range(2):
            weight = blocks[step][2 * h : 2 * h + 2].reshape(2 * part, 4 * E)
            joined_parts[h] += dot(left_part, weight[:, : 3 * E], ((0,), (0,)))
            grad_parts[h] += dot(right_part, weight[:, 3 * E :], ((0,), (0,)))
    parts = []
    for j, g in zip(joined_parts, grad_parts):
        v = j[2 * SEQ :]
        v = jnp.stack([v[0] + v[1], v[2] + v[3]])
        parts.append((jnp.concatenate([j[: 2 * SEQ], g], axis=1), jnp.pad(v, ((0, 6), (0, E)))))
    sent = jnp.stack([jnp.concatenate([p[SEQ:], v]) for p, v in parts])
    kept = jnp.stack([jnp.concatenate([p[:SEQ], v]) for p, v in parts])
    own, away = own_head(kept + swap_cores(sent))
    away_high, away_low = split(away[SEQ:])
    away = swap_far(jnp.concatenate([away[:SEQ].astype(bf16), away_high, away_low]))
    away = away.astype(f32)
    vector = own[SEQ:] + away[SEQ : SEQ + 8] + away[SEQ + 8 :]
    gain_weight, bias_weight = vector[0, : 3 * E], vector[1, : 3 * E]
    whole = own[:SEQ] + away[:SEQ]
    plain = whole[:, : 3 * E]
    joined = (plain + b_qkv).astype(bf16)
    context_grad = whole[:, 3 * E :].astype(bf16)

    slope = 2.0 ** (-8.0 * (rank + 1).astype(f32) / n_tensor)
    context, joined_grad = attention(joined, context_grad, slope)
    joined_grad_f = joined_grad.astype(f32)
    sums = jnp.stack(
        [
            jnp.sum(joined_grad_f * gain_weight, axis=1),
            jnp.sum(joined_grad_f * (plain - bias_weight), axis=1),
        ]
    )

    def pack(sums):
        high, low = split(sums)
        return jnp.concatenate([high, low, jnp.zeros((12, sums.shape[1]), bf16)])

    def unpack(rows):
        rows = rows.astype(f32)
        return rows[0:2] + rows[2:4]

    packed = jnp.pad(pack(sums), ((0, 0), (0, 3 * E)))
    result = jnp.concatenate([jnp.concatenate([context, joined_grad], axis=1), packed])
    result_far = swap_far(result)
    sums = sums + unpack(result_far[SEQ:, :SEQ])
    heads = by_far(result[:SEQ], result_far[:SEQ])
    packed = jnp.pad(pack(sums), ((0, 0), (0, 3 * E)))
    heads_sent = jnp.concatenate([heads, jnp.stack([packed, jnp.zeros_like(packed)])], axis=1)
    heads_other = swap_cores(heads_sent)
    sums = jnp.concatenate([sums, unpack(heads_other[0, SEQ:, :SEQ])], axis=1)
    heads = jnp.concatenate([heads, heads_other[:, :SEQ]], axis=1)

    joined_weight = in_order([b[:, :, : 3 * E] for b in blocks], x).reshape(2, quarter, 3 * E)
    weight_parts = [
        dot(grads, heads[h, :, :E], ((1,), (0,))).astype(bf16).reshape(2, X_COUNT, part, E)
        for h in range(2)
    ]

    def weight_to(step):
        place = (x + step) % X_COUNT
        return jnp.concatenate(
            [lax.dynamic_index_in_dim(w, place, 1, keepdims=False) for w in weight_parts]
        )

    across, heads = lax.optimization_barrier((weight_to(2), heads))

    group_part = sum(
        dot(joined_weight[h], heads[h, :, E:], ((1,), (1,))) for h in range(2)
    ).astype(bf16)
    extra = jnp.broadcast_to(pack(sums)[None], (Z_COUNT, 16, 2 * SEQ))
    payload = jnp.concatenate([group_part.reshape(Z_COUNT, part, 2 * SEQ), extra], axis=1)
    group_parts = lax.all_to_all(payload, "tensor", 0, 0, tiled=True, axis_index_groups=rings)
    total = jnp.sum(group_parts.astype(f32), axis=0)
    weight_parts = ring_scatter_x(weight_to, across)
    grad_out_weight = scatter_y(weight_parts, y)
    sums = total[part : part + 2, :SEQ] + total[part + 2 : part + 4, :SEQ]
    total = total[:part]
    total_other = swap_cores(total[:, SEQ:])
    total = total[:, :SEQ]
    normed_grad = jnp.where(
        core == 0,
        jnp.concatenate([total, total_other]),
        jnp.concatenate([total_other, total]),
    )
    mean_grad = sums[0] / depth
    mean_cross = sums[1] / depth

    own_gain = lax.dynamic_slice_in_dim(norm_gain, rank * width, width)
    scaled_grad = normed_grad * own_gain[:, None]
    scaled = (hidden_t.astype(f32) - mean[:SEQ]) * inv_std[:SEQ]
    input_grad = inv_std[:SEQ] * (scaled_grad - mean_grad - scaled * mean_cross)

    return input_grad.astype(bf16).T, grad_out_weight.T


def solution(mesh):
    in_specs = (
        P("dp", "tensor"),
        P(),
        P(),
        P("dp", "tensor"),
        P("tensor"),
        P("tensor", "dp"),
        P("dp", "tensor"),
    )
    out_specs = (P("dp", "tensor"), P("tensor", "dp"))
    return jax.shard_map(body, mesh=mesh, in_specs=in_specs, out_specs=out_specs, check_vma=False)
```

```python
import jax
import jax.numpy as jnp
from jax import lax
from jax.sharding import PartitionSpec as P

SEQ = 128
E = 128
Z_COUNT = 8
X_COUNT = 4
norm_eps = 1e-05
f32 = jnp.float32
bf16 = jnp.bfloat16


def groups(count, key):
    found = {}
    for i in range(count):
        found.setdefault(key(i), []).append(i)
    return [found[k] for k in sorted(found)]


def swap_cores(x):
    n = lax.axis_size("dp")
    return lax.ppermute(x, "dp", [(i, i ^ 1) for i in range(n)])


def shift_z(x, step):
    n = lax.axis_size("tensor")
    pairs = [(i, i - i % Z_COUNT + (i + step) % Z_COUNT) for i in range(n)]
    return lax.ppermute(x, "tensor", pairs)


def swap_far(x):
    n = lax.axis_size("tensor")
    return lax.ppermute(x, "tensor", [(i, (i + Z_COUNT) % n) for i in range(n)])


def shift_x(x, step):
    n = lax.axis_size("dp")
    row = 2 * X_COUNT
    return lax.ppermute(x, "dp", [(i, i - i % row + (i + 2 * step) % row) for i in range(n)])


def along_y(x, target):
    n_dp, n_tensor = lax.axis_size("dp"), lax.axis_size("tensor")
    row = 2 * X_COUNT
    pairs = []
    for d in range(n_dp):
        for t in range(n_tensor):
            half, place = target(t // Z_COUNT, d // row)
            to = (place * row + d % row) * n_tensor + half * Z_COUNT + t % Z_COUNT
            pairs.append((d * n_tensor + t, to))
    return lax.ppermute(x, ("dp", "tensor"), pairs)


def move_weights(x):
    return along_y(x, lambda half, place: (place // 2, 2 * half + place % 2))


def x_gather(own, place, early):
    middle = own.shape[0] // 2
    up, down = shift_x(own, 1), shift_x(own, -1)
    up, down, early = lax.optimization_barrier((up, down, early))
    across = jnp.concatenate([shift_x(up[:middle], 1), shift_x(down[middle:], -1)])
    return [own, down, across, up], early


def in_order(blocks, place):
    line = jnp.stack(blocks[1:] + blocks, axis=1)
    return lax.dynamic_slice_in_dim(line, X_COUNT - 1 - place, X_COUNT, 1)


def scatter_x(part, across):
    total = part(0).astype(f32) + shift_x(across, 2).astype(f32)
    return total + shift_x(part(1), 1).astype(f32) + shift_x(part(-1), -1).astype(f32)


def scatter_y(parts, place):
    count = parts.shape[0]
    sent = parts.astype(bf16)
    total = None
    for step in range(count):
        one = lax.dynamic_index_in_dim(sent, (place + step) % count, 0, keepdims=False)

        def target(half, place):
            part = (place + step) % count
            return part // 2, 2 * half + part % 2

        one = along_y(one, target).astype(f32)
        total = one if total is None else total + one
    return total


def split(x):
    high = lax.reduce_precision(x, 8, 7)
    return high.astype(bf16), lax.reduce_precision(x - high, 8, 7).astype(bf16)


def dot(a, b, dims):
    return lax.dot_general(a, b, (dims, ((), ())), preferred_element_type=f32)


def attention(joined, context_grad, slope):
    queries = joined[:, :E]
    key_rows = joined[:, E : 2 * E]
    values = joined[:, 2 * E :]
    scores = dot(queries, key_rows, ((1,), (1,))) * E ** (-0.5)
    row = lax.broadcasted_iota(jnp.int32, (SEQ, SEQ), 0)
    col = lax.broadcasted_iota(jnp.int32, (SEQ, SEQ), 1)
    offsets = (col - row).astype(f32)
    scores = jnp.where(offsets <= 0.0, scores + slope * offsets, -1e30)
    soft = jax.nn.softmax(scores, axis=-1)
    soft_round = soft.astype(bf16)
    context = dot(soft_round, values, ((1,), (0,))).astype(bf16)
    prob_grad = dot(context_grad, values, ((1,), (1,)))
    value_grad = dot(soft_round, context_grad, ((0,), (0,)))
    row_dot = jnp.sum(soft * prob_grad, axis=-1, keepdims=True)
    score_grad = (soft * (prob_grad - row_dot) * E ** (-0.5)).astype(bf16)
    query_grad = dot(score_grad, key_rows, ((1,), (0,)))
    key_grad = dot(score_grad, queries, ((0,), (0,)))
    joined_grad = jnp.concatenate([query_grad, key_grad, value_grad], axis=1).astype(bf16)
    return context, joined_grad


def body(hidden_in, norm_gain, norm_bias, w_qkv, b_qkv, w_out, out_grad):
    n_tensor = lax.axis_size("tensor")
    depth = norm_gain.shape[0]
    width = depth // n_tensor
    part = width // 2
    quarter = Z_COUNT * part
    rank = lax.axis_index("tensor")
    z, far = rank % Z_COUNT, rank // Z_COUNT
    dp = lax.axis_index("dp")
    core, x, y = dp % 2, dp // 2 % X_COUNT, dp // (2 * X_COUNT)
    lines = groups(lax.axis_size("dp"), lambda i: i % (2 * X_COUNT))
    rings = groups(n_tensor, lambda i: i // Z_COUNT)

    def by_far(own, other):
        return jnp.stack([jnp.where(far == 0, own, other), jnp.where(far == 0, other, own)])

    hidden_t = hidden_in.T
    acts = jnp.concatenate([hidden_t, out_grad.T], axis=1).reshape(2, part, 2 * SEQ)
    mine = jnp.where(core == 0, acts[0], acts[1])
    other = swap_cores(jnp.where(core == 0, acts[1], acts[0]))
    block = jnp.concatenate([mine[:, :SEQ], other[:, :SEQ], mine[:, SEQ:], other[:, SEQ:]], axis=1)

    weight_block = move_weights(jnp.concatenate([w_qkv, w_out.T], axis=1))

    slice_f = hidden_t.astype(f32)
    mean_part = jnp.mean(slice_f, axis=0)
    stats = jnp.stack([mean_part, jnp.sum((slice_f - mean_part) ** 2, axis=0)])
    stats_far = swap_far(stats)
    gap = stats[0] - stats_far[0]
    stats = jnp.stack(
        [
            0.5 * (stats[0] + stats_far[0]),
            stats[1] + stats_far[1] + gap * gap * (width / 2),
        ]
    )
    stats = jnp.concatenate([stats, swap_cores(stats)], axis=1).reshape(1, 4 * SEQ)
    high, low = split(stats)
    lower = (stats - high.astype(f32) - low.astype(f32)).astype(bf16)
    block = jnp.concatenate([block, high, low, lower, jnp.zeros((13, 4 * SEQ), bf16)])

    weight_block, block = lax.optimization_barrier((weight_block, block))
    rows = lax.all_gather(block, "tensor", axis=0, axis_index_groups=rings)
    column = lax.all_gather(weight_block, "dp", axis=0, axis_index_groups=lines)
    blocks, rows = x_gather(column, x, rows)
    hidden = rows[:, :part, : 2 * SEQ].reshape(quarter, 2 * SEQ).astype(f32)
    grads = rows[:, :part, 2 * SEQ :].reshape(quarter, 2 * SEQ)
    stats = jnp.sum(rows[:, part : part + 3].astype(f32), axis=1)
    mean = jnp.mean(stats[:, : 2 * SEQ], axis=0)
    gap = stats[:, : 2 * SEQ] - mean
    square = jnp.sum(stats[:, 2 * SEQ :], axis=0) + 2 * width * jnp.sum(gap * gap, axis=0)
    inv_std = lax.rsqrt(square / depth + norm_eps)

    def own_part(vector):
        vector = vector.reshape(2, Z_COUNT, 2, part)
        vector = jnp.where(far == 0, vector[0], vector[1])
        return jnp.where(core == 0, vector[:, 0], vector[:, 1]).reshape(quarter)

    gain, bias = own_part(norm_gain), own_part(norm_bias)
    normed = ((hidden - mean) * inv_std * gain[:, None] + bias[:, None]).astype(bf16)
    vectors = jnp.stack([*split(gain), *split(bias)] + [jnp.zeros_like(gain, bf16)] * 4)
    left = jnp.concatenate([normed, vectors.T], axis=1).reshape(2, X_COUNT, part, 2 * SEQ + 8)
    right = grads.reshape(2, X_COUNT, part, 2 * SEQ)

    def own_head(pair):
        return jnp.where(far == 0, pair[0], pair[1]), jnp.where(far == 0, pair[1], pair[0])

    joined_parts, grad_parts = [0.0, 0.0], [0.0, 0.0]
    for step in (0, 3, 1, 2):
        place = (x + step) % X_COUNT
        left_part = lax.dynamic_index_in_dim(left, place, 1, keepdims=False)
        right_part = lax.dynamic_index_in_dim(right, place, 1, keepdims=False)
        left_part = left_part.reshape(2 * part, 2 * SEQ + 8)
        right_part = right_part.reshape(2 * part, 2 * SEQ)
        for h in range(2):
            weight = blocks[step][2 * h : 2 * h + 2].reshape(2 * part, 4 * E)
            joined_parts[h] += dot(left_part, weight[:, : 3 * E], ((0,), (0,)))
            grad_parts[h] += dot(right_part, weight[:, 3 * E :], ((0,), (0,)))
    parts = []
    for j, g in zip(joined_parts, grad_parts):
        v = j[2 * SEQ :]
        v = jnp.stack([v[0] + v[1], v[2] + v[3]])
        parts.append((jnp.concatenate([j[: 2 * SEQ], g], axis=1), jnp.pad(v, ((0, 6), (0, E)))))
    sent = jnp.stack([jnp.concatenate([p[SEQ:], v]) for p, v in parts])
    kept = jnp.stack([jnp.concatenate([p[:SEQ], v]) for p, v in parts])
    own, away = own_head(kept + swap_cores(sent))
    away_high, away_low = split(away[SEQ:])
    away = swap_far(jnp.concatenate([away[:SEQ].astype(bf16), away_high, away_low]))
    away = away.astype(f32)
    vector = own[SEQ:] + away[SEQ : SEQ + 8] + away[SEQ + 8 :]
    gain_weight, bias_weight = vector[0, : 3 * E], vector[1, : 3 * E]
    whole = own[:SEQ] + away[:SEQ]
    plain = whole[:, : 3 * E]
    joined = (plain + b_qkv).astype(bf16)
    context_grad = whole[:, 3 * E :].astype(bf16)

    slope = 2.0 ** (-8.0 * (rank + 1).astype(f32) / n_tensor)
    context, joined_grad = attention(joined, context_grad, slope)
    joined_grad_f = joined_grad.astype(f32)
    sums = jnp.stack(
        [
            jnp.sum(joined_grad_f * gain_weight, axis=1),
            jnp.sum(joined_grad_f * (plain - bias_weight), axis=1),
        ]
    )

    def pack(sums):
        high, low = split(sums)
        return jnp.concatenate([high, low, jnp.zeros((12, sums.shape[1]), bf16)])

    def unpack(rows):
        rows = rows.astype(f32)
        return rows[0:2] + rows[2:4]

    packed = jnp.pad(pack(sums), ((0, 0), (0, 3 * E)))
    result = jnp.concatenate([jnp.concatenate([context, joined_grad], axis=1), packed])
    result_far = swap_far(result)
    sums = sums + unpack(result_far[SEQ:, :SEQ])
    heads = by_far(result[:SEQ], result_far[:SEQ])
    packed = jnp.pad(pack(sums), ((0, 0), (0, 3 * E)))
    heads_sent = jnp.concatenate([heads, jnp.stack([packed, jnp.zeros_like(packed)])], axis=1)
    heads_other = swap_cores(heads_sent)
    sums = jnp.concatenate([sums, unpack(heads_other[0, SEQ:, :SEQ])], axis=1)
    heads = jnp.concatenate([heads, heads_other[:, :SEQ]], axis=1)

    joined_weight = in_order([b[:, :, : 3 * E] for b in blocks], x).reshape(2, quarter, 3 * E)
    weight_parts = [
        dot(grads, heads[h, :, :E], ((1,), (0,))).astype(bf16).reshape(2, X_COUNT, part, E)
        for h in range(2)
    ]

    def weight_to(step):
        place = (x + step) % X_COUNT
        return jnp.concatenate(
            [lax.dynamic_index_in_dim(w, place, 1, keepdims=False) for w in weight_parts]
        )

    across, heads = lax.optimization_barrier((weight_to(2), heads))

    group_part = sum(
        dot(joined_weight[h], heads[h, :, E:], ((1,), (1,))) for h in range(2)
    ).astype(bf16)
    extra = jnp.broadcast_to(pack(sums)[None], (Z_COUNT, 16, 2 * SEQ))
    payload = jnp.concatenate([group_part.reshape(Z_COUNT, part, 2 * SEQ), extra], axis=1)
    group_parts = lax.all_to_all(payload, "tensor", 0, 0, tiled=True, axis_index_groups=rings)
    total = jnp.sum(group_parts.astype(f32), axis=0)
    weight_parts = scatter_x(weight_to, across)
    grad_out_weight = scatter_y(weight_parts, y)
    sums = total[part : part + 2, :SEQ] + total[part + 2 : part + 4, :SEQ]
    total = total[:part]
    total_other = swap_cores(total[:, SEQ:])
    total = total[:, :SEQ]
    normed_grad = jnp.where(
        core == 0,
        jnp.concatenate([total, total_other]),
        jnp.concatenate([total_other, total]),
    )
    mean_grad = sums[0] / depth
    mean_cross = sums[1] / depth

    own_gain = lax.dynamic_slice_in_dim(norm_gain, rank * width, width)
    scaled_grad = normed_grad * own_gain[:, None]
    scaled = (hidden_t.astype(f32) - mean[:SEQ]) * inv_std[:SEQ]
    input_grad = inv_std[:SEQ] * (scaled_grad - mean_grad - scaled * mean_cross)

    return input_grad.astype(bf16).T, grad_out_weight.T


def solution(mesh):
    in_specs = (
        P("dp", "tensor"),
        P(),
        P(),
        P("dp", "tensor"),
        P("tensor"),
        P("tensor", "dp"),
        P("dp", "tensor"),
    )
    out_specs = (P("dp", "tensor"), P("tensor", "dp"))
    return jax.shard_map(body, mesh=mesh, in_specs=in_specs, out_specs=out_specs, check_vma=False)
```

```python
import jax
import jax.numpy as jnp
from jax import lax
from jax.sharding import PartitionSpec as P

SEQ = 128
E = 128
Z_COUNT = 8
X_COUNT = 4
norm_eps = 1e-05
f32 = jnp.float32
bf16 = jnp.bfloat16


def groups(count, key):
    found = {}
    for i in range(count):
        found.setdefault(key(i), []).append(i)
    return [found[k] for k in sorted(found)]


def swap_cores(x):
    n = lax.axis_size("dp")
    return lax.ppermute(x, "dp", [(i, i ^ 1) for i in range(n)])


def shift_z(x, step):
    n = lax.axis_size("tensor")
    pairs = [(i, i - i % Z_COUNT + (i + step) % Z_COUNT) for i in range(n)]
    return lax.ppermute(x, "tensor", pairs)


def swap_far(x):
    n = lax.axis_size("tensor")
    return lax.ppermute(x, "tensor", [(i, (i + Z_COUNT) % n) for i in range(n)])


def shift_x(x, step):
    n = lax.axis_size("dp")
    row = 2 * X_COUNT
    return lax.ppermute(x, "dp", [(i, i - i % row + (i + 2 * step) % row) for i in range(n)])


def along_y(x, target):
    n_dp, n_tensor = lax.axis_size("dp"), lax.axis_size("tensor")
    row = 2 * X_COUNT
    pairs = []
    for d in range(n_dp):
        for t in range(n_tensor):
            half, place = target(t // Z_COUNT, d // row)
            to = (place * row + d % row) * n_tensor + half * Z_COUNT + t % Z_COUNT
            pairs.append((d * n_tensor + t, to))
    return lax.ppermute(x, ("dp", "tensor"), pairs)


def move_weights(x):
    return along_y(x, lambda half, place: (place // 2, 2 * half + place % 2))


def gather_both(block, column, place):
    count = Z_COUNT
    middle, half = column.shape[0] // 2, block.shape[0] // 32 * 16
    x_up, x_down = shift_x(column, 1), shift_x(column, -1)
    found = {0: block}
    up = down = block
    for step in range(1, count // 2):
        up, down = shift_z(up, 1), shift_z(down, -1)
        found[step], found[count - step] = up, down
    x_up, x_down, up, down = lax.optimization_barrier((x_up, x_down, up, down))
    x_across = jnp.concatenate([shift_x(x_up[:middle], 1), shift_x(x_down[middle:], -1)])
    found[count // 2] = jnp.concatenate([shift_z(up[:half], 1), shift_z(down[half:], -1)])
    blocks = [found[count - 1 - j] for j in range(count)]
    rows = lax.dynamic_slice_in_dim(jnp.stack(blocks + blocks[:-1]), count - 1 - place, count, 0)
    return rows, [column, x_down, x_across, x_up]


def in_order(blocks, place):
    line = jnp.stack(blocks[1:] + blocks, axis=1)
    return lax.dynamic_slice_in_dim(line, X_COUNT - 1 - place, X_COUNT, 1)


def scatter_x(part, across):
    total = part(0).astype(f32) + shift_x(across, 2).astype(f32)
    return total + shift_x(part(1), 1).astype(f32) + shift_x(part(-1), -1).astype(f32)


def scatter_y(parts, place):
    count = parts.shape[0]
    sent = parts.astype(bf16)
    total = None
    for step in range(count):
        one = lax.dynamic_index_in_dim(sent, (place + step) % count, 0, keepdims=False)

        def target(half, place):
            part = (place + step) % count
            return part // 2, 2 * half + part % 2

        one = along_y(one, target).astype(f32)
        total = one if total is None else total + one
    return total


def split(x):
    high = lax.reduce_precision(x, 8, 7)
    return high.astype(bf16), lax.reduce_precision(x - high, 8, 7).astype(bf16)


def dot(a, b, dims):
    return lax.dot_general(a, b, (dims, ((), ())), preferred_element_type=f32)


def attention(joined, context_grad, slope):
    queries = joined[:, :E]
    key_rows = joined[:, E : 2 * E]
    values = joined[:, 2 * E :]
    scores = dot(queries, key_rows, ((1,), (1,))) * E ** (-0.5)
    row = lax.broadcasted_iota(jnp.int32, (SEQ, SEQ), 0)
    col = lax.broadcasted_iota(jnp.int32, (SEQ, SEQ), 1)
    offsets = (col - row).astype(f32)
    scores = jnp.where(offsets <= 0.0, scores + slope * offsets, -1e30)
    soft = jax.nn.softmax(scores, axis=-1)
    soft_round = soft.astype(bf16)
    context = dot(soft_round, values, ((1,), (0,))).astype(bf16)
    prob_grad = dot(context_grad, values, ((1,), (1,)))
    value_grad = dot(soft_round, context_grad, ((0,), (0,)))
    row_dot = jnp.sum(soft * prob_grad, axis=-1, keepdims=True)
    score_grad = (soft * (prob_grad - row_dot) * E ** (-0.5)).astype(bf16)
    query_grad = dot(score_grad, key_rows, ((1,), (0,)))
    key_grad = dot(score_grad, queries, ((0,), (0,)))
    joined_grad = jnp.concatenate([query_grad, key_grad, value_grad], axis=1).astype(bf16)
    return context, joined_grad


def body(hidden_in, norm_gain, norm_bias, w_qkv, b_qkv, w_out, out_grad):
    n_tensor = lax.axis_size("tensor")
    depth = norm_gain.shape[0]
    width = depth // n_tensor
    part = width // 2
    quarter = Z_COUNT * part
    rank = lax.axis_index("tensor")
    z, far = rank % Z_COUNT, rank // Z_COUNT
    dp = lax.axis_index("dp")
    core, x, y = dp % 2, dp // 2 % X_COUNT, dp // (2 * X_COUNT)
    lines = groups(lax.axis_size("dp"), lambda i: i % (2 * X_COUNT))
    rings = groups(n_tensor, lambda i: i // Z_COUNT)

    def by_far(own, other):
        return jnp.stack([jnp.where(far == 0, own, other), jnp.where(far == 0, other, own)])

    hidden_t = hidden_in.T
    acts = jnp.concatenate([hidden_t, out_grad.T], axis=1).reshape(2, part, 2 * SEQ)
    mine = jnp.where(core == 0, acts[0], acts[1])
    other = swap_cores(jnp.where(core == 0, acts[1], acts[0]))
    block = jnp.concatenate([mine[:, :SEQ], other[:, :SEQ], mine[:, SEQ:], other[:, SEQ:]], axis=1)

    weight_block = jnp.concatenate([w_qkv, w_out.T], axis=1)
    weight_block, hidden_t = lax.optimization_barrier((weight_block, hidden_t))
    weight_block = move_weights(weight_block)

    slice_f = hidden_t.astype(f32)
    mean_part = jnp.mean(slice_f, axis=0)
    stats = jnp.stack([mean_part, jnp.sum((slice_f - mean_part) ** 2, axis=0)])
    stats_far = swap_far(stats)
    gap = stats[0] - stats_far[0]
    stats = jnp.stack(
        [
            0.5 * (stats[0] + stats_far[0]),
            stats[1] + stats_far[1] + gap * gap * (width / 2),
        ]
    )
    stats = jnp.concatenate([stats, swap_cores(stats)], axis=1).reshape(1, 4 * SEQ)
    high, low = split(stats)
    lower = (stats - high.astype(f32) - low.astype(f32)).astype(bf16)
    block = jnp.concatenate([block, high, low, lower, jnp.zeros((13, 4 * SEQ), bf16)])

    weight_block, block = lax.optimization_barrier((weight_block, block))
    column = lax.all_gather(weight_block, "dp", axis=0, axis_index_groups=lines)
    rows, blocks = gather_both(block, column, z)
    hidden = rows[:, :part, : 2 * SEQ].reshape(quarter, 2 * SEQ).astype(f32)
    grads = rows[:, :part, 2 * SEQ :].reshape(quarter, 2 * SEQ)
    stats = jnp.sum(rows[:, part : part + 3].astype(f32), axis=1)
    mean = jnp.mean(stats[:, : 2 * SEQ], axis=0)
    gap = stats[:, : 2 * SEQ] - mean
    square = jnp.sum(stats[:, 2 * SEQ :], axis=0) + 2 * width * jnp.sum(gap * gap, axis=0)
    inv_std = lax.rsqrt(square / depth + norm_eps)

    def own_part(vector):
        vector = vector.reshape(2, Z_COUNT, 2, part)
        vector = jnp.where(far == 0, vector[0], vector[1])
        return jnp.where(core == 0, vector[:, 0], vector[:, 1]).reshape(quarter)

    gain, bias = own_part(norm_gain), own_part(norm_bias)
    normed = ((hidden - mean) * inv_std * gain[:, None] + bias[:, None]).astype(bf16)
    vectors = jnp.stack([*split(gain), *split(bias)] + [jnp.zeros_like(gain, bf16)] * 4)
    left = jnp.concatenate([normed, vectors.T], axis=1).reshape(2, X_COUNT, part, 2 * SEQ + 8)
    right = grads.reshape(2, X_COUNT, part, 2 * SEQ)

    def own_head(pair):
        return jnp.where(far == 0, pair[0], pair[1]), jnp.where(far == 0, pair[1], pair[0])

    joined_parts, grad_parts = [0.0, 0.0], [0.0, 0.0]
    for step in (0, 3, 1, 2):
        place = (x + step) % X_COUNT
        left_part = lax.dynamic_index_in_dim(left, place, 1, keepdims=False)
        right_part = lax.dynamic_index_in_dim(right, place, 1, keepdims=False)
        left_part = left_part.reshape(2 * part, 2 * SEQ + 8)
        right_part = right_part.reshape(2 * part, 2 * SEQ)
        for h in range(2):
            weight = blocks[step][2 * h : 2 * h + 2].reshape(2 * part, 4 * E)
            joined_parts[h] += dot(left_part, weight[:, : 3 * E], ((0,), (0,)))
            grad_parts[h] += dot(right_part, weight[:, 3 * E :], ((0,), (0,)))
    parts = []
    for j, g in zip(joined_parts, grad_parts):
        v = j[2 * SEQ :]
        v = jnp.stack([v[0] + v[1], v[2] + v[3]])
        parts.append((jnp.concatenate([j[: 2 * SEQ], g], axis=1), jnp.pad(v, ((0, 6), (0, E)))))
    sent = jnp.stack([jnp.concatenate([p[SEQ:], v]) for p, v in parts])
    kept = jnp.stack([jnp.concatenate([p[:SEQ], v]) for p, v in parts])
    own, away = own_head(kept + swap_cores(sent))
    away_high, away_low = split(away[SEQ:])
    away = swap_far(jnp.concatenate([away[:SEQ].astype(bf16), away_high, away_low]))
    away = away.astype(f32)
    vector = own[SEQ:] + away[SEQ : SEQ + 8] + away[SEQ + 8 :]
    gain_weight, bias_weight = vector[0, : 3 * E], vector[1, : 3 * E]
    whole = own[:SEQ] + away[:SEQ]
    plain = whole[:, : 3 * E]
    joined = (plain + b_qkv).astype(bf16)
    context_grad = whole[:, 3 * E :].astype(bf16)

    slope = 2.0 ** (-8.0 * (rank + 1).astype(f32) / n_tensor)
    context, joined_grad = attention(joined, context_grad, slope)
    joined_grad_f = joined_grad.astype(f32)
    sums = jnp.stack(
        [
            jnp.sum(joined_grad_f * gain_weight, axis=1),
            jnp.sum(joined_grad_f * (plain - bias_weight), axis=1),
        ]
    )

    def pack(sums):
        high, low = split(sums)
        return jnp.concatenate([high, low, jnp.zeros((12, sums.shape[1]), bf16)])

    def unpack(rows):
        rows = rows.astype(f32)
        return rows[0:2] + rows[2:4]

    packed = jnp.pad(pack(sums), ((0, 0), (0, 3 * E)))
    result = jnp.concatenate([jnp.concatenate([context, joined_grad], axis=1), packed])
    result_far = swap_far(result)
    sums = sums + unpack(result_far[SEQ:, :SEQ])
    heads = by_far(result[:SEQ], result_far[:SEQ])
    packed = jnp.pad(pack(sums), ((0, 0), (0, 3 * E)))
    heads_sent = jnp.concatenate([heads, jnp.stack([packed, jnp.zeros_like(packed)])], axis=1)
    heads_other = swap_cores(heads_sent)
    sums = jnp.concatenate([sums, unpack(heads_other[0, SEQ:, :SEQ])], axis=1)
    heads = jnp.concatenate([heads, heads_other[:, :SEQ]], axis=1)

    joined_weight = in_order([b[:, :, : 3 * E] for b in blocks], x).reshape(2, quarter, 3 * E)
    weight_parts = [
        dot(grads, heads[h, :, :E], ((1,), (0,))).astype(bf16).reshape(2, X_COUNT, part, E)
        for h in range(2)
    ]

    def weight_to(step):
        place = (x + step) % X_COUNT
        return jnp.concatenate(
            [lax.dynamic_index_in_dim(w, place, 1, keepdims=False) for w in weight_parts]
        )

    across, heads = lax.optimization_barrier((weight_to(2), heads))

    group_part = sum(
        dot(joined_weight[h], heads[h, :, E:], ((1,), (1,))) for h in range(2)
    ).astype(bf16)
    extra = jnp.broadcast_to(pack(sums)[None], (Z_COUNT, 16, 2 * SEQ))
    payload = jnp.concatenate([group_part.reshape(Z_COUNT, part, 2 * SEQ), extra], axis=1)
    group_parts = lax.all_to_all(payload, "tensor", 0, 0, tiled=True, axis_index_groups=rings)
    total = jnp.sum(group_parts.astype(f32), axis=0)
    weight_parts = scatter_x(weight_to, across)
    grad_out_weight = scatter_y(weight_parts, y)
    sums = total[part : part + 2, :SEQ] + total[part + 2 : part + 4, :SEQ]
    total = total[:part]
    total_other = swap_cores(total[:, SEQ:])
    total = total[:, :SEQ]
    normed_grad = jnp.where(
        core == 0,
        jnp.concatenate([total, total_other]),
        jnp.concatenate([total_other, total]),
    )
    mean_grad = sums[0] / depth
    mean_cross = sums[1] / depth

    own_gain = lax.dynamic_slice_in_dim(norm_gain, rank * width, width)
    scaled_grad = normed_grad * own_gain[:, None]
    scaled = (hidden_t.astype(f32) - mean[:SEQ]) * inv_std[:SEQ]
    input_grad = inv_std[:SEQ] * (scaled_grad - mean_grad - scaled * mean_cross)

    return input_grad.astype(bf16).T, grad_out_weight.T


def solution(mesh):
    in_specs = (
        P("dp", "tensor"),
        P(),
        P(),
        P("dp", "tensor"),
        P("tensor"),
        P("tensor", "dp"),
        P("dp", "tensor"),
    )
    out_specs = (P("dp", "tensor"), P("tensor", "dp"))
    return jax.shard_map(body, mesh=mesh, in_specs=in_specs, out_specs=out_specs, check_vma=False)
```

```python
import jax
import jax.numpy as jnp
from jax import lax
from jax.sharding import PartitionSpec as P

SEQ = 128
E = 128
Z_COUNT = 8
X_COUNT = 4
norm_eps = 1e-05
f32 = jnp.float32
bf16 = jnp.bfloat16


def groups(count, key):
    found = {}
    for i in range(count):
        found.setdefault(key(i), []).append(i)
    return [found[k] for k in sorted(found)]


def swap_cores(x):
    n = lax.axis_size("dp")
    return lax.ppermute(x, "dp", [(i, i ^ 1) for i in range(n)])


def shift_z(x, step):
    n = lax.axis_size("tensor")
    pairs = [(i, i - i % Z_COUNT + (i + step) % Z_COUNT) for i in range(n)]
    return lax.ppermute(x, "tensor", pairs)


def swap_far(x):
    n = lax.axis_size("tensor")
    return lax.ppermute(x, "tensor", [(i, (i + Z_COUNT) % n) for i in range(n)])


def shift_x(x, step):
    n = lax.axis_size("dp")
    row = 2 * X_COUNT
    return lax.ppermute(x, "dp", [(i, i - i % row + (i + 2 * step) % row) for i in range(n)])


def along_y(x, target):
    n_dp, n_tensor = lax.axis_size("dp"), lax.axis_size("tensor")
    row = 2 * X_COUNT
    pairs = []
    for d in range(n_dp):
        for t in range(n_tensor):
            half, place = target(t // Z_COUNT, d // row)
            to = (place * row + d % row) * n_tensor + half * Z_COUNT + t % Z_COUNT
            pairs.append((d * n_tensor + t, to))
    return lax.ppermute(x, ("dp", "tensor"), pairs)


def move_weights(x):
    return along_y(x, lambda half, place: (place // 2, 2 * half + place % 2))


def gather_both(block, column, place):
    count = Z_COUNT
    middle, half = column.shape[0] // 2, block.shape[0] // 32 * 16
    x_up, x_down = shift_x(column, 1), shift_x(column, -1)
    found = {0: block}
    up = down = block
    for step in range(1, count // 2):
        up, down = shift_z(up, 1), shift_z(down, -1)
        found[step], found[count - step] = up, down
    x_up, x_down, up, down = lax.optimization_barrier((x_up, x_down, up, down))
    x_across = jnp.concatenate([shift_x(x_up[:middle], 1), shift_x(x_down[middle:], -1)])
    found[count // 2] = jnp.concatenate([shift_z(up[:half], 1), shift_z(down[half:], -1)])
    blocks = [found[count - 1 - j] for j in range(count)]
    rows = lax.dynamic_slice_in_dim(jnp.stack(blocks + blocks[:-1]), count - 1 - place, count, 0)
    return rows, [column, x_down, x_across, x_up]


def in_order(blocks, place):
    line = jnp.stack(blocks[1:] + blocks, axis=1)
    return lax.dynamic_slice_in_dim(line, X_COUNT - 1 - place, X_COUNT, 1)


def scatter_x(part, across):
    total = part(0).astype(f32) + shift_x(across, 2).astype(f32)
    return total + shift_x(part(1), 1).astype(f32) + shift_x(part(-1), -1).astype(f32)


def scatter_y(parts, place):
    count = parts.shape[0]
    sent = parts.astype(bf16)
    total = None
    for step in range(count):
        one = lax.dynamic_index_in_dim(sent, (place + step) % count, 0, keepdims=False)

        def target(half, place):
            part = (place + step) % count
            return part // 2, 2 * half + part % 2

        one = along_y(one, target).astype(f32)
        total = one if total is None else total + one
    return total


def split(x):
    high = lax.reduce_precision(x, 8, 7)
    return high.astype(bf16), lax.reduce_precision(x - high, 8, 7).astype(bf16)


def dot(a, b, dims):
    return lax.dot_general(a, b, (dims, ((), ())), preferred_element_type=f32)


def attention(joined, context_grad, slope):
    queries = joined[:, :E]
    key_rows = joined[:, E : 2 * E]
    values = joined[:, 2 * E :]
    scores = dot(queries, key_rows, ((1,), (1,))) * E ** (-0.5)
    row = lax.broadcasted_iota(jnp.int32, (SEQ, SEQ), 0)
    col = lax.broadcasted_iota(jnp.int32, (SEQ, SEQ), 1)
    offsets = (col - row).astype(f32)
    scores = jnp.where(offsets <= 0.0, scores + slope * offsets, -1e30)
    soft = jax.nn.softmax(scores, axis=-1)
    soft_round = soft.astype(bf16)
    context = dot(soft_round, values, ((1,), (0,))).astype(bf16)
    prob_grad = dot(context_grad, values, ((1,), (1,)))
    value_grad = dot(soft_round, context_grad, ((0,), (0,)))
    row_dot = jnp.sum(soft * prob_grad, axis=-1, keepdims=True)
    score_grad = (soft * (prob_grad - row_dot) * E ** (-0.5)).astype(bf16)
    query_grad = dot(score_grad, key_rows, ((1,), (0,)))
    key_grad = dot(score_grad, queries, ((0,), (0,)))
    joined_grad = jnp.concatenate([query_grad, key_grad, value_grad], axis=1).astype(bf16)
    return context, joined_grad


def body(hidden_in, norm_gain, norm_bias, w_qkv, b_qkv, w_out, out_grad):
    n_tensor = lax.axis_size("tensor")
    depth = norm_gain.shape[0]
    width = depth // n_tensor
    part = width // 2
    quarter = Z_COUNT * part
    rank = lax.axis_index("tensor")
    z, far = rank % Z_COUNT, rank // Z_COUNT
    dp = lax.axis_index("dp")
    core, x, y = dp % 2, dp // 2 % X_COUNT, dp // (2 * X_COUNT)
    lines = groups(lax.axis_size("dp"), lambda i: i % (2 * X_COUNT))
    rings = groups(n_tensor, lambda i: i // Z_COUNT)

    def by_far(own, other):
        return jnp.stack([jnp.where(far == 0, own, other), jnp.where(far == 0, other, own)])

    weight_block = jnp.concatenate([w_qkv, w_out.T], axis=1)
    weight_block, hidden_t, grad_t = lax.optimization_barrier(
        (weight_block, hidden_in.T, out_grad.T)
    )
    weight_block = move_weights(weight_block)
    acts = jnp.concatenate([hidden_t, grad_t], axis=1).reshape(2, part, 2 * SEQ)
    mine = jnp.where(core == 0, acts[0], acts[1])
    other = swap_cores(jnp.where(core == 0, acts[1], acts[0]))
    block = jnp.concatenate([mine[:, :SEQ], other[:, :SEQ], mine[:, SEQ:], other[:, SEQ:]], axis=1)

    slice_f = hidden_t.astype(f32)
    mean_part = jnp.mean(slice_f, axis=0)
    stats = jnp.stack([mean_part, jnp.sum((slice_f - mean_part) ** 2, axis=0)])
    stats_far = swap_far(stats)
    gap = stats[0] - stats_far[0]
    stats = jnp.stack(
        [
            0.5 * (stats[0] + stats_far[0]),
            stats[1] + stats_far[1] + gap * gap * (width / 2),
        ]
    )
    weight_block, stats = lax.optimization_barrier((weight_block, stats))
    stats = jnp.concatenate([stats, swap_cores(stats)], axis=1).reshape(1, 4 * SEQ)
    high, low = split(stats)
    lower = (stats - high.astype(f32) - low.astype(f32)).astype(bf16)
    block = jnp.concatenate([block, high, low, lower, jnp.zeros((13, 4 * SEQ), bf16)])

    weight_block, block = lax.optimization_barrier((weight_block, block))
    column = lax.all_gather(weight_block, "dp", axis=0, axis_index_groups=lines)
    column, block = lax.optimization_barrier((column, block))
    rows, blocks = gather_both(block, column, z)
    hidden = rows[:, :part, : 2 * SEQ].reshape(quarter, 2 * SEQ).astype(f32)
    grads = rows[:, :part, 2 * SEQ :].reshape(quarter, 2 * SEQ)
    stats = jnp.sum(rows[:, part : part + 3].astype(f32), axis=1)
    mean = jnp.mean(stats[:, : 2 * SEQ], axis=0)
    gap = stats[:, : 2 * SEQ] - mean
    square = jnp.sum(stats[:, 2 * SEQ :], axis=0) + 2 * width * jnp.sum(gap * gap, axis=0)
    inv_std = lax.rsqrt(square / depth + norm_eps)

    def own_part(vector):
        vector = vector.reshape(2, Z_COUNT, 2, part)
        vector = jnp.where(far == 0, vector[0], vector[1])
        return jnp.where(core == 0, vector[:, 0], vector[:, 1]).reshape(quarter)

    gain, bias = own_part(norm_gain), own_part(norm_bias)
    normed = ((hidden - mean) * inv_std * gain[:, None] + bias[:, None]).astype(bf16)
    vectors = jnp.stack([*split(gain), *split(bias)] + [jnp.zeros_like(gain, bf16)] * 4)
    left = jnp.concatenate([normed, vectors.T], axis=1).reshape(2, X_COUNT, part, 2 * SEQ + 8)
    right = grads.reshape(2, X_COUNT, part, 2 * SEQ)

    def own_head(pair):
        return jnp.where(far == 0, pair[0], pair[1]), jnp.where(far == 0, pair[1], pair[0])

    joined_parts, grad_parts = [0.0, 0.0], [0.0, 0.0]
    for step in (0, 3, 1, 2):
        place = (x + step) % X_COUNT
        left_part = lax.dynamic_index_in_dim(left, place, 1, keepdims=False)
        right_part = lax.dynamic_index_in_dim(right, place, 1, keepdims=False)
        left_part = left_part.reshape(2 * part, 2 * SEQ + 8)
        right_part = right_part.reshape(2 * part, 2 * SEQ)
        for h in range(2):
            weight = blocks[step][2 * h : 2 * h + 2].reshape(2 * part, 4 * E)
            joined_parts[h] += dot(left_part, weight[:, : 3 * E], ((0,), (0,)))
            grad_parts[h] += dot(right_part, weight[:, 3 * E :], ((0,), (0,)))
    parts = []
    for j, g in zip(joined_parts, grad_parts):
        v = j[2 * SEQ :]
        v = jnp.stack([v[0] + v[1], v[2] + v[3]])
        parts.append((jnp.concatenate([j[: 2 * SEQ], g], axis=1), jnp.pad(v, ((0, 6), (0, E)))))
    sent = jnp.stack([jnp.concatenate([p[SEQ:], v]) for p, v in parts])
    kept = jnp.stack([jnp.concatenate([p[:SEQ], v]) for p, v in parts])
    own, away = own_head(kept + swap_cores(sent))
    away_high, away_low = split(away[SEQ:])
    away = swap_far(jnp.concatenate([away[:SEQ].astype(bf16), away_high, away_low]))
    away = away.astype(f32)
    vector = own[SEQ:] + away[SEQ : SEQ + 8] + away[SEQ + 8 :]
    gain_weight, bias_weight = vector[0, : 3 * E], vector[1, : 3 * E]
    whole = own[:SEQ] + away[:SEQ]
    plain = whole[:, : 3 * E]
    joined = (plain + b_qkv).astype(bf16)
    context_grad = whole[:, 3 * E :].astype(bf16)

    slope = 2.0 ** (-8.0 * (rank + 1).astype(f32) / n_tensor)
    context, joined_grad = attention(joined, context_grad, slope)
    joined_grad_f = joined_grad.astype(f32)
    sums = jnp.stack(
        [
            jnp.sum(joined_grad_f * gain_weight, axis=1),
            jnp.sum(joined_grad_f * (plain - bias_weight), axis=1),
        ]
    )

    def pack(sums):
        high, low = split(sums)
        return jnp.concatenate([high, low, jnp.zeros((12, sums.shape[1]), bf16)])

    def unpack(rows):
        rows = rows.astype(f32)
        return rows[0:2] + rows[2:4]

    packed = jnp.pad(pack(sums), ((0, 0), (0, 3 * E)))
    result = jnp.concatenate([jnp.concatenate([context, joined_grad], axis=1), packed])
    result_far = swap_far(result)
    sums = sums + unpack(result_far[SEQ:, :SEQ])
    heads = by_far(result[:SEQ], result_far[:SEQ])
    packed = jnp.pad(pack(sums), ((0, 0), (0, 3 * E)))
    heads_sent = jnp.concatenate([heads, jnp.stack([packed, jnp.zeros_like(packed)])], axis=1)
    heads_other = swap_cores(heads_sent)
    sums = jnp.concatenate([sums, unpack(heads_other[0, SEQ:, :SEQ])], axis=1)
    heads = jnp.concatenate([heads, heads_other[:, :SEQ]], axis=1)

    joined_weight = in_order([b[:, :, : 3 * E] for b in blocks], x).reshape(2, quarter, 3 * E)
    weight_parts = [
        dot(grads, heads[h, :, :E], ((1,), (0,))).astype(bf16).reshape(2, X_COUNT, part, E)
        for h in range(2)
    ]

    def weight_to(step):
        place = (x + step) % X_COUNT
        return jnp.concatenate(
            [lax.dynamic_index_in_dim(w, place, 1, keepdims=False) for w in weight_parts]
        )

    across, heads = lax.optimization_barrier((weight_to(2), heads))

    group_part = sum(
        dot(joined_weight[h], heads[h, :, E:], ((1,), (1,))) for h in range(2)
    ).astype(bf16)
    extra = jnp.broadcast_to(pack(sums)[None], (Z_COUNT, 16, 2 * SEQ))
    payload = jnp.concatenate([group_part.reshape(Z_COUNT, part, 2 * SEQ), extra], axis=1)
    group_parts = lax.all_to_all(payload, "tensor", 0, 0, tiled=True, axis_index_groups=rings)
    total = jnp.sum(group_parts.astype(f32), axis=0)
    weight_parts = scatter_x(weight_to, across)
    grad_out_weight = scatter_y(weight_parts, y)
    sums = total[part : part + 2, :SEQ] + total[part + 2 : part + 4, :SEQ]
    total = total[:part]
    total_other = swap_cores(total[:, SEQ:])
    total = total[:, :SEQ]
    normed_grad = jnp.where(
        core == 0,
        jnp.concatenate([total, total_other]),
        jnp.concatenate([total_other, total]),
    )
    mean_grad = sums[0] / depth
    mean_cross = sums[1] / depth

    own_gain = lax.dynamic_slice_in_dim(norm_gain, rank * width, width)
    scaled_grad = normed_grad * own_gain[:, None]
    scaled = (hidden_t.astype(f32) - mean[:SEQ]) * inv_std[:SEQ]
    input_grad = inv_std[:SEQ] * (scaled_grad - mean_grad - scaled * mean_cross)

    return input_grad.astype(bf16).T, grad_out_weight.T


def solution(mesh):
    in_specs = (
        P("dp", "tensor"),
        P(),
        P(),
        P("dp", "tensor"),
        P("tensor"),
        P("tensor", "dp"),
        P("dp", "tensor"),
    )
    out_specs = (P("dp", "tensor"), P("tensor", "dp"))
    return jax.shard_map(body, mesh=mesh, in_specs=in_specs, out_specs=out_specs, check_vma=False)
```

```python
import jax
import jax.numpy as jnp
from jax import lax
from jax.sharding import PartitionSpec as P

SEQ = 128
E = 128
Z_COUNT = 8
X_COUNT = 4
norm_eps = 1e-05
f32 = jnp.float32
bf16 = jnp.bfloat16


def groups(count, key):
    found = {}
    for i in range(count):
        found.setdefault(key(i), []).append(i)
    return [found[k] for k in sorted(found)]


def swap_cores(x):
    n = lax.axis_size("dp")
    return lax.ppermute(x, "dp", [(i, i ^ 1) for i in range(n)])


def shift_z(x, step):
    n = lax.axis_size("tensor")
    pairs = [(i, i - i % Z_COUNT + (i + step) % Z_COUNT) for i in range(n)]
    return lax.ppermute(x, "tensor", pairs)


def swap_z(x, bit):
    n = lax.axis_size("tensor")
    return lax.ppermute(x, "tensor", [(i, i ^ bit) for i in range(n)])


def swap_far(x):
    n = lax.axis_size("tensor")
    return lax.ppermute(x, "tensor", [(i, (i + Z_COUNT) % n) for i in range(n)])


def shift_x(x, step):
    n = lax.axis_size("dp")
    row = 2 * X_COUNT
    return lax.ppermute(x, "dp", [(i, i - i % row + (i + 2 * step) % row) for i in range(n)])


def along_y(x, target):
    n_dp, n_tensor = lax.axis_size("dp"), lax.axis_size("tensor")
    row = 2 * X_COUNT
    pairs = []
    for d in range(n_dp):
        for t in range(n_tensor):
            half, place = target(t // Z_COUNT, d // row)
            to = (place * row + d % row) * n_tensor + half * Z_COUNT + t % Z_COUNT
            pairs.append((d * n_tensor + t, to))
    return lax.ppermute(x, ("dp", "tensor"), pairs)


def move_weights(x):
    return along_y(x, lambda half, place: (place // 2, 2 * half + place % 2))


def x_gather(own, place, early):
    middle = own.shape[0] // 2
    up, down = shift_x(own, 1), shift_x(own, -1)
    up, down, early = lax.optimization_barrier((up, down, early))
    across = jnp.concatenate([shift_x(up[:middle], 1), shift_x(down[middle:], -1)])
    return [own, down, across, up], early


def in_order(blocks, place):
    line = jnp.stack(blocks[1:] + blocks, axis=1)
    return lax.dynamic_slice_in_dim(line, X_COUNT - 1 - place, X_COUNT, 1)


def scatter_x(part, across):
    total = part(0).astype(f32) + shift_x(across, 2).astype(f32)
    return total + shift_x(part(1), 1).astype(f32) + shift_x(part(-1), -1).astype(f32)


def scatter_y(parts, place):
    count = parts.shape[0]
    sent = parts.astype(bf16)
    total = None
    for step in range(count):
        one = lax.dynamic_index_in_dim(sent, (place + step) % count, 0, keepdims=False)

        def target(half, place):
            part = (place + step) % count
            return part // 2, 2 * half + part % 2

        one = along_y(one, target).astype(f32)
        total = one if total is None else total + one
    return total


def split(x):
    high = lax.reduce_precision(x, 8, 7)
    return high.astype(bf16), lax.reduce_precision(x - high, 8, 7).astype(bf16)


def dot(a, b, dims):
    return lax.dot_general(a, b, (dims, ((), ())), preferred_element_type=f32)


def attention(joined, context_grad, slope):
    queries = joined[:, :E]
    key_rows = joined[:, E : 2 * E]
    values = joined[:, 2 * E :]
    scores = dot(queries, key_rows, ((1,), (1,))) * E ** (-0.5)
    row = lax.broadcasted_iota(jnp.int32, (SEQ, SEQ), 0)
    col = lax.broadcasted_iota(jnp.int32, (SEQ, SEQ), 1)
    offsets = (col - row).astype(f32)
    scores = jnp.where(offsets <= 0.0, scores + slope * offsets, -1e30)
    soft = jax.nn.softmax(scores, axis=-1)
    soft_round = soft.astype(bf16)
    context = dot(soft_round, values, ((1,), (0,))).astype(bf16)
    prob_grad = dot(context_grad, values, ((1,), (1,)))
    value_grad = dot(soft_round, context_grad, ((0,), (0,)))
    row_dot = jnp.sum(soft * prob_grad, axis=-1, keepdims=True)
    score_grad = (soft * (prob_grad - row_dot) * E ** (-0.5)).astype(bf16)
    query_grad = dot(score_grad, key_rows, ((1,), (0,)))
    key_grad = dot(score_grad, queries, ((0,), (0,)))
    joined_grad = jnp.concatenate([query_grad, key_grad, value_grad], axis=1).astype(bf16)
    return context, joined_grad


def body(hidden_in, norm_gain, norm_bias, w_qkv, b_qkv, w_out, out_grad):
    n_tensor = lax.axis_size("tensor")
    depth = norm_gain.shape[0]
    width = depth // n_tensor
    part = width // 2
    quarter = Z_COUNT * part
    rank = lax.axis_index("tensor")
    z, far = rank % Z_COUNT, rank // Z_COUNT
    dp = lax.axis_index("dp")
    core, x, y = dp % 2, dp // 2 % X_COUNT, dp // (2 * X_COUNT)
    lines = groups(lax.axis_size("dp"), lambda i: i % (2 * X_COUNT))
    rings = groups(n_tensor, lambda i: i // Z_COUNT)

    def by_far(own, other):
        return jnp.stack([jnp.where(far == 0, own, other), jnp.where(far == 0, other, own)])

    hidden_t = hidden_in.T
    acts = jnp.concatenate([hidden_t, out_grad.T], axis=1).reshape(2, part, 2 * SEQ)
    mine = jnp.where(core == 0, acts[0], acts[1])
    other = swap_cores(jnp.where(core == 0, acts[1], acts[0]))
    block = jnp.concatenate([mine[:, :SEQ], other[:, :SEQ], mine[:, SEQ:], other[:, SEQ:]], axis=1)

    weight_block = move_weights(jnp.concatenate([w_qkv, w_out.T], axis=1))

    rows = lax.all_gather(block, "tensor", axis=0, tiled=True, axis_index_groups=rings)
    weight_block, _ = lax.optimization_barrier((weight_block, block))
    column = lax.all_gather(weight_block, "dp", axis=0, axis_index_groups=lines)

    def merge(stats, stats_other, count):
        gap = stats[0] - stats_other[0]
        return jnp.stack(
            [
                0.5 * (stats[0] + stats_other[0]),
                stats[1] + stats_other[1] + gap * gap * (count / 2),
            ]
        )

    _, slice_f = lax.optimization_barrier((block, hidden_t.astype(f32)))
    mean_part = jnp.mean(slice_f, axis=0)
    stats = jnp.stack([mean_part, jnp.sum((slice_f - mean_part) ** 2, axis=0)])
    stats = merge(stats, swap_far(stats), width)
    _, stats = lax.optimization_barrier((column, stats))
    for bit in (1, 2, 4):
        stats = merge(stats, swap_z(stats, bit), 2 * width * bit)
    stats = jnp.stack([stats[0], lax.rsqrt(stats[1] / depth + norm_eps)])
    stats = jnp.concatenate([stats, swap_cores(stats)], axis=1)

    blocks, (rows, stats) = x_gather(column, x, (rows, stats))
    mean, inv_std = stats
    hidden = rows[:, : 2 * SEQ].astype(f32)
    grads = rows[:, 2 * SEQ :]

    def own_part(vector):
        vector = vector.reshape(2, Z_COUNT, 2, part)
        vector = jnp.where(far == 0, vector[0], vector[1])
        return jnp.where(core == 0, vector[:, 0], vector[:, 1]).reshape(quarter)

    gain, bias = own_part(norm_gain), own_part(norm_bias)
    normed = ((hidden - mean) * inv_std * gain[:, None] + bias[:, None]).astype(bf16)
    vectors = jnp.stack([*split(gain), *split(bias)] + [jnp.zeros_like(gain, bf16)] * 4)
    left = jnp.concatenate([normed, vectors.T], axis=1).reshape(2, X_COUNT, part, 2 * SEQ + 8)
    right = grads.reshape(2, X_COUNT, part, 2 * SEQ)

    def own_head(pair):
        return jnp.where(far == 0, pair[0], pair[1]), jnp.where(far == 0, pair[1], pair[0])

    joined_parts, grad_parts = [0.0, 0.0], [0.0, 0.0]
    for step in (0, 3, 1, 2):
        place = (x + step) % X_COUNT
        left_part = lax.dynamic_index_in_dim(left, place, 1, keepdims=False)
        right_part = lax.dynamic_index_in_dim(right, place, 1, keepdims=False)
        left_part = left_part.reshape(2 * part, 2 * SEQ + 8)
        right_part = right_part.reshape(2 * part, 2 * SEQ)
        for h in range(2):
            weight = blocks[step][2 * h : 2 * h + 2].reshape(2 * part, 4 * E)
            joined_parts[h] += dot(left_part, weight[:, : 3 * E], ((0,), (0,)))
            grad_parts[h] += dot(right_part, weight[:, 3 * E :], ((0,), (0,)))
    parts = []
    for j, g in zip(joined_parts, grad_parts):
        v = j[2 * SEQ :]
        v = jnp.stack([v[0] + v[1], v[2] + v[3]])
        parts.append((jnp.concatenate([j[: 2 * SEQ], g], axis=1), jnp.pad(v, ((0, 6), (0, E)))))
    sent = jnp.stack([jnp.concatenate([p[SEQ:], v]) for p, v in parts])
    kept = jnp.stack([jnp.concatenate([p[:SEQ], v]) for p, v in parts])
    own, away = own_head(kept + swap_cores(sent))
    away_high, away_low = split(away[SEQ:])
    away = swap_far(jnp.concatenate([away[:SEQ].astype(bf16), away_high, away_low]))
    away = away.astype(f32)
    vector = own[SEQ:] + away[SEQ : SEQ + 8] + away[SEQ + 8 :]
    gain_weight, bias_weight = vector[0, : 3 * E], vector[1, : 3 * E]
    whole = own[:SEQ] + away[:SEQ]
    plain = whole[:, : 3 * E]
    joined = (plain + b_qkv).astype(bf16)
    context_grad = whole[:, 3 * E :].astype(bf16)

    slope = 2.0 ** (-8.0 * (rank + 1).astype(f32) / n_tensor)
    context, joined_grad = attention(joined, context_grad, slope)
    joined_grad_f = joined_grad.astype(f32)
    sums = jnp.stack(
        [
            jnp.sum(joined_grad_f * gain_weight, axis=1),
            jnp.sum(joined_grad_f * (plain - bias_weight), axis=1),
        ]
    )

    def pack(sums):
        high, low = split(sums)
        return jnp.concatenate([high, low, jnp.zeros((12, sums.shape[1]), bf16)])

    def unpack(rows):
        rows = rows.astype(f32)
        return rows[0:2] + rows[2:4]

    packed = jnp.pad(pack(sums), ((0, 0), (0, 3 * E)))
    result = jnp.concatenate([jnp.concatenate([context, joined_grad], axis=1), packed])
    result_far = swap_far(result)
    sums = sums + unpack(result_far[SEQ:, :SEQ])
    heads = by_far(result[:SEQ], result_far[:SEQ])
    packed = jnp.pad(pack(sums), ((0, 0), (0, 3 * E)))
    heads_sent = jnp.concatenate([heads, jnp.stack([packed, jnp.zeros_like(packed)])], axis=1)
    heads_other = swap_cores(heads_sent)
    sums = jnp.concatenate([sums, unpack(heads_other[0, SEQ:, :SEQ])], axis=1)
    heads = jnp.concatenate([heads, heads_other[:, :SEQ]], axis=1)

    joined_weight = in_order([b[:, :, : 3 * E] for b in blocks], x).reshape(2, quarter, 3 * E)
    weight_parts = [
        dot(grads, heads[h, :, :E], ((1,), (0,))).astype(bf16).reshape(2, X_COUNT, part, E)
        for h in range(2)
    ]

    def weight_to(step):
        place = (x + step) % X_COUNT
        return jnp.concatenate(
            [lax.dynamic_index_in_dim(w, place, 1, keepdims=False) for w in weight_parts]
        )

    across, heads = lax.optimization_barrier((weight_to(2), heads))

    group_part = sum(
        dot(joined_weight[h], heads[h, :, E:], ((1,), (1,))) for h in range(2)
    ).astype(bf16)
    extra = jnp.broadcast_to(pack(sums)[None], (Z_COUNT, 16, 2 * SEQ))
    payload = jnp.concatenate([group_part.reshape(Z_COUNT, part, 2 * SEQ), extra], axis=1)
    group_parts = lax.all_to_all(payload, "tensor", 0, 0, tiled=True, axis_index_groups=rings)
    total = jnp.sum(group_parts.astype(f32), axis=0)
    weight_parts = scatter_x(weight_to, across)
    grad_out_weight = scatter_y(weight_parts, y)
    sums = total[part : part + 2, :SEQ] + total[part + 2 : part + 4, :SEQ]
    total = total[:part]
    total_other = swap_cores(total[:, SEQ:])
    total = total[:, :SEQ]
    normed_grad = jnp.where(
        core == 0,
        jnp.concatenate([total, total_other]),
        jnp.concatenate([total_other, total]),
    )
    mean_grad = sums[0] / depth
    mean_cross = sums[1] / depth

    own_gain = lax.dynamic_slice_in_dim(norm_gain, rank * width, width)
    scaled_grad = normed_grad * own_gain[:, None]
    scaled = (hidden_t.astype(f32) - mean[:SEQ]) * inv_std[:SEQ]
    input_grad = inv_std[:SEQ] * (scaled_grad - mean_grad - scaled * mean_cross)

    return input_grad.astype(bf16).T, grad_out_weight.T


def solution(mesh):
    in_specs = (
        P("dp", "tensor"),
        P(),
        P(),
        P("dp", "tensor"),
        P("tensor"),
        P("tensor", "dp"),
        P("dp", "tensor"),
    )
    out_specs = (P("dp", "tensor"), P("tensor", "dp"))
    return jax.shard_map(body, mesh=mesh, in_specs=in_specs, out_specs=out_specs, check_vma=False)
```

```python
import jax
import jax.numpy as jnp
from jax import lax
from jax.sharding import PartitionSpec as P

SEQ = 128
E = 128
Z_COUNT = 8
X_COUNT = 4
norm_eps = 1e-05
f32 = jnp.float32
bf16 = jnp.bfloat16


def groups(count, key):
    found = {}
    for i in range(count):
        found.setdefault(key(i), []).append(i)
    return [found[k] for k in sorted(found)]


def swap_cores(x):
    n = lax.axis_size("dp")
    return lax.ppermute(x, "dp", [(i, i ^ 1) for i in range(n)])


def shift_z(x, step):
    n = lax.axis_size("tensor")
    pairs = [(i, i - i % Z_COUNT + (i + step) % Z_COUNT) for i in range(n)]
    return lax.ppermute(x, "tensor", pairs)


def swap_far(x):
    n = lax.axis_size("tensor")
    return lax.ppermute(x, "tensor", [(i, (i + Z_COUNT) % n) for i in range(n)])


def shift_x(x, step):
    n = lax.axis_size("dp")
    row = 2 * X_COUNT
    return lax.ppermute(x, "dp", [(i, i - i % row + (i + 2 * step) % row) for i in range(n)])


def along_y(x, target):
    n_dp, n_tensor = lax.axis_size("dp"), lax.axis_size("tensor")
    row = 2 * X_COUNT
    pairs = []
    for d in range(n_dp):
        for t in range(n_tensor):
            half, place = target(t // Z_COUNT, d // row)
            to = (place * row + d % row) * n_tensor + half * Z_COUNT + t % Z_COUNT
            pairs.append((d * n_tensor + t, to))
    return lax.ppermute(x, ("dp", "tensor"), pairs)


def move_weights(x):
    return along_y(x, lambda half, place: (place // 2, 2 * half + place % 2))


def x_gather(own, place, early):
    middle = own.shape[0] // 2
    up, down = shift_x(own, 1), shift_x(own, -1)
    up, down, early = lax.optimization_barrier((up, down, early))
    across = jnp.concatenate([shift_x(up[:middle], 1), shift_x(down[middle:], -1)])
    return [own, down, across, up], early


def in_order(blocks, place):
    line = jnp.stack(blocks[1:] + blocks, axis=1)
    return lax.dynamic_slice_in_dim(line, X_COUNT - 1 - place, X_COUNT, 1)


def scatter_x(part, across):
    total = part(0).astype(f32) + shift_x(across, 2).astype(f32)
    return total + shift_x(part(1), 1).astype(f32) + shift_x(part(-1), -1).astype(f32)


def scatter_y(parts, place):
    count = parts.shape[0]
    sent = parts.astype(bf16)
    total = None
    for step in range(count):
        one = lax.dynamic_index_in_dim(sent, (place + step) % count, 0, keepdims=False)

        def target(half, place):
            part = (place + step) % count
            return part // 2, 2 * half + part % 2

        one = along_y(one, target).astype(f32)
        total = one if total is None else total + one
    return total


def split(x):
    high = lax.reduce_precision(x, 8, 7)
    return high.astype(bf16), lax.reduce_precision(x - high, 8, 7).astype(bf16)


def dot(a, b, dims):
    return lax.dot_general(a, b, (dims, ((), ())), preferred_element_type=f32)


def attention(joined, context_grad, slope):
    queries = joined[:, :E]
    key_rows = joined[:, E : 2 * E]
    values = joined[:, 2 * E :]
    scores = dot(queries, key_rows, ((1,), (1,))) * E ** (-0.5)
    row = lax.broadcasted_iota(jnp.int32, (SEQ, SEQ), 0)
    col = lax.broadcasted_iota(jnp.int32, (SEQ, SEQ), 1)
    offsets = (col - row).astype(f32)
    scores = jnp.where(offsets <= 0.0, scores + slope * offsets, -1e30)
    soft = jax.nn.softmax(scores, axis=-1)
    soft_round = soft.astype(bf16)
    context = dot(soft_round, values, ((1,), (0,))).astype(bf16)
    prob_grad = dot(context_grad, values, ((1,), (1,)))
    value_grad = dot(soft_round, context_grad, ((0,), (0,)))
    row_dot = jnp.sum(soft * prob_grad, axis=-1, keepdims=True)
    score_grad = (soft * (prob_grad - row_dot) * E ** (-0.5)).astype(bf16)
    query_grad = dot(score_grad, key_rows, ((1,), (0,)))
    key_grad = dot(score_grad, queries, ((0,), (0,)))
    joined_grad = jnp.concatenate([query_grad, key_grad, value_grad], axis=1).astype(bf16)
    return context, joined_grad


def body(hidden_in, norm_gain, norm_bias, w_qkv, b_qkv, w_out, out_grad):
    n_tensor = lax.axis_size("tensor")
    depth = norm_gain.shape[0]
    width = depth // n_tensor
    part = width // 2
    quarter = Z_COUNT * part
    rank = lax.axis_index("tensor")
    z, far = rank % Z_COUNT, rank // Z_COUNT
    dp = lax.axis_index("dp")
    core, x, y = dp % 2, dp // 2 % X_COUNT, dp // (2 * X_COUNT)
    lines = groups(lax.axis_size("dp"), lambda i: i % (2 * X_COUNT))
    rings = groups(n_tensor, lambda i: i // Z_COUNT)

    def by_far(own, other):
        return jnp.stack([jnp.where(far == 0, own, other), jnp.where(far == 0, other, own)])

    hidden_t = hidden_in.T
    acts = jnp.concatenate([hidden_t, out_grad.T], axis=1).reshape(2, part, 2 * SEQ)
    mine = jnp.where(core == 0, acts[0], acts[1])
    other = swap_cores(jnp.where(core == 0, acts[1], acts[0]))
    block = jnp.concatenate([mine[:, :SEQ], other[:, :SEQ], mine[:, SEQ:], other[:, SEQ:]], axis=1)

    weight_block = move_weights(jnp.concatenate([w_qkv, w_out.T], axis=1))

    rows = lax.all_gather(block, "tensor", axis=0, tiled=True, axis_index_groups=rings)
    weight_block, _ = lax.optimization_barrier((weight_block, block))
    column = lax.all_gather(weight_block, "dp", axis=0, axis_index_groups=lines)

    def merge(stats, stats_other, count):
        gap = stats[0] - stats_other[0]
        return jnp.stack(
            [
                0.5 * (stats[0] + stats_other[0]),
                stats[1] + stats_other[1] + gap * gap * (count / 2),
            ]
        )

    hidden = rows[:, : 2 * SEQ].astype(f32)
    mean_part = jnp.sum(hidden, axis=0) / quarter
    stats = jnp.stack([mean_part, jnp.sum((hidden - mean_part) ** 2, axis=0)])
    stats = merge(stats, swap_far(stats), quarter)
    stats_other = swap_cores(stats)
    stats_other = jnp.concatenate([stats_other[:, SEQ:], stats_other[:, :SEQ]], axis=1)
    mean, square = merge(stats, stats_other, 2 * quarter)
    inv_std = lax.rsqrt(square / depth + norm_eps)

    blocks, (rows, mean, inv_std) = x_gather(column, x, (rows, mean, inv_std))
    hidden = rows[:, : 2 * SEQ].astype(f32)
    grads = rows[:, 2 * SEQ :]

    def own_part(vector):
        vector = vector.reshape(2, Z_COUNT, 2, part)
        vector = jnp.where(far == 0, vector[0], vector[1])
        return jnp.where(core == 0, vector[:, 0], vector[:, 1]).reshape(quarter)

    gain, bias = own_part(norm_gain), own_part(norm_bias)
    normed = ((hidden - mean) * inv_std * gain[:, None] + bias[:, None]).astype(bf16)
    vectors = jnp.stack([*split(gain), *split(bias)] + [jnp.zeros_like(gain, bf16)] * 4)
    left = jnp.concatenate([normed, vectors.T], axis=1).reshape(2, X_COUNT, part, 2 * SEQ + 8)
    right = grads.reshape(2, X_COUNT, part, 2 * SEQ)

    def own_head(pair):
        return jnp.where(far == 0, pair[0], pair[1]), jnp.where(far == 0, pair[1], pair[0])

    joined_parts, grad_parts = [0.0, 0.0], [0.0, 0.0]
    for step in (0, 3, 1, 2):
        place = (x + step) % X_COUNT
        left_part = lax.dynamic_index_in_dim(left, place, 1, keepdims=False)
        right_part = lax.dynamic_index_in_dim(right, place, 1, keepdims=False)
        left_part = left_part.reshape(2 * part, 2 * SEQ + 8)
        right_part = right_part.reshape(2 * part, 2 * SEQ)
        for h in range(2):
            weight = blocks[step][2 * h : 2 * h + 2].reshape(2 * part, 4 * E)
            joined_parts[h] += dot(left_part, weight[:, : 3 * E], ((0,), (0,)))
            grad_parts[h] += dot(right_part, weight[:, 3 * E :], ((0,), (0,)))
    parts = []
    for j, g in zip(joined_parts, grad_parts):
        v = j[2 * SEQ :]
        v = jnp.stack([v[0] + v[1], v[2] + v[3]])
        parts.append((jnp.concatenate([j[: 2 * SEQ], g], axis=1), jnp.pad(v, ((0, 6), (0, E)))))
    sent = jnp.stack([jnp.concatenate([p[SEQ:], v]) for p, v in parts])
    kept = jnp.stack([jnp.concatenate([p[:SEQ], v]) for p, v in parts])
    own, away = own_head(kept + swap_cores(sent))
    away_high, away_low = split(away[SEQ:])
    away = swap_far(jnp.concatenate([away[:SEQ].astype(bf16), away_high, away_low]))
    away = away.astype(f32)
    vector = own[SEQ:] + away[SEQ : SEQ + 8] + away[SEQ + 8 :]
    gain_weight, bias_weight = vector[0, : 3 * E], vector[1, : 3 * E]
    whole = own[:SEQ] + away[:SEQ]
    plain = whole[:, : 3 * E]
    joined = (plain + b_qkv).astype(bf16)
    context_grad = whole[:, 3 * E :].astype(bf16)

    slope = 2.0 ** (-8.0 * (rank + 1).astype(f32) / n_tensor)
    context, joined_grad = attention(joined, context_grad, slope)
    joined_grad_f = joined_grad.astype(f32)
    sums = jnp.stack(
        [
            jnp.sum(joined_grad_f * gain_weight, axis=1),
            jnp.sum(joined_grad_f * (plain - bias_weight), axis=1),
        ]
    )

    def pack(sums):
        high, low = split(sums)
        return jnp.concatenate([high, low, jnp.zeros((12, sums.shape[1]), bf16)])

    def unpack(rows):
        rows = rows.astype(f32)
        return rows[0:2] + rows[2:4]

    packed = jnp.pad(pack(sums), ((0, 0), (0, 3 * E)))
    result = jnp.concatenate([jnp.concatenate([context, joined_grad], axis=1), packed])
    result_far = swap_far(result)
    sums = sums + unpack(result_far[SEQ:, :SEQ])
    heads = by_far(result[:SEQ], result_far[:SEQ])
    packed = jnp.pad(pack(sums), ((0, 0), (0, 3 * E)))
    heads_sent = jnp.concatenate([heads, jnp.stack([packed, jnp.zeros_like(packed)])], axis=1)
    heads_other = swap_cores(heads_sent)
    sums = jnp.concatenate([sums, unpack(heads_other[0, SEQ:, :SEQ])], axis=1)
    heads = jnp.concatenate([heads, heads_other[:, :SEQ]], axis=1)

    joined_weight = in_order([b[:, :, : 3 * E] for b in blocks], x).reshape(2, quarter, 3 * E)
    weight_parts = [
        dot(grads, heads[h, :, :E], ((1,), (0,))).astype(bf16).reshape(2, X_COUNT, part, E)
        for h in range(2)
    ]

    def weight_to(step):
        place = (x + step) % X_COUNT
        return jnp.concatenate(
            [lax.dynamic_index_in_dim(w, place, 1, keepdims=False) for w in weight_parts]
        )

    across, heads = lax.optimization_barrier((weight_to(2), heads))

    group_part = sum(
        dot(joined_weight[h], heads[h, :, E:], ((1,), (1,))) for h in range(2)
    ).astype(bf16)
    extra = jnp.broadcast_to(pack(sums)[None], (Z_COUNT, 16, 2 * SEQ))
    payload = jnp.concatenate([group_part.reshape(Z_COUNT, part, 2 * SEQ), extra], axis=1)
    group_parts = lax.all_to_all(payload, "tensor", 0, 0, tiled=True, axis_index_groups=rings)
    total = jnp.sum(group_parts.astype(f32), axis=0)
    weight_parts = scatter_x(weight_to, across)
    grad_out_weight = scatter_y(weight_parts, y)
    sums = total[part : part + 2, :SEQ] + total[part + 2 : part + 4, :SEQ]
    total = total[:part]
    total_other = swap_cores(total[:, SEQ:])
    total = total[:, :SEQ]
    normed_grad = jnp.where(
        core == 0,
        jnp.concatenate([total, total_other]),
        jnp.concatenate([total_other, total]),
    )
    mean_grad = sums[0] / depth
    mean_cross = sums[1] / depth

    own_gain = lax.dynamic_slice_in_dim(norm_gain, rank * width, width)
    scaled_grad = normed_grad * own_gain[:, None]
    scaled = (hidden_t.astype(f32) - mean[:SEQ]) * inv_std[:SEQ]
    input_grad = inv_std[:SEQ] * (scaled_grad - mean_grad - scaled * mean_cross)

    return input_grad.astype(bf16).T, grad_out_weight.T


def solution(mesh):
    in_specs = (
        P("dp", "tensor"),
        P(),
        P(),
        P("dp", "tensor"),
        P("tensor"),
        P("tensor", "dp"),
        P("dp", "tensor"),
    )
    out_specs = (P("dp", "tensor"), P("tensor", "dp"))
    return jax.shard_map(body, mesh=mesh, in_specs=in_specs, out_specs=out_specs, check_vma=False)
```
